32 devices in a mesh: dp: 4 (over z), fsdp: 8 (over y, x, core).
Axes of the slice: x: 2, y: 2, z: 4, core: 2. Of those that a mesh axis runs over, the one named last changes fastest.
Arguments:
- tokens: bfloat16 [32, 512, 768], P(('dp', 'fsdp')), may hold values from -6 to 6
- cotangent: bfloat16 [32, 512, 768], P(('dp', 'fsdp')), may hold values from -6 to 6
- lengths: int32 [32], P(('dp', 'fsdp')), may hold values from 128 to 512, as said below
- weights: float32 [440, 128, 128], P('dp', 'fsdp')
- vectors: float32 [13, 768], replicated
- moments: float32 [13, 768], replicated
- left_stats: float32 [440, 128, 128], P('dp', 'fsdp')
- right_stats: float32 [440, 128, 128], P('dp', 'fsdp')
- left_root: float32 [440, 128, 128], P('dp', 'fsdp')
- right_root: float32 [440, 128, 128], P('dp', 'fsdp'), as said below
- decays: float32 [440, 2], P('dp'), may hold values from 0.9 to 0.99
Outputs:
- outputs: bfloat16 [32, 512, 768], P(('dp', 'fsdp'))
- input_grads: bfloat16 [32, 512, 768], P(('dp', 'fsdp'))
- new_weights: float32 [440, 128, 128], P('dp', 'fsdp')
- weight_grads: float32 [440, 128, 128], P('dp', 'fsdp')
- new_left: float32 [440, 128, 128], P('dp', 'fsdp')
- new_right: float32 [440, 128, 128], P('dp', 'fsdp')
- new_vectors: float32 [13, 768], replicated
- new_moments: float32 [13, 768], replicated
- summary_norms: float32 [2], replicated
The draws below stay inside these ranges and needn't reach their ends.
Inputs may be any that keep to these rules, and one draw needn't show every extreme that they name: `lengths`: some slot has length exactly 512. `right_root`: every block is symmetric.
All inputs are finite; a program needn't handle non-finite values.
Results may differ from the reference program's by a relative error of at most 0.02.
The reference program's roundings to bfloat16 on the way count: a program that leaves them out, or rounds other values in their place, can miss the bound.
Values may be sent and summed in bfloat16 or wider, within the bound.
No kernel may reach another device: no remote copies, remote signals or barrier semaphores. Data moves between devices by JAX's collectives and lax.ppermute only.
A program may use at most 192 MiB of HBM per device.

```python
import math
import jax
import jax.numpy as jnp
from jax import lax

D = 768
H = 12
HD = 64
FF = 3072
K = 256
NMAX = 512
MINLEN = 128
TB = 128
SEQS = 32
NBLK = 440
NVEC = 13


def gradient_scale():
    return math.sqrt((MINLEN + NMAX) / (2.0 * SEQS))


def row_ratio():
    return math.log(3.0)


def row_profile(sign):
    place = jnp.arange(TB, dtype=jnp.float32) / (TB - 1.0) - 0.5
    return jnp.exp(sign * row_ratio() * place)


def tile_select(attn_value, output_value, compress_value, hidden_value, return_value):
    quarter = (D // TB) ** 2
    att_count = 4 * quarter + NMAX // TB * (K // TB)
    hidden_count = D // TB * (FF // TB)
    tile_index = jnp.arange(NBLK)
    chosen = jnp.where(tile_index < 3 * quarter, attn_value, output_value)
    chosen = jnp.where(tile_index >= 4 * quarter, compress_value, chosen)
    chosen = jnp.where(tile_index >= att_count, hidden_value, chosen)
    chosen = jnp.where(tile_index >= att_count + hidden_count, return_value, chosen)
    return chosen.astype(jnp.float32)


def symmetric_tiles(key, amplitude):
    subkeys = jax.random.split(key, 3)
    diagonal = jnp.exp(jax.random.uniform(subkeys[0], (NBLK, TB), jnp.float32, math.log(0.7), math.log(2.0)))
    gaussian = jax.random.normal(subkeys[1], (NBLK, TB, TB), jnp.float32)
    identity = jnp.eye(TB, dtype=jnp.float32)
    coupled = (gaussian + jnp.swapaxes(gaussian, 1, 2)) * (0.25 / math.sqrt(2.0 * TB)) * (1.0 - identity)
    factor = amplitude * jnp.exp(jax.random.uniform(subkeys[2], (NBLK,), jnp.float32, 0.0, math.log(4.0)))
    return (coupled + identity * diagonal[:, :, None]) * factor[:, None, None]


def stats_amplitude():
    kinds = tile_select(0.3, 0.55, 0.3, 0.25, 0.45) * gradient_scale()
    return TB * kinds * kinds * (0.05 / 0.95)


def draw_lengths(key, part):
    subkeys = jax.random.split(jax.random.fold_in(key, 11), 2)
    drawn = jax.random.randint(subkeys[0], (SEQS,), MINLEN, NMAX + 1)
    chosen = jax.random.randint(subkeys[1], (), 0, SEQS)
    return jnp.where(jnp.arange(SEQS) == chosen, NMAX, drawn).astype(jnp.int32)


def draw_weights(key, part):
    scales = tile_select(D ** (-0.5), (D / 2.0) ** (-0.5), (NMAX / 8.0) ** (-0.5), D ** (-0.5), FF ** (-0.5))
    rising = row_profile(1.0)
    gaussian = jax.random.normal(jax.random.fold_in(key, 21), (NBLK, TB, TB), jnp.float32)
    return gaussian * scales[:, None, None] * rising[None, :, None]


def draw_vectors(key, part):
    spread_rows = FF // D
    row_index = jnp.arange(NVEC)[:, None]
    gaussian = jax.random.normal(jax.random.fold_in(key, 31), (NVEC, D), jnp.float32)
    gain_rows = (row_index == 4) | (row_index == 7 + spread_rows)
    return jnp.where(gain_rows, 1.0 + 0.1 * gaussian, 0.2 * gaussian)


def draw_moments(key, part):
    spread_rows = FF // D
    row_index = jnp.arange(NVEC)
    scales = jnp.where(row_index < 3, 0.3, 0.8)
    scales = jnp.where(row_index == 3, 0.6, scales)
    scales = jnp.where((row_index >= 6) & (row_index < 6 + spread_rows), 0.25, scales)
    scales = jnp.where(row_index == 6 + spread_rows, 0.7, scales)
    scales = jnp.where(row_index >= 7 + spread_rows, 1.0, scales)
    subkeys = jax.random.split(jax.random.fold_in(key, 41), 2)
    spread = jnp.exp(jax.random.uniform(subkeys[1], (NVEC, 1), jnp.float32, 0.0, math.log(2.0)))
    gaussian = jax.random.normal(subkeys[0], (NVEC, D), jnp.float32)
    return gaussian * (0.11 * gradient_scale()) * scales[:, None].astype(jnp.float32) * spread


def draw_left_stats(key, part):
    return symmetric_tiles(jax.random.fold_in(key, 51), stats_amplitude())


def draw_right_stats(key, part):
    return symmetric_tiles(jax.random.fold_in(key, 52), stats_amplitude())


def draw_left_root(key, part):
    base = symmetric_tiles(jax.random.fold_in(key, 61), jnp.ones((NBLK,), jnp.float32))
    falling = row_profile(-0.5)
    return base * falling[None, :, None] * falling[None, None, :]


def draw_right_root(key, part):
    return symmetric_tiles(jax.random.fold_in(key, 62), jnp.ones((NBLK,), jnp.float32))


def block_levels(rng, shape, pieces, least, top_value):
    def one(position, parts):
        heights = jax.random.uniform(jax.random.fold_in(jax.random.fold_in(rng, 6), position), (parts,), jnp.float32, least / len(pieces), top_value / len(pieces))
        return jnp.repeat(jnp.exp(heights), shape[position] // parts).reshape((-1,) + (1,) * (len(shape) - position - 1))

    level = one(*pieces[0])
    for cut in pieces[1:]:
        level = level * one(*cut)
    return level


def centred(key, shape, scale, most, cuts=(), kind=jnp.bfloat16):
    factor_of = block_levels(key, shape, cuts, -0.22, 0.18) if cuts else 1.0
    entries = jax.random.normal(key, shape, jnp.float32) * scale * factor_of
    return jnp.minimum(jnp.maximum(entries, -most), most).astype(kind)


def setup_inputs(seed: int = 0) -> dict:
    splits = jax.random.split(jax.random.key(seed), 12)
    tokens = centred(splits[0], (SEQS, NMAX, D), 1.0, 6.0, ((0, 32),))
    cotangent = centred(splits[1], (SEQS, NMAX, D), 1.0, 6.0, ((0, 32),))
    lengths = draw_lengths(jax.random.fold_in(splits[11], 71), 0)
    weights = draw_weights(jax.random.fold_in(splits[11], 71), 0)
    vectors = draw_vectors(jax.random.fold_in(splits[11], 71), 0)
    moments = draw_moments(jax.random.fold_in(splits[11], 71), 0)
    left_stats = draw_left_stats(jax.random.fold_in(splits[11], 71), 0)
    right_stats = draw_right_stats(jax.random.fold_in(splits[11], 71), 0)
    left_root = draw_left_root(jax.random.fold_in(splits[11], 71), 0)
    right_root = draw_right_root(jax.random.fold_in(splits[11], 71), 0)
    decays = jnp.clip(0.9 + 0.09000003 * jax.random.uniform(splits[10], (NBLK, 2), jnp.float32) ** block_levels(splits[10], (NBLK, 2), ((0, 4),), -0.2, 0.2), 0.9, 0.99)
    return {"tokens": tokens, "cotangent": cotangent, "lengths": lengths, "weights": weights, "vectors": vectors, "moments": moments, "left_stats": left_stats, "right_stats": right_stats, "left_root": left_root, "right_root": right_root, "decays": decays}


HIGHEST_PRECISION = lax.Precision.HIGHEST
EPS_NORM = 1e-05
EPS_STEP = 1e-06
STEP_RATE = 0.25
MOMENT_DECAY = 0.9

@jax.custom_vjp
def low(v):
    return lax.optimization_barrier(v.astype(jnp.bfloat16)).astype(jnp.float32)

@jax.custom_vjp
def low_back(v):
    return v

def low_keep(v):
    return (low(v), None)

def low_pass(kept, grad):
    return (grad,)

def back_keep(v):
    return (v, None)

def back_low(kept, grad):
    return (low(grad),)
low.defvjp(low_keep, low_pass)
low_back.defvjp(back_keep, back_low)

def round_both(value):
    return low(low_back(value))

def matmul(left, right):
    return jnp.dot(left, right, precision=HIGHEST_PRECISION, preferred_element_type=jnp.float32)

def untile(tiles, height, width):
    return tiles.reshape(height // TB, width // TB, TB, TB).transpose(0, 2, 1, 3).reshape(height, width)

def retile(matrix):
    height, width = matrix.shape
    return matrix.reshape(height // TB, TB, width // TB, TB).transpose(0, 2, 1, 3).reshape(-1, TB, TB)

def normalize(value):
    centre = lax.optimization_barrier(jnp.mean(value, axis=-1, keepdims=True))
    spread = lax.optimization_barrier(jnp.mean(jnp.square(value - centre), axis=-1, keepdims=True))
    return (value - centre) * lax.rsqrt(spread + EPS_NORM)

def gelu_value(value):
    return value * 0.5 * (1.0 + lax.erf(value * 0.7071067811865476))

def block_forward(params, seq_inputs, validity):
    w_query, w_key, w_value, w_output, compress, w_hidden, w_return, vectors = params
    spread_rows = FF // D
    queries = round_both(matmul(seq_inputs, low(w_query)) + vectors[0])
    key_rows = round_both(matmul(seq_inputs, low(w_key)) + vectors[1])
    value_rows = round_both(matmul(seq_inputs, low(w_value)) + vectors[2])
    masked = low(compress) * validity[:, None]
    key_summary = round_both(matmul(masked.T, key_rows))
    value_summary = round_both(matmul(masked.T, value_rows))
    score_scale = HD ** (-0.5)
    raw_scores = jnp.einsum('nhd,khd->hnk', queries.reshape(NMAX, H, HD), key_summary.reshape(K, H, HD), precision=HIGHEST_PRECISION)
    scores = low_back(raw_scores * score_scale)
    raised = jnp.exp(scores - lax.optimization_barrier(jnp.max(scores, axis=-1, keepdims=True)))
    attend = low(raised / lax.optimization_barrier(jnp.sum(raised, axis=-1, keepdims=True)))
    mixed = round_both(jnp.einsum('hnk,khd->nhd', attend, value_summary.reshape(K, H, HD), precision=HIGHEST_PRECISION).reshape(NMAX, D))
    branch = low_back(matmul(mixed, low(w_output)) + vectors[3])
    first = normalize(seq_inputs + branch) * vectors[4] + vectors[5]
    hidden = low_back(matmul(low(first), low(w_hidden)) + vectors[6:6 + spread_rows].reshape(FF))
    active = low(gelu_value(hidden))
    second = low_back(matmul(active, low(w_return)) + vectors[6 + spread_rows])
    result = normalize(first + second) * vectors[7 + spread_rows] + vectors[8 + spread_rows]
    return (result * validity[:, None], (key_summary, value_summary))

def reference(tokens, cotangent, lengths, weights, vectors, moments, left_stats, right_stats, left_root, right_root, decays):
    quarter = (D // TB) ** 2
    att_count = 4 * quarter + NMAX // TB * (K // TB)
    hidden_count = D // TB * (FF // TB)
    matrices = (untile(weights[0:quarter], D, D), untile(weights[quarter:2 * quarter], D, D), untile(weights[2 * quarter:3 * quarter], D, D), untile(weights[3 * quarter:4 * quarter], D, D), untile(weights[4 * quarter:att_count], NMAX, K), untile(weights[att_count:att_count + hidden_count], D, FF), untile(weights[att_count + hidden_count:], FF, D))
    params = matrices + (vectors,)
    positions = jnp.arange(NMAX, dtype=jnp.int32)
    zero_grads = jax.tree.map(jnp.zeros_like, params)

    def one_sequence(state_pair, sequence):
        grad_sums, norm_sums = state_pair
        seq_tokens, seq_cotangent, seq_length = sequence
        validity = (positions < seq_length).astype(jnp.float32)

        def forward(params_in, inputs_in):
            return block_forward(params_in, inputs_in, validity)
        result, pullback, summaries = jax.vjp(forward, params, seq_tokens.astype(jnp.float32), has_aux=True)
        param_grads, input_grad = pullback(seq_cotangent.astype(jnp.float32))
        grad_sums = jax.tree.map(lambda total, term: total + term, grad_sums, param_grads)
        key_norm = jnp.sqrt(jnp.sum(jnp.square(summaries[0])))
        value_norm = jnp.sqrt(jnp.sum(jnp.square(summaries[1])))
        norm_sums = norm_sums + jnp.stack([key_norm, value_norm])
        return ((grad_sums, norm_sums), (result.astype(jnp.bfloat16), input_grad.astype(jnp.bfloat16)))
    (grad_sums, norm_sums), (outputs, input_grads) = lax.scan(one_sequence, (zero_grads, jnp.zeros((2,), jnp.float32)), (tokens, cotangent, lengths))
    grad_tiles = jnp.concatenate([retile(grad_sums[index]) for index in range(7)], axis=0) / SEQS
    vector_grad = grad_sums[7] / SEQS
    gram_left = jnp.einsum('brc,bsc->brs', grad_tiles, grad_tiles, precision=HIGHEST_PRECISION)
    gram_right = jnp.einsum('bic,bis->bcs', grad_tiles, grad_tiles, precision=HIGHEST_PRECISION)
    decay_left = decays[:, 0][:, None, None]
    decay_right = decays[:, 1][:, None, None]
    new_left = decay_left * left_stats + (1.0 - decay_left) * gram_left
    new_right = decay_right * right_stats + (1.0 - decay_right) * gram_right
    right_applied = jnp.einsum('bis,bsc->bic', grad_tiles, right_root, precision=HIGHEST_PRECISION)
    precond = jnp.einsum('brs,bsc->brc', left_root, right_applied, precision=HIGHEST_PRECISION)
    weight_scale = jnp.sqrt(lax.optimization_barrier(jnp.mean(jnp.square(weights), axis=(1, 2))))
    precond_scale = lax.rsqrt(lax.optimization_barrier(jnp.mean(jnp.square(precond), axis=(1, 2))) + EPS_STEP)
    new_weights = weights - STEP_RATE * (weight_scale * precond_scale)[:, None, None] * precond
    new_moments = MOMENT_DECAY * moments + (1.0 - MOMENT_DECAY) * vector_grad
    row_scale = jnp.sqrt(lax.optimization_barrier(jnp.mean(jnp.square(vectors), axis=1, keepdims=True)))
    moment_scale = lax.rsqrt(lax.optimization_barrier(jnp.mean(jnp.square(new_moments), axis=1, keepdims=True)) + EPS_STEP)
    new_vectors = vectors - STEP_RATE * row_scale * new_moments * moment_scale
    summary_norms = norm_sums / SEQS
    return (outputs, input_grads, new_weights, grad_tiles, new_left, new_right, new_vectors, new_moments, summary_norms)
```

```python
import functools

import jax
import jax.numpy as jnp
from jax import lax
from jax.experimental import pallas as pl
from jax.experimental.pallas import tpu as pltpu
from jax.sharding import PartitionSpec as P

D = 768
H = 12
HD = 64
FF = 3072
K = 256
NMAX = 512
TB = 128
LANES = 128
PART = 110
GROUPS = 8

EPS_NORM = 1e-05
EPS_STEP = 1e-06
STEP_RATE = 0.25
MOMENT_DECAY = 0.9
SQRT_HALF = 0.7071067811865476
INV_SQRT_TWO_PI = 0.3989422804014327
SCALE = HD ** (-0.5)

QUARTER = (D // TB) ** 2
ATT = 4 * QUARTER + NMAX // TB * (K // TB)
HID = D // TB * (FF // TB)
NBLK = ATT + 2 * HID
BF = jnp.bfloat16
F32 = jnp.float32

ANY = pl.BlockSpec(memory_space=pl.ANY)
VM = pl.BlockSpec(memory_space=pltpu.VMEM)
SM = pl.BlockSpec(memory_space=pltpu.SMEM)


def sds(shape, dtype):
    return jax.ShapeDtypeStruct(shape, dtype)


def nn(a, b):
    return lax.dot_general(a, b, (((1,), (0,)), ((), ())), preferred_element_type=F32)


def nt(a, b):
    return lax.dot_general(a, b, (((1,), (1,)), ((), ())), preferred_element_type=F32)


def tn(a, b):
    return lax.dot_general(a, b, (((0,), (0,)), ((), ())), preferred_element_type=F32)


def layer_norm(value):
    centre = jnp.mean(value, axis=-1, keepdims=True)
    shifted = value - centre
    spread = jnp.mean(shifted * shifted, axis=-1, keepdims=True)
    inverse = lax.rsqrt(spread + EPS_NORM)
    return shifted * inverse, inverse


def norm_backward(grad_out, normed, inverse, gain):
    scaled = grad_out * gain
    centred = scaled - jnp.mean(scaled, axis=-1, keepdims=True)
    return inverse * (centred - normed * jnp.mean(scaled * normed, axis=-1, keepdims=True))


def column_sum(value):
    return jnp.sum(value.astype(F32), axis=0, keepdims=True)


def valid_rows(length, width):
    return lax.broadcasted_iota(jnp.int32, (NMAX, width), 0) < length


def fetch(sc, pieces, steps, parts, raw, sem):
    for step in range(steps):
        for at, part in enumerate(parts):

            @pl.when(sc[8 + part] == step)
            def _():
                for s in range(GROUPS):
                    pltpu.make_async_copy(pieces[step * GROUPS + s], raw.at[at, s], sem.at[at, s]).start()


def fetched(pieces, raw, sem, at):
    for s in range(GROUPS):
        pltpu.make_async_copy(pieces[s], raw.at[at, s], sem.at[at, s]).wait()


def lay_out(slots, raw, at, first, count, dst, dst_first, per_row):
    def body(n, carry):
        b = n + dst_first
        i, j = b // per_row, b % per_row
        for r in range(GROUPS):
            dst[pl.ds(pl.multiple_of(i * TB + 16 * r, 16), 16), pl.ds(pl.multiple_of(j * TB, TB), TB)] = raw[
                at, slots[r], first + n
            ]
        return carry

    lax.fori_loop(0, count, body, 0)


def splitter(sc):
    even = sc[13] == 0
    mine = [jnp.where(even, sc[2 * m], sc[2 * m + 1]) for m in range(4)]
    other = [jnp.where(even, sc[2 * m + 1], sc[2 * m]) - 4 for m in range(4)]

    def put(keep, send, b, value):
        low = value.astype(BF)
        for m in range(4):
            first = low[32 * m : 32 * m + 16]
            second = low[32 * m + 16 : 32 * m + 32]
            keep[mine[m], b] = jnp.where(even, first, second)
            send[other[m], b] = jnp.where(even, second, first)

    return put


def attention_forward(sc, tok, vec, *rest):
    pieces = rest[:24]
    (q_o, k_o, v_o, ks_o, vs_o, lse_o, mix_o, mixt_o, nf_o, inv_o, norm_o, wq_o, wk_o, wv_o, wo_o, cm_o) = rest[24:40]
    raw, sem = rest[40:]
    fetch(sc, pieces, 3, (0, 1), raw, sem)
    slots = [sc[r] for r in range(GROUPS)]
    nb = D // TB
    for at in (0, 1):
        fetched(pieces, raw, sem, at)
    for m, dst in enumerate((wq_o, wk_o, wv_o)):
        lay_out(slots, raw, 0, m * QUARTER, QUARTER, dst, 0, nb)
    head = PART - 3 * QUARTER
    lay_out(slots, raw, 0, 3 * QUARTER, head, wo_o, 0, nb)
    lay_out(slots, raw, 1, 0, QUARTER - head, wo_o, head, nb)
    lay_out(slots, raw, 1, QUARTER - head, ATT - 4 * QUARTER, cm_o, 0, K // TB)
    x = tok[...]
    q_o[...] = (nn(x, wq_o[...]) + vec[0:1]).astype(BF)
    k_o[...] = (nn(x, wk_o[...]) + vec[1:2]).astype(BF)
    v_o[...] = (nn(x, wv_o[...]) + vec[2:3]).astype(BF)
    masked = jnp.where(valid_rows(sc[12], K), cm_o[...], jnp.zeros((), BF))
    ks_o[...] = tn(masked, k_o[...]).astype(BF)
    vs_o[...] = tn(masked, v_o[...]).astype(BF)
    for n, ref in enumerate((ks_o, vs_o)):
        square = jnp.square(ref[...].astype(F32))
        total = jnp.sum(jnp.sum(square, axis=0, keepdims=True), axis=1, keepdims=True)
        norm_o[n : n + 1, :] = jnp.broadcast_to(jnp.sqrt(total), (1, LANES))
    lane = lax.broadcasted_iota(jnp.int32, (K, LANES), 1) < HD
    for p in range(H // 2):
        cols = slice(p * LANES, (p + 1) * LANES)
        q_p, ks_p, vs_p = q_o[:, cols], ks_o[:, cols], vs_o[:, cols]
        zero = jnp.zeros((), BF)
        parts, values = [], []
        for half in range(2):
            sel = lane if half == 0 else jnp.logical_not(lane)
            scores = nt(jnp.where(sel, ks_p, zero), q_p) * SCALE
            peak = jnp.max(scores, axis=0, keepdims=True)
            raised = jnp.exp(scores - peak)
            total = jnp.sum(raised, axis=0, keepdims=True)
            lse_o[2 * p + half : 2 * p + half + 1, :] = peak + jnp.log(total)
            parts.append((raised * (1.0 / total)).astype(BF))
            values.append(jnp.where(sel, vs_p, zero))
        mixt = tn(jnp.concatenate(values, axis=0), jnp.concatenate(parts, axis=0)).astype(BF)
        mixt_o[cols, :] = mixt
        mix_o[:, cols] = mixt.T
    branch = nn(mix_o[...], wo_o[...]) + vec[3:4]
    normed, inverse = layer_norm(x.astype(F32) + branch)
    nf_o[...] = normed
    inv_o[...] = jnp.broadcast_to(inverse, (NMAX, LANES))


STEP = 256


def ffn_forward(sc, nf, cot, vec, *rest):
    pieces = rest[:32]
    (out_o, gs_o, gsl_o, slope_o, fl_o, keep_o, send_o, sums_o, wh_o, wr_o) = rest[32:42]
    raw, sem, wh, wr, act, acc, osem = rest[42:]
    fetch(sc, pieces, 4, (1, 2, 3), raw, sem)
    slots = [sc[r] for r in range(GROUPS)]
    put = splitter(sc)
    nh, nd = FF // TB, D // TB
    for at in range(3):
        fetched(pieces, raw, sem, at)
    head = ATT - PART
    lay_out(slots, raw, 0, head, PART - head, wh, 0, nh)
    rest_h = HID - (PART - head)
    lay_out(slots, raw, 1, 0, rest_h, wh, PART - head, nh)
    lay_out(slots, raw, 1, rest_h, PART - rest_h, wr, 0, nd)
    lay_out(slots, raw, 2, 0, PART, wr, PART - rest_h, nd)
    copies = [pltpu.make_async_copy(wh, wh_o, osem.at[0]), pltpu.make_async_copy(wr, wr_o, osem.at[1])]
    for copy in copies:
        copy.start()
    normed = nf[...]
    first = normed * vec[4:5] + vec[5:6]
    fl_o[...] = first.astype(BF)
    acc[...] = jnp.zeros((NMAX, D), F32)
    for g in range(FF // STEP):
        cols = slice(g * STEP, (g + 1) * STEP)
        row, off = 6 + (g * STEP) // D, (g * STEP) % D
        hidden = nn(fl_o[...], wh[:, cols]) + vec[row : row + 1, off : off + STEP]
        phi = 0.5 * (1.0 + lax.erf(hidden * SQRT_HALF))
        low = (hidden * phi).astype(BF)
        act[:, cols] = low
        slope_o[:, cols] = phi + hidden * INV_SQRT_TWO_PI * jnp.exp(-0.5 * hidden * hidden)
        acc[...] += nn(low, wr[cols, :])
    second = acc[...] + vec[10:11]
    valid = valid_rows(sc[12], D)
    normed2, inverse2 = layer_norm(first + second)
    result = normed2 * vec[11:12] + vec[12:13]
    out_o[...] = jnp.where(valid, result, 0.0).astype(BF)
    grad_result = jnp.where(valid, cot[...].astype(F32), 0.0)
    sums_o[1:2, :] = column_sum(grad_result * normed2)
    sums_o[2:3, :] = column_sum(grad_result)
    grad_second = norm_backward(grad_result, normed2, inverse2, vec[11:12])
    gs_o[...] = grad_second
    low = grad_second.astype(BF)
    gsl_o[...] = low
    sums_o[0:1, :] = column_sum(low)
    for g in range(FF // STEP):
        terms = tn(act[:, g * STEP : (g + 1) * STEP], gsl_o[...])
        for i in range(STEP // TB):
            for j in range(nd):
                put(keep_o, send_o, (g * (STEP // TB) + i) * nd + j, terms[i * TB : (i + 1) * TB, j * TB : (j + 1) * TB])
    for copy in copies:
        copy.wait()


def ffn_backward(gs, gsl, slope, nf, inv, vec, wh, wr, wo, gh_o, gr_o, gb_o, gm_o, sums_o, acc):
    low = gsl[...]
    acc[...] = jnp.zeros((NMAX, D), F32)
    for g in range(FF // STEP):
        cols = slice(g * STEP, (g + 1) * STEP)
        grad_active = nt(low, wr[cols, :])
        gh = (grad_active * slope[:, cols]).astype(BF)
        gh_o[:, cols] = gh
        row, off = (g * STEP) // D, (g * STEP) % D
        sums_o[3 + row : 4 + row, off : off + STEP] = column_sum(gh)
        acc[...] += nt(gh, wh[:, cols])
    grad_first = gs[...] + acc[...]
    normed = nf[...]
    sums_o[1:2, :] = column_sum(grad_first * normed)
    sums_o[2:3, :] = column_sum(grad_first)
    grad_resid = norm_backward(grad_first, normed, inv[:, 0:1], vec[4:5])
    gr_o[...] = grad_resid
    branch = grad_resid.astype(BF)
    gb_o[...] = branch
    sums_o[0:1, :] = column_sum(branch)
    gm_o[...] = nt(branch, wo[...]).astype(BF)


def attention_backward(q, ks, vs, lse, gm, gq_o, gks_o, gvs_o):
    lane = lax.broadcasted_iota(jnp.int32, (K, LANES), 1) < HD
    zero = jnp.zeros((), BF)
    for p in range(H // 2):
        cols = slice(p * LANES, (p + 1) * LANES)
        q_p, ks_p, vs_p, gm_p = q[:, cols], ks[:, cols], vs[:, cols], gm[:, cols]
        keys, grads, gvs, gks = [], [], [], []
        for half in range(2):
            sel = lane if half == 0 else jnp.logical_not(lane)
            key = jnp.where(sel, ks_p, zero)
            attend = jnp.exp(nt(key, q_p) * SCALE - lse[2 * p + half : 2 * p + half + 1, :])
            grad_attend = nt(jnp.where(sel, vs_p, zero), gm_p)
            mean = jnp.sum(grad_attend * attend, axis=0, keepdims=True)
            grad_scores = (attend * (grad_attend - mean)).astype(BF)
            gvs.append(nn(attend.astype(BF), gm_p))
            gks.append(nn(grad_scores, q_p))
            keys.append(key)
            grads.append(grad_scores)
        gvs_o[:, cols] = jnp.where(lane, gvs[0], gvs[1]).astype(BF)
        gks_o[:, cols] = (jnp.where(lane, gks[0], gks[1]) * SCALE).astype(BF)
        gqt = tn(jnp.concatenate(keys, axis=0), jnp.concatenate(grads, axis=0)) * SCALE
        gq_o[:, cols] = gqt.astype(BF).T


def projection_backward(sc, tok, k, v, gq, gks, gvs, gb, gr, mixt, cm, wq, wk, wv, in_o, keep_o, send_o, sums_o):
    put = splitter(sc)
    nd, nk = D // TB, K // TB
    masked = jnp.where(valid_rows(sc[12], K), cm[...], jnp.zeros((), BF))
    gk = nn(masked, gks[...]).astype(BF)
    gv = nn(masked, gvs[...]).astype(BF)
    tokt = tok[...].T
    lhs = (tokt, tokt, tokt, mixt[...])
    for m, grad in enumerate((gq[...], gk, gv, gb[...])):
        if m < 3:
            sums_o[m : m + 1, :] = column_sum(grad)
        terms = nn(lhs[m], grad)
        for i in range(nd):
            for j in range(nd):
                put(keep_o, send_o, m * QUARTER + i * nd + j, terms[i * TB : (i + 1) * TB, j * TB : (j + 1) * TB])
    comp = nt(k[...], gks[...]) + nt(v[...], gvs[...])
    comp = jnp.where(valid_rows(sc[12], K), comp, 0.0)
    for i in range(NMAX // TB):
        for j in range(nk):
            put(keep_o, send_o, 4 * QUARTER + i * nk + j, comp[i * TB : (i + 1) * TB, j * TB : (j + 1) * TB])
    total = gr[...] + nt(gq[...], wq[...])
    total = total + nt(gk, wk[...])
    total = total + nt(gv, wv[...])
    in_o[...] = total.astype(BF)


def hidden_terms(sc, fl, gh, keep_o, send_o):
    put = splitter(sc)
    nh, nd = FF // TB, D // TB
    flt = fl[...].T
    for g in range(FF // STEP):
        terms = nn(flt, gh[:, g * STEP : (g + 1) * STEP])
        for i in range(nd):
            for j in range(STEP // TB):
                put(keep_o, send_o, i * nh + g * (STEP // TB) + j, terms[i * TB : (i + 1) * TB, j * TB : (j + 1) * TB])


def step_kernel(sc, dec, own, lroot, lstat, rstat, *rest):
    gp, rp = rest[:GROUPS], rest[GROUPS : 2 * GROUPS]
    nl_o, nr_o, pre_o, sq_o = rest[2 * GROUPS : 2 * GROUPS + 4]
    graw, rraw, sem = rest[2 * GROUPS + 4 :]
    for s in range(GROUPS):
        pltpu.make_async_copy(rp[s], rraw.at[s], sem.at[1, s]).start()
        pltpu.make_async_copy(gp[s], graw.at[s], sem.at[0, s]).start()
    slots = [sc[r] for r in range(GROUPS)]
    me = sc[14]
    pick_row = lax.broadcasted_iota(jnp.int32, (16, TB), 0) + me * 16
    select = (lax.broadcasted_iota(jnp.int32, (16, TB), 1) == pick_row).astype(BF)
    for s in range(GROUPS):
        pltpu.make_async_copy(rp[s], rraw.at[s], sem.at[1, s]).wait()
        pltpu.make_async_copy(gp[s], graw.at[s], sem.at[0, s]).wait()

    def body(b, carry):
        grad = jnp.concatenate([graw[slots[r], b] for r in range(GROUPS)], axis=0)
        right = jnp.concatenate([rraw[slots[r], b] for r in range(GROUPS)], axis=0)
        rows = own[b].astype(BF)
        across = nt(jnp.concatenate([rows, select], axis=0), grad)
        decay = dec[2 * b]
        nl_o[b] = decay * lstat[b] + (1.0 - decay) * across[:16]
        root = lroot[b]
        high = root.astype(BF)
        rest_root = (root - high.astype(F32)).astype(BF)
        down = nn(jnp.concatenate([high, rest_root, across[16:].astype(BF)], axis=0), grad)
        decay = dec[2 * b + 1]
        nr_o[b] = decay * rstat[b] + (1.0 - decay) * down[32:]
        mid = down[:16] + down[16:32]
        high = mid.astype(BF)
        rest_mid = (mid - high.astype(F32)).astype(BF)
        last = nn(jnp.concatenate([high, rest_mid], axis=0), right)
        pre = last[:16] + last[16:]
        pre_o[b] = pre
        sq_o[pl.ds(b, 1), :] = jnp.sum(pre * pre, axis=0, keepdims=True)
        return carry

    lax.fori_loop(0, PART, body, 0, unroll=2)


def call(kernel, ins, outs, in_specs, out_specs=None, scratch=(), limit=60, flops=0, nbytes=0):
    return pl.pallas_call(
        kernel,
        out_shape=outs,
        in_specs=in_specs,
        out_specs=out_specs if out_specs is not None else [VM] * len(outs),
        scratch_shapes=list(scratch),
        compiler_params=pltpu.CompilerParams(vmem_limit_bytes=limit * 1024 * 1024),
        cost_estimate=pl.CostEstimate(flops=flops, bytes_accessed=nbytes, transcendentals=0),
    )(*ins)


SLOT_TABLE = (0, 4, 1, 6, 2, 5, 3, 7)


def slot_of(code, core):
    other, x, y = code & 1, (code >> 1) & 1, code >> 2
    return 4 * other + jnp.where((other ^ core) == 0, x + 2 * y, y + 2 * x)


def toward(x, move):
    return lax.ppermute(x, "fsdp", [(i, move(i)) for i in range(GROUPS)])


def near(x):
    return toward(x, lambda i: i ^ 2 if i % 2 == 0 else i ^ 4)


def far(x):
    return toward(x, lambda i: i ^ 4 if i % 2 == 0 else i ^ 2)


def sibling(x):
    return toward(x, lambda i: i ^ 1)


def along(x, pairs):
    return lax.ppermute(x, "dp", pairs)


def plane_gather(own):
    a = near(own)
    b = far(own)
    c = far(a)
    d = sibling(jnp.stack([own, a, b, c]))
    return [own, a, b, c] + [d[i] for i in range(4)]


def chosen(index, options):
    value = options[0]
    for i in range(1, len(options)):
        value = jnp.where(index == i, options[i], value)
    return value


def gather_weights(narrow):
    me = lax.axis_index("dp")
    up, down = [(0, 1), (1, 2), (2, 3)], [(3, 2), (2, 1), (1, 0)]
    u1, d1 = along(narrow, up), along(narrow, down)
    u2, d2 = along(u1, up), along(d1, down)
    u3, d3 = along(u2, up), along(d2, down)
    shards = [
        narrow,
        chosen(me, [d1, u1, u1, u2]),
        chosen(me, [d2, d1, u2, u3]),
        chosen(me, [d3, d2, d1, u1]),
    ]
    steps = chosen(me, [jnp.array(row, jnp.int32) for row in ((0, 1, 2, 3), (1, 0, 2, 3), (2, 1, 0, 3), (2, 1, 3, 0))])
    return [piece for shard in shards for piece in plane_gather(shard)], steps


def added(a, b):
    return (a.astype(F32) + b.astype(F32)).astype(BF)


def plane_scatter(keep, send):
    got = sibling(send)
    own = added(keep[0], got[0])
    first = added(keep[1], got[1])
    pair = added(keep[2:4], got[2:4])
    back = far(pair)
    first = added(first, back[1])
    last = near(first)
    return own.astype(F32) + back[0].astype(F32) + last.astype(F32)


def line_scatter(part, even_at, odd_at):
    for_even, for_odd = part
    down = along(for_even, [(1, 0), (3, 2)])
    up = along(for_odd, [(0, 1), (2, 3)])
    for_even, for_odd = added(for_even, down), added(for_odd, up)
    far_even = along(for_even, [(even_at ^ 2, even_at)])
    far_odd = along(for_odd, [(odd_at ^ 2, odd_at)])
    return for_even.astype(F32) + far_even.astype(F32), for_odd.astype(F32) + far_odd.astype(F32)


def plane_sum(x):
    for bit in (1, 2, 4):
        x = x + toward(x, lambda i, bit=bit: i ^ bit)
    return x


def whole_sum(x):
    x = plane_sum(x)
    for bit in (1, 2):
        x = x + along(x, [(i, i ^ bit) for i in range(4)])
    return x


def local(
    tokens,
    cotangent,
    lengths,
    weights,
    vectors,
    moments,
    left_stats,
    right_stats,
    left_root,
    right_root,
    decays,
):
    dp, fsdp = lax.axis_size("dp"), lax.axis_size("fsdp")
    assert tokens.shape[0] == 1
    staged = (dp, fsdp) == (4, GROUPS)
    seq_total = tokens.shape[0] * dp * fsdp
    tok, cot = tokens[0], cotangent[0]
    narrow = weights.astype(BF)
    if staged:
        me = lax.axis_index("fsdp")
        core = lax.rem(me, 2)
        slots = slot_of(jnp.arange(GROUPS, dtype=jnp.int32) ^ me, core)
        pieces, steps = gather_weights(narrow)
        roots = plane_gather(right_root.astype(BF))
    else:
        me = jnp.int32(0)
        core = jnp.int32(0)
        slots = slot_of(jnp.arange(GROUPS, dtype=jnp.int32), core)
        full = lax.all_gather(lax.all_gather(narrow, "dp", axis=0, tiled=True), "fsdp", axis=1, tiled=True)
        full = full.reshape(NBLK // PART, PART, GROUPS, TB // GROUPS, TB)
        place = [SLOT_TABLE.index(s) for s in range(GROUPS)]
        pieces = [full[t, :, place[s]] for t in range(NBLK // PART) for s in range(GROUPS)]
        steps = jnp.arange(4, dtype=jnp.int32)
    scalars = jnp.concatenate([slots, steps, lengths, core[None], me[None]]).astype(jnp.int32)

    act = sds((NMAX, D), BF)
    wide = sds((NMAX, D), F32)
    summary = sds((K, D), BF)
    square = sds((D, D), BF)
    row16 = TB // GROUPS
    piece = pltpu.VMEM((2, GROUPS, PART, row16, TB), BF)
    (q, k, v, ks, vs, lse, mix, mixt, nf, inv, norms, wq, wk, wv, wo, cm) = call(
        attention_forward,
        [scalars, tok, vectors] + pieces[:24],
        [act, act, act, summary, summary, sds((H, NMAX), F32), act, sds((D, NMAX), BF), wide,
         sds((NMAX, LANES), F32), sds((2, LANES), F32), square, square, square, square, sds((NMAX, K), BF)],
        [SM, VM, VM] + [ANY] * 24,
        scratch=[piece, pltpu.SemaphoreType.DMA((2, GROUPS))],
        limit=40, flops=5 * 10**9, nbytes=10**7,
    )
    del mix
    terms = sds((4, HID, row16, TB), BF)
    (out, gs, gsl, slope, fl, r_keep, r_send, sums_c, wh, wr) = call(
        ffn_forward,
        [scalars, nf, cot, vectors] + pieces,
        [act, wide, act, sds((NMAX, FF), F32), act, terms, terms, sds((3, D), F32), sds((D, FF), BF), sds((FF, D), BF)],
        [SM, VM, VM, VM] + [ANY] * 32,
        [VM] * 8 + [ANY] * 2,
        scratch=[
            pltpu.VMEM((3, GROUPS, PART, row16, TB), BF),
            pltpu.SemaphoreType.DMA((3, GROUPS)),
            pltpu.VMEM((D, FF), BF),
            pltpu.VMEM((FF, D), BF),
            pltpu.VMEM((NMAX, FF), BF),
            pltpu.VMEM((NMAX, D), F32),
            pltpu.SemaphoreType.DMA((2,)),
        ],
        limit=58, flops=8 * 10**9, nbytes=3 * 10**7,
    )
    gh, gr, gb, gm, sums_b = call(
        ffn_backward,
        [gs, gsl, slope, nf, inv, vectors, wh, wr, wo],
        [sds((NMAX, FF), BF), wide, act, act, sds((3 + FF // D, D), F32)],
        [VM] * 9,
        scratch=[pltpu.VMEM((NMAX, D), F32)],
        limit=44, flops=6 * 10**9, nbytes=2 * 10**7,
    )
    gq, gks, gvs = call(
        attention_backward, [q, ks, vs, lse, gm], [act, summary, summary], [VM] * 5,
        limit=32, flops=4 * 10**9, nbytes=4 * 10**6,
    )
    a_terms = sds((4, ATT, row16, TB), BF)
    in_grads, a_keep, a_send, sums_a = call(
        projection_backward,
        [scalars, tok, k, v, gq, gks, gvs, gb, gr, mixt, cm, wq, wk, wv],
        [act, a_terms, a_terms, sds((3, D), F32)],
        [SM] + [VM] * 13,
        limit=40, flops=5 * 10**9, nbytes=2 * 10**7,
    )
    h_keep, h_send = call(
        hidden_terms, [scalars, fl, gh], [terms, terms], [SM, VM, VM],
        limit=40, flops=3 * 10**9, nbytes=10**7,
    )

    local_vectors = jnp.concatenate([sums_a, sums_b, sums_c], axis=0)
    local_norms = norms[:, 0]
    if staged:
        z = lax.axis_index("dp")
        r_rows = plane_scatter(r_keep, r_send).astype(BF)
        a_rows = plane_scatter(a_keep, a_send).astype(BF)
        h_rows = plane_scatter(h_keep, h_send).astype(BF)
        cut_r = 3 * PART - (ATT + HID)
        cut_h = 2 * PART - ATT
        r_two, r_three = line_scatter((r_rows[:cut_r], r_rows[cut_r:]), 2, 3)
        a_zero, a_one = line_scatter((a_rows[:PART], a_rows[PART:]), 0, 1)
        h_two, h_one = line_scatter((h_rows[cut_h:], h_rows[:cut_h]), 2, 1)
        total = chosen(
            z, [a_zero, jnp.concatenate([a_one, h_one]), jnp.concatenate([h_two, r_two]), r_three]
        )
        grad_rows = total / seq_total
        packed = jnp.concatenate([local_vectors, jnp.pad(local_norms[None], ((0, 0), (0, D - 2)))], axis=0)
        packed = whole_sum(packed)
        vector_total, norm_totals = packed[:-1], packed[-1, :2]
        blocks = plane_gather(grad_rows.astype(BF))
        rows = sds(weights.shape, F32)
        new_left, new_right, precond, squares = call(
            step_kernel,
            [scalars, decays.reshape(-1), grad_rows, left_root, left_stats, right_stats] + blocks + roots,
            [rows, rows, rows, sds((PART, LANES), F32)],
            [SM, SM] + [VM] * 4 + [ANY] * 16,
            scratch=[
                pltpu.VMEM((GROUPS, PART, row16, TB), BF),
                pltpu.VMEM((GROUPS, PART, row16, TB), BF),
                pltpu.SemaphoreType.DMA((2, GROUPS)),
            ],
            limit=32, flops=10**9, nbytes=10**7,
        )
        both = jnp.stack([jnp.sum(squares, axis=1), jnp.sum(weights * weights, axis=(1, 2))])
        precond_squares, weight_squares = plane_sum(both)
    else:
        def join(keep, send):
            both = jnp.concatenate([keep, send], axis=0)
            return jnp.stack([both[s] for s in SLOT_TABLE], axis=1).reshape(-1, TB, TB)

        every = jnp.concatenate([join(a_keep, a_send), join(h_keep, h_send), join(r_keep, r_send)], axis=0)
        inner = lax.psum_scatter(every, "fsdp", scatter_dimension=1, tiled=True)
        total = lax.psum_scatter(inner, "dp", scatter_dimension=0, tiled=True).astype(F32)
        grad_rows = total / seq_total
        vector_total, norm_totals = lax.psum((local_vectors, local_norms), ("dp", "fsdp"))
        high = lax.Precision.HIGHEST
        whole = lax.all_gather(grad_rows.astype(BF), "fsdp", axis=1, tiled=True).astype(F32)
        count = grad_rows.shape[1]
        slab = lax.dynamic_slice_in_dim(whole, lax.axis_index("fsdp") * count, count, 2)
        gram_left = jnp.einsum("brc,bsc->brs", grad_rows, whole, precision=high)
        gram_right = jnp.einsum("bic,bis->bcs", slab, whole, precision=high)
        decay_left = decays[:, 0][:, None, None]
        decay_right = decays[:, 1][:, None, None]
        new_left = decay_left * left_stats + (1.0 - decay_left) * gram_left
        new_right = decay_right * right_stats + (1.0 - decay_right) * gram_right
        columns = jnp.einsum("bis,bcs->bic", whole, right_root, precision=high)
        applied = lax.all_gather(columns.astype(BF), "fsdp", axis=2, tiled=True).astype(F32)
        precond = jnp.einsum("brs,bsc->brc", left_root, applied, precision=high)
        precond_squares, weight_squares = lax.psum(
            (jnp.sum(precond * precond, axis=(1, 2)), jnp.sum(weights * weights, axis=(1, 2))), "fsdp"
        )
    vector_grad = vector_total / seq_total
    summary_norms = norm_totals / seq_total
    tile_area = TB * TB
    weight_scale = jnp.sqrt(weight_squares / tile_area)
    precond_scale = lax.rsqrt(precond_squares / tile_area + EPS_STEP)
    new_weights = weights - STEP_RATE * (weight_scale * precond_scale)[:, None, None] * precond
    new_moments = MOMENT_DECAY * moments + (1.0 - MOMENT_DECAY) * vector_grad
    row_scale = jnp.sqrt(jnp.mean(jnp.square(vectors), axis=1, keepdims=True))
    moment_scale = lax.rsqrt(jnp.mean(jnp.square(new_moments), axis=1, keepdims=True) + EPS_STEP)
    new_vectors = vectors - STEP_RATE * row_scale * new_moments * moment_scale
    return (
        out[None],
        in_grads[None],
        new_weights,
        grad_rows,
        new_left,
        new_right,
        new_vectors,
        new_moments,
        summary_norms,
    )


def solution(mesh):
    in_specs = (
        P(("dp", "fsdp"), None, None),
        P(("dp", "fsdp"), None, None),
        P(("dp", "fsdp")),
        P("dp", "fsdp", None),
        P(),
        P(),
        P("dp", "fsdp", None),
        P("dp", "fsdp", None),
        P("dp", "fsdp", None),
        P("dp", "fsdp", None),
        P("dp", None),
    )
    out_specs = (
        P(("dp", "fsdp"), None, None),
        P(("dp", "fsdp"), None, None),
        P("dp", "fsdp", None),
        P("dp", "fsdp", None),
        P("dp", "fsdp", None),
        P("dp", "fsdp", None),
        P(),
        P(),
        P(),
    )
    return jax.shard_map(local, mesh=mesh, in_specs=in_specs, out_specs=out_specs, check_vma=False)
```

```python
import functools

import jax
import jax.numpy as jnp
from jax import lax
from jax.experimental import pallas as pl
from jax.experimental.pallas import tpu as pltpu
from jax.sharding import PartitionSpec as P

D = 768
H = 12
HD = 64
FF = 3072
K = 256
NMAX = 512
TB = 128
LANES = 128
PART = 110
GROUPS = 8

EPS_NORM = 1e-05
EPS_STEP = 1e-06
STEP_RATE = 0.25
MOMENT_DECAY = 0.9
SQRT_HALF = 0.7071067811865476
INV_SQRT_TWO_PI = 0.3989422804014327
SCALE = HD ** (-0.5)

QUARTER = (D // TB) ** 2
ATT = 4 * QUARTER + NMAX // TB * (K // TB)
HID = D // TB * (FF // TB)
NBLK = ATT + 2 * HID
BF = jnp.bfloat16
F32 = jnp.float32

ANY = pl.BlockSpec(memory_space=pl.ANY)
VM = pl.BlockSpec(memory_space=pltpu.VMEM)
SM = pl.BlockSpec(memory_space=pltpu.SMEM)


def sds(shape, dtype):
    return jax.ShapeDtypeStruct(shape, dtype)


def nn(a, b):
    return lax.dot_general(a, b, (((1,), (0,)), ((), ())), preferred_element_type=F32)


def nt(a, b):
    return lax.dot_general(a, b, (((1,), (1,)), ((), ())), preferred_element_type=F32)


def tn(a, b):
    return lax.dot_general(a, b, (((0,), (0,)), ((), ())), preferred_element_type=F32)


def layer_norm(value):
    centre = jnp.mean(value, axis=-1, keepdims=True)
    shifted = value - centre
    spread = jnp.mean(shifted * shifted, axis=-1, keepdims=True)
    inverse = lax.rsqrt(spread + EPS_NORM)
    return shifted * inverse, inverse


def norm_backward(grad_out, normed, inverse, gain):
    scaled = grad_out * gain
    centred = scaled - jnp.mean(scaled, axis=-1, keepdims=True)
    return inverse * (centred - normed * jnp.mean(scaled * normed, axis=-1, keepdims=True))


def column_sum(value):
    return jnp.sum(value.astype(F32), axis=0, keepdims=True)


def valid_rows(length, width):
    return lax.broadcasted_iota(jnp.int32, (NMAX, width), 0) < length


HELD = GROUPS // 2
SET = 2


def piece_at(pieces, s):
    return pieces[s // HELD].at[s % HELD]


def fetch(sc, pieces, steps, parts, raw, sem):
    for step in range(steps):
        for at, part in enumerate(parts):

            @pl.when(sc[8 + part] == step)
            def _():
                for s in range(GROUPS):
                    source = piece_at(pieces[step * SET : (step + 1) * SET], s)
                    pltpu.make_async_copy(source, raw.at[at, s], sem.at[at, s]).start()


def fetched(pieces, raw, sem, at):
    for s in range(GROUPS):
        pltpu.make_async_copy(piece_at(pieces, s), raw.at[at, s], sem.at[at, s]).wait()


def lay_out(slots, raw, at, first, count, dst, dst_first, per_row):
    for n in range(count):
        i, j = divmod(n + dst_first, per_row)
        for r in range(GROUPS):
            dst[i * TB + 16 * r : i * TB + 16 * r + 16, j * TB : (j + 1) * TB] = raw[at, slots[r], first + n]


def splitter(sc):
    even = sc[13] == 0
    mine = [jnp.where(even, sc[2 * m], sc[2 * m + 1]) for m in range(4)]
    other = [jnp.where(even, sc[2 * m + 1], sc[2 * m]) - 4 for m in range(4)]

    def put(keep, send, b, value):
        low = value.astype(BF)
        for m in range(4):
            first = low[32 * m : 32 * m + 16]
            second = low[32 * m + 16 : 32 * m + 32]
            keep[mine[m], b] = jnp.where(even, first, second)
            send[other[m], b] = jnp.where(even, second, first)

    return put


STEP = 256


def tiles(raw, slots, block):
    part, b = divmod(block, PART)
    return [raw[part, slots[r], b] for r in range(GROUPS)]


def hidden_columns(raw, slots, g):
    count = STEP // TB
    rows = []
    for i in range(D // TB):
        blocks = [tiles(raw, slots, ATT + i * (FF // TB) + g * count + c) for c in range(count)]
        rows += [jnp.concatenate([block[r] for block in blocks], axis=1) for r in range(GROUPS)]
    return jnp.concatenate(rows, axis=0)


def return_rows(raw, slots, g):
    count = STEP // TB
    rows = []
    for i in range(count):
        blocks = [tiles(raw, slots, ATT + HID + (g * count + i) * (D // TB) + j) for j in range(D // TB)]
        rows += [jnp.concatenate([block[r] for block in blocks], axis=1) for r in range(GROUPS)]
    return jnp.concatenate(rows, axis=0)


KEPT = 10


def layer(sc, tok, cot, vec, *rest):
    pieces, rest = rest[: 4 * SET], rest[4 * SET :]
    stored, rest = rest[:KEPT], rest[KEPT:]
    (ks_o, vs_o, lse_o, norm_o, out_o, gr_o, gb_o, gm_o, keep_o, send_o, sums_o) = rest[:11]
    (raw, q_o, k_o, v_o, mixt_o, wq_o, wk_o, wv_o, wo_o, cm_o, mix_o, fl_o, gh_o, slope, act, gsl, acc, sem, osem) = rest[11:]
    fetch(sc, pieces, 4, range(4), raw, sem)
    slots = [sc[r] for r in range(GROUPS)]
    put = splitter(sc)
    nb = nd = D // TB
    copies = []

    def store(*refs):
        for ref in refs:
            copy = pltpu.make_async_copy(ref, stored[len(copies)], osem.at[len(copies)])
            copy.start()
            copies.append(copy)

    for at in (0, 1):
        fetched(pieces, raw, sem, at)
    for m, dst in enumerate((wq_o, wk_o, wv_o)):
        lay_out(slots, raw, 0, m * QUARTER, QUARTER, dst, 0, nb)
    head = PART - 3 * QUARTER
    lay_out(slots, raw, 0, 3 * QUARTER, head, wo_o, 0, nb)
    lay_out(slots, raw, 1, 0, QUARTER - head, wo_o, head, nb)
    lay_out(slots, raw, 1, QUARTER - head, ATT - 4 * QUARTER, cm_o, 0, K // TB)
    store(wq_o, wk_o, wv_o, cm_o)
    x = tok[...]
    q_o[...] = (nn(x, wq_o[...]) + vec[0:1]).astype(BF)
    k_o[...] = (nn(x, wk_o[...]) + vec[1:2]).astype(BF)
    v_o[...] = (nn(x, wv_o[...]) + vec[2:3]).astype(BF)
    store(q_o, k_o, v_o)
    masked = jnp.where(valid_rows(sc[12], K), cm_o[...], jnp.zeros((), BF))
    ks_o[...] = tn(masked, k_o[...]).astype(BF)
    vs_o[...] = tn(masked, v_o[...]).astype(BF)
    for n, ref in enumerate((ks_o, vs_o)):
        square = jnp.square(ref[...].astype(F32))
        total = jnp.sum(jnp.sum(square, axis=0, keepdims=True), axis=1, keepdims=True)
        norm_o[n : n + 1, :] = jnp.broadcast_to(jnp.sqrt(total), (1, LANES))
    lane = lax.broadcasted_iota(jnp.int32, (K, LANES), 1) < HD
    for p in range(H // 2):
        cols = slice(p * LANES, (p + 1) * LANES)
        q_p, ks_p, vs_p = q_o[:, cols], ks_o[:, cols], vs_o[:, cols]
        zero = jnp.zeros((), BF)
        parts, values = [], []
        for half in range(2):
            sel = lane if half == 0 else jnp.logical_not(lane)
            scores = nt(jnp.where(sel, ks_p, zero), q_p) * SCALE
            peak = jnp.max(scores, axis=0, keepdims=True)
            raised = jnp.exp(scores - peak)
            total = jnp.sum(raised, axis=0, keepdims=True)
            lse_o[2 * p + half : 2 * p + half + 1, :] = peak + jnp.log(total)
            parts.append((raised * (1.0 / total)).astype(BF))
            values.append(jnp.where(sel, vs_p, zero))
        mixt = tn(jnp.concatenate(values, axis=0), jnp.concatenate(parts, axis=0)).astype(BF)
        mixt_o[cols, :] = mixt
        mix_o[:, cols] = mixt.T
    store(mixt_o)
    branch = nn(mix_o[...], wo_o[...]) + vec[3:4]
    normed, inverse = layer_norm(x.astype(F32) + branch)
    first = normed * vec[4:5] + vec[5:6]
    fl_o[...] = first.astype(BF)
    store(fl_o)
    acc[...] = first + vec[10:11]
    for at in (2, 3):
        fetched(pieces, raw, sem, at)
    for g in range(FF // STEP):
        cols = slice(g * STEP, (g + 1) * STEP)
        row, off = 6 + (g * STEP) // D, (g * STEP) % D
        hidden = nn(fl_o[...], hidden_columns(raw, slots, g)) + vec[row : row + 1, off : off + STEP]
        phi = 0.5 * (1.0 + lax.erf(hidden * SQRT_HALF))
        low = (hidden * phi).astype(BF)
        act[:, cols] = low
        slope[:, cols] = phi + hidden * INV_SQRT_TWO_PI * jnp.exp(-0.5 * hidden * hidden)
        acc[...] += nn(low, return_rows(raw, slots, g))
    valid = valid_rows(sc[12], D)
    normed2, inverse2 = layer_norm(acc[...])
    result = normed2 * vec[11:12] + vec[12:13]
    out_o[...] = jnp.where(valid, result, 0.0).astype(BF)
    grad_result = jnp.where(valid, cot[...].astype(F32), 0.0)
    sums_o[8:9, :] = column_sum(grad_result * normed2)
    sums_o[9:10, :] = column_sum(grad_result)
    grad_second = norm_backward(grad_result, normed2, inverse2, vec[11:12])
    acc[...] = grad_second
    gsl[...] = grad_second.astype(BF)
    sums_o[7:8, :] = column_sum(gsl[...])
    for g in range(FF // STEP):
        cols = slice(g * STEP, (g + 1) * STEP)
        gh = (nt(gsl[...], return_rows(raw, slots, g)) * slope[:, cols]).astype(BF)
        gh_o[:, cols] = gh
        row, off = (g * STEP) // D, (g * STEP) % D
        sums_o[3 + row : 4 + row, off : off + STEP] = column_sum(gh)
        acc[...] += nt(gh, hidden_columns(raw, slots, g))
        terms = tn(act[:, cols], gsl[...])
        for i in range(STEP // TB):
            for j in range(nd):
                put(keep_o, send_o, (g * (STEP // TB) + i) * nd + j, terms[i * TB : (i + 1) * TB, j * TB : (j + 1) * TB])
    store(gh_o)
    grad_first = acc[...]
    normed, inverse = layer_norm(tok[...].astype(F32) + (nn(mix_o[...], wo_o[...]) + vec[3:4]))
    sums_o[1:2, :] = column_sum(grad_first * normed)
    sums_o[2:3, :] = column_sum(grad_first)
    grad_resid = norm_backward(grad_first, normed, inverse, vec[4:5])
    gr_o[...] = grad_resid
    low = grad_resid.astype(BF)
    gb_o[...] = low
    sums_o[0:1, :] = column_sum(low)
    gm_o[...] = nt(low, wo_o[...]).astype(BF)
    for copy in copies:
        copy.wait()


def attention_backward(sc, tok, q, ks, vs, lse, gm, k, v, gb, mixt, cm, *rest):
    gq_o, gk_o, gv_o, keep_o, send_o, sums_o, gks_o, gvs_o, *held, sem = rest[-15:]
    copies = [
        pltpu.make_async_copy(source, target, sem.at[n])
        for n, (source, target) in enumerate(zip((q, tok, mixt, cm, k, v), held))
    ]
    for copy in copies:
        copy.start()
    q, tok, mixt, cm, k, v = held
    copies[0].wait()
    lane = lax.broadcasted_iota(jnp.int32, (K, LANES), 1) < HD
    zero = jnp.zeros((), BF)
    for p in range(H // 2):
        cols = slice(p * LANES, (p + 1) * LANES)
        q_p, ks_p, vs_p, gm_p = q[:, cols], ks[:, cols], vs[:, cols], gm[:, cols]
        keys, grads, gvs, gks = [], [], [], []
        for half in range(2):
            sel = lane if half == 0 else jnp.logical_not(lane)
            key = jnp.where(sel, ks_p, zero)
            attend = jnp.exp(nt(key, q_p) * SCALE - lse[2 * p + half : 2 * p + half + 1, :])
            grad_attend = nt(jnp.where(sel, vs_p, zero), gm_p)
            mean = jnp.sum(grad_attend * attend, axis=0, keepdims=True)
            grad_scores = (attend * (grad_attend - mean)).astype(BF)
            gvs.append(nn(attend.astype(BF), gm_p))
            gks.append(nn(grad_scores, q_p))
            keys.append(key)
            grads.append(grad_scores)
        gvs_o[:, cols] = jnp.where(lane, gvs[0], gvs[1]).astype(BF)
        gks_o[:, cols] = (jnp.where(lane, gks[0], gks[1]) * SCALE).astype(BF)
        gqt = tn(jnp.concatenate(keys, axis=0), jnp.concatenate(grads, axis=0)) * SCALE
        gq_o[:, cols] = gqt.astype(BF).T
    put = splitter(sc)
    nd, nk = D // TB, K // TB
    for copy in copies[1:]:
        copy.wait()
    masked = jnp.where(valid_rows(sc[12], K), cm[...], zero)
    gk_o[...] = nn(masked, gks_o[...]).astype(BF)
    gv_o[...] = nn(masked, gvs_o[...]).astype(BF)
    tokt = tok[...].T
    lhs = (tokt, tokt, tokt, mixt[...])
    for m, grad in enumerate((gq_o, gk_o, gv_o, gb)):
        if m < 3:
            sums_o[m : m + 1, :] = column_sum(grad[...])
        terms = nn(lhs[m], grad[...])
        for i in range(nd):
            for j in range(nd):
                put(keep_o, send_o, m * QUARTER + i * nd + j, terms[i * TB : (i + 1) * TB, j * TB : (j + 1) * TB])
    comp = nt(k[...], gks_o[...]) + nt(v[...], gvs_o[...])
    comp = jnp.where(valid_rows(sc[12], K), comp, 0.0)
    for i in range(NMAX // TB):
        for j in range(nk):
            put(keep_o, send_o, 4 * QUARTER + i * nk + j, comp[i * TB : (i + 1) * TB, j * TB : (j + 1) * TB])


def closing(sc, fl, gh, gr, gq, gk, gv, wq, wk, wv, *rest):
    keep_o, send_o, in_o, *held, sem = rest[-9:]
    copies = [
        pltpu.make_async_copy(source, target, sem.at[n])
        for n, (source, target) in enumerate(zip((fl, gh, wq, wk, wv), held))
    ]
    for copy in copies:
        copy.start()
    fl, gh, wq, wk, wv = held
    put = splitter(sc)
    for copy in copies[:2]:
        copy.wait()
    nh, nd = FF // TB, D // TB
    flt = fl[...].T
    for g in range(FF // STEP):
        terms = nn(flt, gh[:, g * STEP : (g + 1) * STEP])
        for i in range(nd):
            for j in range(STEP // TB):
                put(keep_o, send_o, i * nh + g * (STEP // TB) + j, terms[i * TB : (i + 1) * TB, j * TB : (j + 1) * TB])
    for copy in copies[2:]:
        copy.wait()
    total = gr[...] + nt(gq[...], wq[...])
    total = total + nt(gk[...], wk[...])
    total = total + nt(gv[...], wv[...])
    in_o[...] = total.astype(BF)


def assemble(at, wide_a, wide_r, wide_x, slim_x, h_half, h_x, *rest):
    rows_o, low_o, scale = rest[-2], rest[-1], at[1].astype(F32)
    upper = at[0] >= 2
    end = at[0] % 3 == 0
    size, slim, late = wide_a.shape[0], slim_x.shape[0], h_half.shape[0]

    def emit(first, count, value):
        low = (value * (1.0 / scale))
        rows_o[first : first + count] = low
        low_o[first : first + count] = low.astype(BF)

    @pl.when(end)
    def _():
        emit(0, size, jnp.where(upper, wide_r[...], wide_a[...]).astype(F32) + wide_x[...].astype(F32))

    @pl.when(at[0] == 1)
    def _():
        emit(0, slim, wide_a[size - slim :].astype(F32) + slim_x[...].astype(F32))
        emit(slim, size - slim, h_half[: size - slim].astype(F32) + h_x[: size - slim].astype(F32))

    @pl.when(at[0] == 2)
    def _():
        emit(0, late, h_half[...].astype(F32) + h_x[...].astype(F32))
        emit(late, size - late, wide_r[: size - late].astype(F32) + slim_x[: size - late].astype(F32))


BATCH = 10


def halves(value):
    high = value.astype(BF)
    return high, (value - high.astype(F32)).astype(BF)


def step_kernel(sc, dec, own, lroot, lstat, rstat, g0, g1, r0, r1, nl_o, nr_o, pre_o, sq_o):
    slots = [sc[r] for r in range(GROUPS)]
    even = sc[13] == 0
    mine = [jnp.where(even, slots[2 * m], slots[2 * m + 1]) for m in range(4)]
    other = [jnp.where(even, slots[2 * m + 1], slots[2 * m]) - HELD for m in range(4)]
    pick_row = lax.broadcasted_iota(jnp.int32, (16, TB), 0) + sc[14] * 16
    select = (lax.broadcasted_iota(jnp.int32, (16, TB), 1) == pick_row).astype(BF)
    start = pl.program_id(0) * BATCH

    def whole(here, there, n):
        rows = []
        for m in range(4):
            a, b = here[mine[m], n], there[other[m], n]
            rows += [jnp.where(even, a, b), jnp.where(even, b, a)]
        return jnp.concatenate(rows, axis=0)

    bs = range(BATCH)
    grads = [whole(g0, g1, n) for n in bs]
    across = [nt(jnp.concatenate([own[n].astype(BF), select], axis=0), g) for n, g in zip(bs, grads)]
    heads = [halves(lroot[n]) for n in bs]
    down = [nn(jnp.concatenate([*h, a[16:].astype(BF)], axis=0), g) for h, a, g in zip(heads, across, grads)]
    mids = [halves(d[:16] + d[16:32]) for d in down]
    last = [nn(jnp.concatenate(m, axis=0), whole(r0, r1, n)) for n, m in zip(bs, mids)]
    for n, a, d, p in zip(bs, across, down, last):
        decay = dec[2 * (start + n)]
        nl_o[n] = decay * lstat[n] + (1.0 - decay) * a[:16]
        decay = dec[2 * (start + n) + 1]
        nr_o[n] = decay * rstat[n] + (1.0 - decay) * d[32:]
        pre = p[:16] + p[16:]
        pre_o[n] = pre
        sq_o[n] = jnp.sum(pre * pre, axis=0, keepdims=True)


def in_hbm(arrays):
    return [pltpu.with_memory_space_constraint(a, pltpu.HBM) for a in arrays]


def call(kernel, ins, outs, in_specs, out_specs=None, scratch=(), limit=60, deps=()):
    return pl.pallas_call(
        kernel,
        out_shape=outs,
        in_specs=in_specs + [ANY] * len(deps),
        out_specs=out_specs or [VM] * len(outs),
        scratch_shapes=list(scratch),
        compiler_params=pltpu.CompilerParams(vmem_limit_bytes=limit * 1024 * 1024),
        cost_estimate=pl.CostEstimate(flops=1, bytes_accessed=1, transcendentals=0),
    )(*ins, *deps)


SLOT_TABLE = (0, 4, 1, 6, 2, 5, 3, 7)


def slot_of(code, core):
    other, x, y = code & 1, (code >> 1) & 1, code >> 2
    return 4 * other + jnp.where((other ^ core) == 0, x + 2 * y, y + 2 * x)


def toward(x, move):
    return lax.ppermute(x, "fsdp", [(i, move(i)) for i in range(GROUPS)])


def near(x):
    return toward(x, lambda i: i ^ 2 if i % 2 == 0 else i ^ 4)


def far(x):
    return toward(x, lambda i: i ^ 4 if i % 2 == 0 else i ^ 2)


def sibling(x):
    return toward(x, lambda i: i ^ 1)


def along(x, pairs):
    return lax.ppermute(x, "dp", pairs)


def gate(index, options, copies, deps=()):
    flat, plan = [], []
    for entry in copies:
        group = entry if isinstance(entry, list) else [entry]
        plan.append((len(flat), len(group) if isinstance(entry, list) else 0))
        flat += group
    count = len(options)
    outs = [sds(options[0].shape, options[0].dtype)] if count else []
    for entry in copies:
        if isinstance(entry, list):
            outs.append(pltpu.HBM((len(entry),) + entry[0].shape, BF))
        else:
            outs.append(pltpu.HBM(entry.shape, BF) if entry.ndim == 4 else sds(entry.shape, BF))

    def kernel(at, *refs):
        sem = refs[-1]
        out = refs[-1 - len(outs) : -1]
        given = refs[count : count + len(flat)]
        started = []
        for n, (first, size) in enumerate(plan):
            target = out[n + (1 if count else 0)]
            for m in range(max(size, 1)):
                copy = pltpu.make_async_copy(
                    given[first + m], target.at[m] if size else target, sem.at[1 + first + m]
                )
                copy.start()
                started.append(copy)
        for n in range(count):

            @pl.when(at[0] == n)
            def _():
                pltpu.make_async_copy(refs[n], out[0], sem.at[0]).start()

        for copy in started:
            copy.wait()
        if count:
            pltpu.make_async_copy(refs[0], out[0], sem.at[0]).wait()

    return pl.pallas_call(
        kernel,
        out_shape=outs,
        in_specs=[SM] + [ANY] * (count + len(flat) + len(deps)),
        out_specs=[ANY] * len(outs),
        scratch_shapes=[pltpu.SemaphoreType.DMA((1 + len(flat),))],
        compiler_params=pltpu.CompilerParams(vmem_limit_bytes=2**20),
        cost_estimate=pl.CostEstimate(flops=1, bytes_accessed=1, transcendentals=0),
    )(index[None], *options, *flat, *deps)


def tie(x, deps):
    def kernel(*refs):
        pass

    return pl.pallas_call(
        kernel,
        out_shape=sds(x.shape, x.dtype),
        in_specs=[ANY] * (1 + len(deps)),
        out_specs=ANY,
        input_output_aliases={0: 0},
        compiler_params=pltpu.CompilerParams(vmem_limit_bytes=2**20),
        cost_estimate=pl.CostEstimate(flops=1, bytes_accessed=1, transcendentals=0),
    )(x, *deps)


def plane_gather(own):
    a = near(own)
    b = far(own)
    c = far(a)
    four = jnp.stack([own, a, b, c])
    return [four, sibling(four)]


def chosen(index, options):
    value = options[0]
    for i in range(1, len(options)):
        value = jnp.where(index == i, options[i], value)
    return value


EDGE = [(0, 1), (1, 0), (2, 3), (3, 2)]
INNER = [(0, 0), (1, 2), (2, 1), (3, 3)]


def gather_weights(narrow):
    z = lax.axis_index("dp")
    e, o = along(narrow, EDGE), along(narrow, INNER)
    a0, b0 = near(narrow), far(narrow)
    t1, a0 = gate(z, [e, e, o, e], [a0], (b0,))
    eo, oe = along(o, EDGE), along(e, INNER)
    a1, b1, c0 = near(t1), far(t1), far(a0)
    t2, a1, four0 = gate(z, [eo, o, oe, eo], [a1, [narrow, a0, b0, c0]], (b1,))
    eoe, d0 = along(oe, EDGE), sibling(four0)
    a2, b2, c1 = near(t2), far(t2), far(a1)
    t3, a2, four1, d0 = gate(z, [eoe, oe, e, eoe], [a2, [t1, a1, b1, c1], d0], (b2,))
    a3, b3, c2, d1 = near(t3), far(t3), far(a2), sibling(four1)
    a3, four2, d1 = gate(z, [], [a3, [t2, a2, b2, c2], d1], (b3,))
    c3, d2 = far(a3), sibling(four2)
    four3, d2 = gate(z, [], [[t3, a3, b3, c3], d2])
    d3 = sibling(four3)
    steps = chosen(z, [jnp.array(row, jnp.int32) for row in ((0, 1, 2, 3), (1, 0, 2, 3), (2, 1, 0, 3), (3, 2, 1, 0))])
    return [four0, d0, four1, d1, four2, d2, four3, d3], steps


def added(a, b, deps=()):
    def kernel(x, y, *rest):
        rest[-1][...] = (x[...].astype(F32) + y[...].astype(F32)).astype(BF)

    return call(kernel, [a, b], [sds(a.shape, BF)], [VM, VM], limit=8, deps=deps)[0]


def core_sum(keep, send, deps=()):
    got = sibling(send)

    def kernel(x, y, *rest):
        own, first, pair = rest[-3:]
        for n, (ref, at) in enumerate(((own, None), (first, None), (pair, 0), (pair, 1))):
            value = (x[n].astype(F32) + y[n].astype(F32)).astype(BF)
            if at is None:
                ref[...] = value
            else:
                ref[at] = value

    one = keep.shape[1:]
    return call(
        kernel, [keep, got], [sds(one, BF), sds(one, BF), sds((2,) + one, BF)], [VM, VM], limit=14,
        deps=deps,
    )


def last_sum(own, back, last, deps=()):
    def kernel(x, y, w, *rest):
        rest[-1][...] = (x[...].astype(F32) + y[0].astype(F32) + w[...].astype(F32)).astype(BF)

    return call(kernel, [own, back, last], [sds(own.shape, BF)], [VM] * 3, limit=8, deps=deps)[0]


def first_sum(first, back, deps=()):
    def kernel(x, y, *rest):
        rest[-1][...] = (x[...].astype(F32) + y[1].astype(F32)).astype(BF)

    return call(kernel, [first, back], [sds(first.shape, BF)], [VM] * 2, limit=8, deps=deps)[0]


CROSS = [(0, 2), (1, 3), (2, 0), (3, 1)]
SKIP = [(0, 1), (1, 3), (2, 0), (3, 2)]
TURN = [(0, 2), (1, 0), (2, 3), (3, 1)]


def pair_parts(odd, rows, cut):
    size = max(cut, rows.shape[0] - cut)
    even_at, odd_at = 0, rows.shape[0] - size
    stay = lax.dynamic_slice_in_dim(rows, jnp.where(odd, odd_at, even_at), size, 0)
    leave = lax.dynamic_slice_in_dim(rows, jnp.where(odd, even_at, odd_at), size, 0)
    return stay, leave


def plane_sum(x):
    for bit in (1, 2, 4):
        x = x + toward(x, lambda i, bit=bit: i ^ bit)
    return x


def local(
    tokens,
    cotangent,
    lengths,
    weights,
    vectors,
    moments,
    left_stats,
    right_stats,
    left_root,
    right_root,
    decays,
):
    dp, fsdp = lax.axis_size("dp"), lax.axis_size("fsdp")
    assert tokens.shape[0] == 1
    staged = (dp, fsdp) == (4, GROUPS)
    seq_total = tokens.shape[0] * dp * fsdp
    tok, cot = tokens[0], cotangent[0]
    narrow = weights.astype(BF)
    if staged:
        me = lax.axis_index("fsdp")
        core = lax.rem(me, 2)
        slots = slot_of(jnp.arange(GROUPS, dtype=jnp.int32) ^ me, core)
        pieces, steps = gather_weights(narrow)
    else:
        me = jnp.int32(0)
        core = jnp.int32(0)
        slots = slot_of(jnp.arange(GROUPS, dtype=jnp.int32), core)
        full = lax.all_gather(lax.all_gather(narrow, "dp", axis=0, tiled=True), "fsdp", axis=1, tiled=True)
        full = full.reshape(NBLK // PART, PART, GROUPS, TB // GROUPS, TB)
        place = [SLOT_TABLE.index(s) for s in range(GROUPS)]
        pieces = []
        for t in range(NBLK // PART):
            every = [full[t, :, place[s]] for s in range(GROUPS)]
            pieces += [jnp.stack(every[:HELD]), jnp.stack(every[HELD:])]
        steps = jnp.arange(4, dtype=jnp.int32)
    scalars = jnp.concatenate([slots, steps, lengths, core[None], me[None]]).astype(jnp.int32)

    row16 = TB // GROUPS
    act = sds((NMAX, D), BF)
    wide = sds((NMAX, D), F32)
    summary = sds((K, D), BF)
    shape = (NMAX, D)
    square = (D, D)
    r_terms = sds((4, HID, row16, TB), BF)
    a_terms = sds((4, ATT, row16, TB), BF)
    held = [square, square, square, (NMAX, K), shape, shape, shape, (D, NMAX), shape, (NMAX, FF)]
    (wq, wk, wv, cm, q, k, v, mixt, fl, gh,
     ks, vs, lse, norms, out, gr, gb, gm, r_keep, r_send, sums_b) = call(
        layer,
        [scalars, tok, cot, vectors] + in_hbm(pieces),
        [pltpu.HBM(one, BF) for one in held]
        + [summary, summary, sds((H, NMAX), F32), sds((2, LANES), F32), act, wide, act, act, r_terms, r_terms, sds((10, D), F32)],
        [SM, VM, VM, VM] + [ANY] * (4 * SET),
        [ANY] * KEPT + [VM] * 11,
        scratch=[
            pltpu.VMEM((4, GROUPS, PART, row16, TB), BF),
            *[pltpu.VMEM(one, BF) for one in (shape, shape, shape, (D, NMAX), square, square, square, square, (NMAX, K), shape, shape, (NMAX, FF))],
            pltpu.VMEM((NMAX, FF), F32),
            pltpu.VMEM((NMAX, FF), BF),
            pltpu.VMEM(shape, BF),
            pltpu.VMEM(shape, F32),
            pltpu.SemaphoreType.DMA((4, GROUPS)),
            pltpu.SemaphoreType.DMA((KEPT,)),
        ],
        limit=58,
    )
    deps = ()
    if staged:
        r_here, r_first, r_pair = core_sum(r_keep, r_send)
        r_back = far(r_pair)
        deps = (r_pair,)
    gq, gk, gv, a_keep, a_send, sums_a = call(
        attention_backward,
        [scalars, *in_hbm([tok, q]), ks, vs, lse, gm, *in_hbm([k, v]), gb, *in_hbm([mixt, cm])],
        [act, act, act, a_terms, a_terms, sds((3, D), F32)],
        [SM, ANY, ANY] + [VM] * 4 + [ANY, ANY, VM, ANY, ANY],
        scratch=[
            *[pltpu.VMEM(one, BF) for one in ((K, D), (K, D), shape, shape, (D, NMAX), (NMAX, K), shape, shape)],
            pltpu.SemaphoreType.DMA((6,)),
        ],
        limit=28, deps=deps,
    )
    if staged:
        r_first = first_sum(r_first, r_back)
        r_last = near(r_first)
        a_here, a_first, a_pair = core_sum(a_keep, tie(a_send, (r_first,)), (r_last,))
        r_rows = last_sum(r_here, r_back, r_last)
        r_stay, r_leave = pair_parts(lax.axis_index("dp") % 2 == 1, r_rows, 3 * PART - (ATT + HID))
        a_back = far(a_pair)
        r_came = along(r_leave, EDGE)
        deps = (a_pair, r_leave)
    h_keep, h_send, in_grads = call(
        closing,
        [scalars, *in_hbm([fl, gh]), gr, gq, gk, gv, *in_hbm([wq, wk, wv])],
        [r_terms, r_terms, act],
        [SM, ANY, ANY] + [VM] * 4 + [ANY] * 3,
        scratch=[
            *[pltpu.VMEM(one, BF) for one in (shape, (NMAX, FF), square, square, square)],
            pltpu.SemaphoreType.DMA((5,)),
        ],
        limit=28, deps=deps,
    )
    local_vectors = jnp.concatenate([sums_a, sums_b], axis=0)
    local_norms = norms[:, 0]
    if staged:
        z = lax.axis_index("dp")
        odd = z % 2 == 1
        cut_r = 3 * PART - (ATT + HID)
        cut_h = 2 * PART - ATT
        rest_a, rest_h = ATT - PART, HID - cut_h
        packed = jnp.concatenate([local_vectors, jnp.pad(local_norms[None], ((0, 0), (0, D - 2)))], axis=0)
        packed = packed + sibling(packed)
        a_first = first_sum(a_first, a_back, (r_came, packed))
        r_half = added(r_stay, r_came, (a_back,))
        a_last = near(a_first)
        packed = packed + toward(packed, lambda i: i ^ 2)
        h_here, h_first, h_pair = core_sum(h_keep, tie(h_send, (a_first,)), (a_last, packed))
        a_rows = last_sum(a_here, a_back, a_last)
        h_back = far(h_pair)
        a_stay, a_leave = pair_parts(odd, a_rows, PART)
        a_came = along(a_leave, EDGE)
        packed = packed + toward(packed, lambda i: i ^ 4)
        h_first = first_sum(h_first, h_back, (a_came, packed))
        a_half = added(a_stay, a_came, (h_back,))
        h_last = near(h_first)
        upper = z >= 2
        wide_cross = along(jnp.where(upper, a_half, r_half), SKIP)
        slim_cross = along(jnp.where(upper, a_half[PART - rest_a :], r_half[:rest_a]), TURN)
        packed = packed + along(packed, EDGE)
        h_rows = last_sum(h_here, h_back, h_last, (wide_cross, slim_cross, packed))
        h_stay = lax.dynamic_slice_in_dim(h_rows, jnp.where(odd, 0, cut_h), rest_h, 0)
        h_leave = lax.dynamic_slice_in_dim(h_rows, jnp.where(odd, cut_h, 0), rest_h, 0)
        h_came = along(h_leave, EDGE)
        root = right_root.astype(BF)
        root_near, root_far = near(root), far(root)
        packed = packed + along(packed, CROSS)
        h_half = added(h_stay, h_came, (root_near, root_far, packed))
        h_cross = along(h_half, TURN)
        root_diag = far(root_near)
        grad_rows, low_rows = call(
            assemble,
            [jnp.stack([z, jnp.int32(seq_total)]), a_half, r_half, wide_cross, slim_cross, h_half, h_cross],
            [sds(weights.shape, F32), sds(weights.shape, BF)],
            [SM] + [VM] * 6,
            limit=8, deps=(root_diag,),
        )
        vector_total, norm_totals = packed[:-1], packed[-1, :2]
        root_four = jnp.stack([root, root_near, root_far, root_diag])
        blocks = plane_gather(low_rows) + [root_four, sibling(root_four)]
        rows = sds(weights.shape, F32)
        one = pl.BlockSpec((BATCH, row16, TB), lambda n: (n, 0, 0))
        four = pl.BlockSpec((HELD, BATCH, row16, TB), lambda n: (0, n, 0, 0))
        new_left, new_right, precond, squares = pl.pallas_call(
            step_kernel,
            grid=(PART // BATCH,),
            out_shape=[rows, rows, rows, sds((PART, 1, LANES), F32)],
            in_specs=[SM, SM] + [one] * 4 + [four] * 4,
            out_specs=[one, one, one, pl.BlockSpec((BATCH, 1, LANES), lambda n: (n, 0, 0))],
            compiler_params=pltpu.CompilerParams(vmem_limit_bytes=16 * 1024 * 1024),
            cost_estimate=pl.CostEstimate(flops=1, bytes_accessed=1, transcendentals=0),
        )(scalars, decays.reshape(-1), grad_rows, left_root, left_stats, right_stats, *blocks)
        squares = squares[:, 0]
        both = jnp.stack([jnp.sum(squares, axis=1), jnp.sum(weights * weights, axis=(1, 2))])
        precond_squares, weight_squares = plane_sum(both)
    else:
        def join(keep, send):
            both = jnp.concatenate([keep, send], axis=0)
            return jnp.stack([both[s] for s in SLOT_TABLE], axis=1).reshape(-1, TB, TB)

        every = jnp.concatenate([join(a_keep, a_send), join(h_keep, h_send), join(r_keep, r_send)], axis=0)
        inner = lax.psum_scatter(every, "fsdp", scatter_dimension=1, tiled=True)
        total = lax.psum_scatter(inner, "dp", scatter_dimension=0, tiled=True).astype(F32)
        grad_rows = total / seq_total
        vector_total, norm_totals = lax.psum((local_vectors, local_norms), ("dp", "fsdp"))
        high = lax.Precision.HIGHEST
        whole = lax.all_gather(grad_rows.astype(BF), "fsdp", axis=1, tiled=True).astype(F32)
        count = grad_rows.shape[1]
        slab = lax.dynamic_slice_in_dim(whole, lax.axis_index("fsdp") * count, count, 2)
        gram_left = jnp.einsum("brc,bsc->brs", grad_rows, whole, precision=high)
        gram_right = jnp.einsum("bic,bis->bcs", slab, whole, precision=high)
        decay_left = decays[:, 0][:, None, None]
        decay_right = decays[:, 1][:, None, None]
        new_left = decay_left * left_stats + (1.0 - decay_left) * gram_left
        new_right = decay_right * right_stats + (1.0 - decay_right) * gram_right
        columns = jnp.einsum("bis,bcs->bic", whole, right_root, precision=high)
        applied = lax.all_gather(columns.astype(BF), "fsdp", axis=2, tiled=True).astype(F32)
        precond = jnp.einsum("brs,bsc->brc", left_root, applied, precision=high)
        precond_squares, weight_squares = lax.psum(
            (jnp.sum(precond * precond, axis=(1, 2)), jnp.sum(weights * weights, axis=(1, 2))), "fsdp"
        )
    vector_grad = vector_total / seq_total
    summary_norms = norm_totals / seq_total
    tile_area = TB * TB
    weight_scale = jnp.sqrt(weight_squares / tile_area)
    precond_scale = lax.rsqrt(precond_squares / tile_area + EPS_STEP)
    new_weights = weights - STEP_RATE * (weight_scale * precond_scale)[:, None, None] * precond
    new_moments = MOMENT_DECAY * moments + (1.0 - MOMENT_DECAY) * vector_grad
    row_scale = jnp.sqrt(jnp.mean(jnp.square(vectors), axis=1, keepdims=True))
    moment_scale = lax.rsqrt(jnp.mean(jnp.square(new_moments), axis=1, keepdims=True) + EPS_STEP)
    new_vectors = vectors - STEP_RATE * row_scale * new_moments * moment_scale
    return (
        out[None],
        in_grads[None],
        new_weights,
        grad_rows,
        new_left,
        new_right,
        new_vectors,
        new_moments,
        summary_norms,
    )


def solution(mesh):
    in_specs = (
        P(("dp", "fsdp"), None, None),
        P(("dp", "fsdp"), None, None),
        P(("dp", "fsdp")),
        P("dp", "fsdp", None),
        P(),
        P(),
        P("dp", "fsdp", None),
        P("dp", "fsdp", None),
        P("dp", "fsdp", None),
        P("dp", "fsdp", None),
        P("dp", None),
    )
    out_specs = (
        P(("dp", "fsdp"), None, None),
        P(("dp", "fsdp"), None, None),
        P("dp", "fsdp", None),
        P("dp", "fsdp", None),
        P("dp", "fsdp", None),
        P("dp", "fsdp", None),
        P(),
        P(),
        P(),
    )
    return jax.shard_map(local, mesh=mesh, in_specs=in_specs, out_specs=out_specs, check_vma=False)
```

```python
import functools

import jax
import jax.numpy as jnp
from jax import lax
from jax.experimental import pallas as pl
from jax.experimental.pallas import tpu as pltpu
from jax.sharding import PartitionSpec as P

D = 768
H = 12
HD = 64
FF = 3072
K = 256
NMAX = 512
TB = 128
LANES = 128
PART = 110
GROUPS = 8

EPS_NORM = 1e-05
EPS_STEP = 1e-06
STEP_RATE = 0.25
MOMENT_DECAY = 0.9
SQRT_HALF = 0.7071067811865476
INV_SQRT_TWO_PI = 0.3989422804014327
SCALE = HD ** (-0.5)

QUARTER = (D // TB) ** 2
ATT = 4 * QUARTER + NMAX // TB * (K // TB)
HID = D // TB * (FF // TB)
NBLK = ATT + 2 * HID
BF = jnp.bfloat16
F32 = jnp.float32

ANY = pl.BlockSpec(memory_space=pl.ANY)
VM = pl.BlockSpec(memory_space=pltpu.VMEM)
SM = pl.BlockSpec(memory_space=pltpu.SMEM)


def sds(shape, dtype):
    return jax.ShapeDtypeStruct(shape, dtype)


def nn(a, b):
    return lax.dot_general(a, b, (((1,), (0,)), ((), ())), preferred_element_type=F32)


def nt(a, b):
    return lax.dot_general(a, b, (((1,), (1,)), ((), ())), preferred_element_type=F32)


def tn(a, b):
    return lax.dot_general(a, b, (((0,), (0,)), ((), ())), preferred_element_type=F32)


def layer_norm(value):
    centre = jnp.mean(value, axis=-1, keepdims=True)
    shifted = value - centre
    spread = jnp.mean(shifted * shifted, axis=-1, keepdims=True)
    inverse = lax.rsqrt(spread + EPS_NORM)
    return shifted * inverse, inverse


def norm_backward(grad_out, normed, inverse, gain):
    scaled = grad_out * gain
    centred = scaled - jnp.mean(scaled, axis=-1, keepdims=True)
    return inverse * (centred - normed * jnp.mean(scaled * normed, axis=-1, keepdims=True))


def column_sum(value):
    return jnp.sum(value.astype(F32), axis=0, keepdims=True)


def valid_rows(length, width):
    return lax.broadcasted_iota(jnp.int32, (NMAX, width), 0) < length


HELD = GROUPS // 2
ARRAYS = 10


def piece_at(pieces, step, s):
    if step < 3:
        return pieces[2 * step + s // HELD].at[s % HELD]
    trio, last = pieces[6 + 2 * (s // HELD)], pieces[7 + 2 * (s // HELD)]
    return last if s % HELD == HELD - 1 else trio.at[s % HELD]


def fetch(sc, pieces, raw, sem):
    for part in range(4):
        for step in range(4):

            @pl.when(sc[8 + part] == step)
            def _():
                for s in range(GROUPS):
                    pltpu.make_async_copy(piece_at(pieces, step, s), raw.at[part, s], sem.at[part, s]).start()


def fetched(pieces, raw, sem, part):
    for s in range(GROUPS):
        pltpu.make_async_copy(piece_at(pieces, 0, s), raw.at[part, s], sem.at[part, s]).wait()


def lay_out(slots, raw, at, first, count, dst, dst_first, per_row):
    for n in range(count):
        i, j = divmod(n + dst_first, per_row)
        for r in range(GROUPS):
            dst[i * TB + 16 * r : i * TB + 16 * r + 16, j * TB : (j + 1) * TB] = raw[at, slots[r], first + n]


def splitter(sc):
    even = sc[13] == 0
    mine = [jnp.where(even, sc[2 * m], sc[2 * m + 1]) for m in range(4)]
    other = [jnp.where(even, sc[2 * m + 1], sc[2 * m]) - 4 for m in range(4)]

    def put(keep, send, b, value):
        low = value.astype(BF)
        for m in range(4):
            first = low[32 * m : 32 * m + 16]
            second = low[32 * m + 16 : 32 * m + 32]
            keep[mine[m], b] = jnp.where(even, first, second)
            send[other[m], b] = jnp.where(even, second, first)

    return put


SHIPPED = 5


def shipped(keep, send, outs, span, sem):
    cuts = [(keep, pl.ds(0, 2)), (keep, pl.ds(2, 2)), (send, pl.ds(0, 2)), (send, 2), (send, 3)]
    return [
        pltpu.make_async_copy(source.at[at, span], out.at[span] if isinstance(at, int) else out.at[:, span], sem.at[n])
        for n, ((source, at), out) in enumerate(zip(cuts, outs))
    ]


def shipped_shapes(count):
    one = (count, TB // GROUPS, TB)
    return [pltpu.HBM((2,) + one, BF)] * 3 + [pltpu.HBM(one, BF)] * 2


STEP = 256


def tiles(raw, slots, block):
    part, b = divmod(block, PART)
    return [raw[part, slots[r], b] for r in range(GROUPS)]


def hidden_columns(raw, slots, g):
    count = STEP // TB
    rows = []
    for i in range(D // TB):
        blocks = [tiles(raw, slots, ATT + i * (FF // TB) + g * count + c) for c in range(count)]
        rows += [jnp.concatenate([block[r] for block in blocks], axis=1) for r in range(GROUPS)]
    return jnp.concatenate(rows, axis=0)


def return_rows(raw, slots, g):
    count = STEP // TB
    rows = []
    for i in range(count):
        blocks = [tiles(raw, slots, ATT + HID + (g * count + i) * (D // TB) + j) for j in range(D // TB)]
        rows += [jnp.concatenate([block[r] for block in blocks], axis=1) for r in range(GROUPS)]
    return jnp.concatenate(rows, axis=0)


KEPT = 19


def layer(sc, tok, cot, vec, *rest):
    pieces, rest = rest[:ARRAYS], rest[ARRAYS:]
    stored, rest = rest[:KEPT], rest[KEPT:]
    ks_o, vs_o, lse_o, norm_o, sums_o = rest[:5]
    (raw, q_o, k_o, v_o, mixt_o, wq_o, wk_o, wv_o, wo_o, cm_o, mix_o, fl_o, gh_o, slope, act, gsl, acc, nf, ni,
     cot_v, out_o, gr_o, gb_o, gm_o, keep_o, send_o, sem, osem, csem, tsem) = rest[5:]
    fetch(sc, pieces, raw, sem)
    cot_copy = pltpu.make_async_copy(cot, cot_v, csem)
    cot_copy.start()
    slots = [sc[r] for r in range(GROUPS)]
    put = splitter(sc)
    nb = nd = D // TB
    copies = []

    def store(*refs):
        for ref in refs:
            copy = pltpu.make_async_copy(ref, stored[len(copies)], osem.at[len(copies)])
            copy.start()
            copies.append(copy)

    fetched(pieces, raw, sem, 0)
    for m, dst in enumerate((wq_o, wk_o, wv_o)):
        lay_out(slots, raw, 0, m * QUARTER, QUARTER, dst, 0, nb)
    head = PART - 3 * QUARTER
    lay_out(slots, raw, 0, 3 * QUARTER, head, wo_o, 0, nb)
    x = tok[...]
    q_o[...] = (nn(x, wq_o[...]) + vec[0:1]).astype(BF)
    k_o[...] = (nn(x, wk_o[...]) + vec[1:2]).astype(BF)
    v_o[...] = (nn(x, wv_o[...]) + vec[2:3]).astype(BF)
    fetched(pieces, raw, sem, 1)
    lay_out(slots, raw, 1, 0, QUARTER - head, wo_o, head, nb)
    lay_out(slots, raw, 1, QUARTER - head, ATT - 4 * QUARTER, cm_o, 0, K // TB)
    store(wq_o, wk_o, wv_o, cm_o, q_o, k_o, v_o)
    masked = jnp.where(valid_rows(sc[12], K), cm_o[...], jnp.zeros((), BF))
    ks_o[...] = tn(masked, k_o[...]).astype(BF)
    vs_o[...] = tn(masked, v_o[...]).astype(BF)
    for n, ref in enumerate((ks_o, vs_o)):
        square = jnp.square(ref[...].astype(F32))
        total = jnp.sum(jnp.sum(square, axis=0, keepdims=True), axis=1, keepdims=True)
        norm_o[n : n + 1, :] = jnp.broadcast_to(jnp.sqrt(total), (1, LANES))
    lane = lax.broadcasted_iota(jnp.int32, (K, LANES), 1) < HD
    for p in range(H // 2):
        cols = slice(p * LANES, (p + 1) * LANES)
        q_p, ks_p, vs_p = q_o[:, cols], ks_o[:, cols], vs_o[:, cols]
        zero = jnp.zeros((), BF)
        parts, values = [], []
        for half in range(2):
            sel = lane if half == 0 else jnp.logical_not(lane)
            scores = nt(jnp.where(sel, ks_p, zero), q_p) * SCALE
            peak = jnp.max(scores, axis=0, keepdims=True)
            raised = jnp.exp(scores - peak)
            total = jnp.sum(raised, axis=0, keepdims=True)
            lse_o[2 * p + half : 2 * p + half + 1, :] = peak + jnp.log(total)
            parts.append((raised * (1.0 / total)).astype(BF))
            values.append(jnp.where(sel, vs_p, zero))
        mixt = tn(jnp.concatenate(values, axis=0), jnp.concatenate(parts, axis=0)).astype(BF)
        mixt_o[cols, :] = mixt
        mix_o[:, cols] = mixt.T
    store(mixt_o)
    branch = nn(mix_o[...], wo_o[...]) + vec[3:4]
    normed, inverse = layer_norm(x.astype(F32) + branch)
    nf[...] = normed
    ni[...] = jnp.broadcast_to(inverse, (NMAX, LANES))
    first = normed * vec[4:5] + vec[5:6]
    fl_o[...] = first.astype(BF)
    store(fl_o)
    acc[...] = first + vec[10:11]
    for at in (2, 3):
        fetched(pieces, raw, sem, at)
    for g in range(FF // STEP):
        cols = slice(g * STEP, (g + 1) * STEP)
        row, off = 6 + (g * STEP) // D, (g * STEP) % D
        hidden = nn(fl_o[...], hidden_columns(raw, slots, g)) + vec[row : row + 1, off : off + STEP]
        phi = 0.5 * (1.0 + lax.erf(hidden * SQRT_HALF))
        low = (hidden * phi).astype(BF)
        act[:, cols] = low
        slope[:, cols] = phi + hidden * INV_SQRT_TWO_PI * jnp.exp(-0.5 * hidden * hidden)
        acc[...] += nn(low, return_rows(raw, slots, g))
    valid = valid_rows(sc[12], D)
    normed2, inverse2 = layer_norm(acc[...])
    result = normed2 * vec[11:12] + vec[12:13]
    out_o[...] = jnp.where(valid, result, 0.0).astype(BF)
    store(out_o)
    cot_copy.wait()
    grad_result = jnp.where(valid, cot_v[...].astype(F32), 0.0)
    sums_o[8:9, :] = column_sum(grad_result * normed2)
    sums_o[9:10, :] = column_sum(grad_result)
    grad_second = norm_backward(grad_result, normed2, inverse2, vec[11:12])
    acc[...] = grad_second
    gsl[...] = grad_second.astype(BF)
    sums_o[7:8, :] = column_sum(gsl[...])
    for g in range(FF // STEP):
        cols = slice(g * STEP, (g + 1) * STEP)
        gh = (nt(gsl[...], return_rows(raw, slots, g)) * slope[:, cols]).astype(BF)
        gh_o[:, cols] = gh
        row, off = (g * STEP) // D, (g * STEP) % D
        sums_o[3 + row : 4 + row, off : off + STEP] = column_sum(gh)
        acc[...] += nt(gh, hidden_columns(raw, slots, g))
        terms = tn(act[:, cols], gsl[...])
        for i in range(STEP // TB):
            for j in range(nd):
                put(keep_o, send_o, (g * (STEP // TB) + i) * nd + j, terms[i * TB : (i + 1) * TB, j * TB : (j + 1) * TB])
        span = pl.ds(g * (STEP // TB) * nd, (STEP // TB) * nd)
        for copy in shipped(keep_o, send_o, stored[-SHIPPED:], span, tsem.at[g]):
            copy.start()
    store(gh_o)
    grad_first = acc[...]
    normed, inverse = nf[...], ni[:, 0:1]
    sums_o[1:2, :] = column_sum(grad_first * normed)
    sums_o[2:3, :] = column_sum(grad_first)
    grad_resid = norm_backward(grad_first, normed, inverse, vec[4:5])
    gr_o[...] = grad_resid
    low = grad_resid.astype(BF)
    gb_o[...] = low
    sums_o[0:1, :] = column_sum(low)
    store(gr_o, gb_o)
    gm_o[...] = nt(low, wo_o[...]).astype(BF)
    store(gm_o)
    for copy in copies:
        copy.wait()
    for g in range(FF // STEP):
        span = pl.ds(g * (STEP // TB) * nd, (STEP // TB) * nd)
        for copy in shipped(keep_o, send_o, stored[-SHIPPED:], span, tsem.at[g]):
            copy.wait()


def attention_backward(sc, tok, q, ks, vs, lse, gm, k, v, gb, mixt, cm, *rest):
    gq_o, gk_o, gv_o, sums_o, *outs = rest[-23:-14]
    gks_o, gvs_o, keep_o, send_o, *held, sem, tsem = rest[-14:]
    ships = []

    def ship(n, first, count):
        for copy in shipped(keep_o, send_o, outs, pl.ds(first, count), tsem.at[n]):
            copy.start()
            ships.append(copy)

    copies = [
        pltpu.make_async_copy(source, target, sem.at[n])
        for n, (source, target) in enumerate(zip((q, gm, tok, mixt, cm, k, v, gb), held))
    ]
    for copy in copies:
        copy.start()
    q, gm, tok, mixt, cm, k, v, gb = held
    for copy in copies[:2]:
        copy.wait()
    lane = lax.broadcasted_iota(jnp.int32, (K, LANES), 1) < HD
    zero = jnp.zeros((), BF)
    for p in range(H // 2):
        cols = slice(p * LANES, (p + 1) * LANES)
        q_p, ks_p, vs_p, gm_p = q[:, cols], ks[:, cols], vs[:, cols], gm[:, cols]
        keys, grads, gvs, gks = [], [], [], []
        for half in range(2):
            sel = lane if half == 0 else jnp.logical_not(lane)
            key = jnp.where(sel, ks_p, zero)
            attend = jnp.exp(nt(key, q_p) * SCALE - lse[2 * p + half : 2 * p + half + 1, :])
            grad_attend = nt(jnp.where(sel, vs_p, zero), gm_p)
            mean = jnp.sum(grad_attend * attend, axis=0, keepdims=True)
            grad_scores = (attend * (grad_attend - mean)).astype(BF)
            gvs.append(nn(attend.astype(BF), gm_p))
            gks.append(nn(grad_scores, q_p))
            keys.append(key)
            grads.append(grad_scores)
        gvs_o[:, cols] = jnp.where(lane, gvs[0], gvs[1]).astype(BF)
        gks_o[:, cols] = (jnp.where(lane, gks[0], gks[1]) * SCALE).astype(BF)
        gqt = tn(jnp.concatenate(keys, axis=0), jnp.concatenate(grads, axis=0)) * SCALE
        gq_o[:, cols] = gqt.astype(BF).T
    put = splitter(sc)
    nd, nk = D // TB, K // TB
    for copy in copies[2:]:
        copy.wait()
    masked = jnp.where(valid_rows(sc[12], K), cm[...], zero)
    gk_o[...] = nn(masked, gks_o[...]).astype(BF)
    gv_o[...] = nn(masked, gvs_o[...]).astype(BF)
    tokt = tok[...].T
    lhs = (tokt, tokt, tokt, mixt[...])
    for m, grad in enumerate((gq_o, gk_o, gv_o, gb)):
        if m < 3:
            sums_o[m : m + 1, :] = column_sum(grad[...])
        terms = nn(lhs[m], grad[...])
        for i in range(nd):
            for j in range(nd):
                put(keep_o, send_o, m * QUARTER + i * nd + j, terms[i * TB : (i + 1) * TB, j * TB : (j + 1) * TB])
        ship(m, m * QUARTER, QUARTER)
    comp = nt(k[...], gks_o[...]) + nt(v[...], gvs_o[...])
    comp = jnp.where(valid_rows(sc[12], K), comp, 0.0)
    for i in range(NMAX // TB):
        for j in range(nk):
            put(keep_o, send_o, 4 * QUARTER + i * nk + j, comp[i * TB : (i + 1) * TB, j * TB : (j + 1) * TB])
    ship(4, 4 * QUARTER, ATT - 4 * QUARTER)
    for copy in ships:
        copy.wait()


def closing(sc, fl, gh, gr, gq, gk, gv, wq, wk, wv, *rest):
    in_o, *outs = rest[-16:-10]
    keep_o, send_o, *held, gr_v, sem, tsem = rest[-10:]
    copies = [
        pltpu.make_async_copy(source, target, sem.at[n])
        for n, (source, target) in enumerate(zip((fl, gh, wq, wk, wv, gr), (*held, gr_v)))
    ]
    for copy in copies:
        copy.start()
    fl, gh, wq, wk, wv = held
    put = splitter(sc)
    for copy in copies[:2]:
        copy.wait()
    nh, nd = FF // TB, D // TB
    flt = fl[...].T
    for g in range(FF // STEP):
        terms = nn(flt, gh[:, g * STEP : (g + 1) * STEP])
        for i in range(nd):
            for j in range(STEP // TB):
                put(keep_o, send_o, i * nh + g * (STEP // TB) + j, terms[i * TB : (i + 1) * TB, j * TB : (j + 1) * TB])
    ships = shipped(keep_o, send_o, outs, pl.ds(0, HID), tsem)
    for copy in ships:
        copy.start()
    for copy in copies[2:]:
        copy.wait()
    total = gr_v[...] + nt(gq[...], wq[...])
    total = total + nt(gk[...], wk[...])
    total = total + nt(gv[...], wv[...])
    in_o[...] = total.astype(BF)
    for copy in ships:
        copy.wait()


def assemble(at, wide_a, wide_r, wide_x, slim_x, h_stay, h_x, h_y, h_z, *rest):
    rows_o, low_o, scale = rest[-2], rest[-1], at[1].astype(F32)
    upper = at[0] >= 2
    size, slim, late = wide_a.shape[0], slim_x.shape[0], h_stay.shape[0]

    def emit(first, count, value):
        value = value * (1.0 / scale)
        rows_o[first : first + count] = value
        low_o[first : first + count] = value.astype(BF)

    def hidden(count):
        value = h_stay[:count].astype(F32)
        for ref in (h_x, h_y, h_z):
            value = value + ref[:count].astype(F32)
        return value

    @pl.when(at[0] % 3 == 0)
    def _():
        emit(0, size, jnp.where(upper, wide_r[...], wide_a[...]).astype(F32) + wide_x[...].astype(F32))

    @pl.when(at[0] == 1)
    def _():
        emit(0, slim, wide_a[size - slim :].astype(F32) + slim_x[...].astype(F32))
        emit(slim, size - slim, hidden(size - slim))

    @pl.when(at[0] == 2)
    def _():
        emit(0, late, hidden(late))
        emit(late, size - late, wide_r[: size - late].astype(F32) + slim_x[: size - late].astype(F32))


BATCH = 22


def halves(value):
    high = value.astype(BF)
    return high, (value - high.astype(F32)).astype(BF)


def step_kernel(sc, dec, size, own, lroot, lstat, rstat, weight, *rest):
    here, there, lefts, rights = (rest[n * HELD : (n + 1) * HELD] for n in (0, 1, 2, 4))
    other_lefts, other_rights = rest[3 * HELD : 4 * HELD], rest[5 * HELD : 6 * HELD]
    nw_o, nl_o, nr_o = rest[6 * HELD :]
    slots = [sc[r] for r in range(GROUPS)]
    even = sc[13] == 0
    mine = [jnp.where(even, slots[2 * m], slots[2 * m + 1]) for m in range(4)]
    other = [jnp.where(even, slots[2 * m + 1], slots[2 * m]) - HELD for m in range(4)]
    pick_row = lax.broadcasted_iota(jnp.int32, (16, TB), 0) + sc[14] * 16
    select = (lax.broadcasted_iota(jnp.int32, (16, TB), 1) == pick_row).astype(BF)
    start = pl.program_id(0) * BATCH

    def ordered(pairs):
        rows = []
        for a, b in pairs:
            rows += [jnp.where(even, a, b), jnp.where(even, b, a)]
        return jnp.concatenate(rows, axis=0)

    def tile(refs, slot, n):
        value = refs[0][n]
        for at in range(1, HELD):
            value = jnp.where(slot == at, refs[at][n], value)
        return value

    def whole(here, there, n):
        return ordered([(tile(here, mine[m], n), tile(there, other[m], n)) for m in range(4)])

    bs = range(BATCH)
    grads = [whole(here, there, n) for n in bs]
    across = [nt(jnp.concatenate([own[n].astype(BF), select], axis=0), g) for n, g in zip(bs, grads)]
    left = [jnp.concatenate([whole(lefts, other_lefts, n), *halves(lroot[n])], axis=0) for n in bs]
    down = [nn(jnp.concatenate([f, a[16:].astype(BF)], axis=0), g) for f, a, g in zip(left, across, grads)]
    mids = [
        jnp.concatenate([d[:TB].astype(BF), *halves(d[TB : TB + 16] + d[TB + 16 : TB + 32])], axis=0) for d in down
    ]
    last = [nn(m, whole(rights, other_rights, n)) for n, m in zip(bs, mids)]
    for n, a, d, p in zip(bs, across, down, last):
        decay = dec[2 * (start + n)]
        nl_o[n] = decay * lstat[n] + (1.0 - decay) * a[:16]
        decay = dec[2 * (start + n) + 1]
        nr_o[n] = decay * rstat[n] + (1.0 - decay) * d[TB + 32 :]
        full = p[:TB]
        squares = jnp.sum(jnp.sum(full * full, axis=0, keepdims=True), axis=1, keepdims=True)
        scale = size[start + n] * lax.rsqrt(squares * (1.0 / (TB * TB)) + EPS_STEP)
        nw_o[n] = weight[n] - STEP_RATE * scale * (p[TB : TB + 16] + p[TB + 16 :])


def in_hbm(arrays):
    return [pltpu.with_memory_space_constraint(a, pltpu.HBM) for a in arrays]


def call(kernel, ins, outs, in_specs, out_specs=None, scratch=(), limit=60, deps=()):
    return pl.pallas_call(
        kernel,
        out_shape=outs,
        in_specs=in_specs + [ANY] * len(deps),
        out_specs=out_specs or [VM] * len(outs),
        scratch_shapes=list(scratch),
        compiler_params=pltpu.CompilerParams(vmem_limit_bytes=limit * 1024 * 1024),
        cost_estimate=pl.CostEstimate(flops=1, bytes_accessed=1, transcendentals=0),
    )(*ins, *deps)


SLOT_TABLE = (0, 4, 1, 6, 2, 5, 3, 7)


def slot_of(code, core):
    other, x, y = code & 1, (code >> 1) & 1, code >> 2
    return 4 * other + jnp.where((other ^ core) == 0, x + 2 * y, y + 2 * x)


def toward(x, move):
    return lax.ppermute(x, "fsdp", [(i, move(i)) for i in range(GROUPS)])


def near(x):
    return toward(x, lambda i: i ^ 2 if i % 2 == 0 else i ^ 4)


def far(x):
    return toward(x, lambda i: i ^ 4 if i % 2 == 0 else i ^ 2)


def sibling(x):
    return toward(x, lambda i: i ^ 1)


def along(x, pairs):
    return lax.ppermute(x, "dp", pairs)


def gate(index, options, copies, deps=()):
    flat, plan = [], []
    for entry in copies:
        group = entry if isinstance(entry, list) else [entry]
        plan.append((len(flat), len(group) if isinstance(entry, list) else 0))
        flat += group
    count = len(options)
    outs = [sds(options[0].shape, options[0].dtype)] if count else []
    for entry in copies:
        if isinstance(entry, list):
            outs.append(pltpu.HBM((len(entry),) + entry[0].shape, BF))
        else:
            outs.append(pltpu.HBM(entry.shape, BF) if entry.ndim == 4 else sds(entry.shape, BF))

    def kernel(at, *refs):
        sem = refs[-1]
        out = refs[-1 - len(outs) : -1]
        given = refs[count : count + len(flat)]
        started = []
        for n, (first, size) in enumerate(plan):
            target = out[n + (1 if count else 0)]
            for m in range(max(size, 1)):
                copy = pltpu.make_async_copy(
                    given[first + m], target.at[m] if size else target, sem.at[1 + first + m]
                )
                copy.start()
                started.append(copy)
        for n in range(count):

            @pl.when(at[0] == n)
            def _():
                pltpu.make_async_copy(refs[n], out[0], sem.at[0]).start()

        for copy in started:
            copy.wait()
        if count:
            pltpu.make_async_copy(refs[0], out[0], sem.at[0]).wait()

    return pl.pallas_call(
        kernel,
        out_shape=outs,
        in_specs=[SM] + [ANY] * (count + len(flat) + len(deps)),
        out_specs=[ANY] * len(outs),
        scratch_shapes=[pltpu.SemaphoreType.DMA((1 + len(flat),))],
        compiler_params=pltpu.CompilerParams(vmem_limit_bytes=2**20),
        cost_estimate=pl.CostEstimate(flops=1, bytes_accessed=1, transcendentals=0),
    )(index[None], *options, *flat, *deps)


def tie(x, deps):
    def kernel(*refs):
        pass

    return pl.pallas_call(
        kernel,
        out_shape=sds(x.shape, x.dtype),
        in_specs=[ANY] * (1 + len(deps)),
        out_specs=ANY,
        input_output_aliases={0: 0},
        compiler_params=pltpu.CompilerParams(vmem_limit_bytes=2**20),
        cost_estimate=pl.CostEstimate(flops=1, bytes_accessed=1, transcendentals=0),
    )(*in_hbm([x]), *deps)


def chosen(index, options):
    value = options[0]
    for i in range(1, len(options)):
        value = jnp.where(index == i, options[i], value)
    return value


EDGE = [(0, 1), (1, 0), (2, 3), (3, 2)]
INNER = [(0, 0), (1, 2), (2, 1), (3, 3)]


CROSS = [(0, 2), (1, 3), (2, 0), (3, 1)]
SKIP = [(0, 1), (1, 3), (2, 0), (3, 2)]
TURN = [(0, 2), (1, 0), (2, 3), (3, 1)]


def gather_weights(narrow):
    z = lax.axis_index("dp")
    e, o = along(narrow, EDGE), along(narrow, INNER)
    a0, b0 = near(narrow), far(narrow)
    t1, a0 = gate(z, [e, e, o, e], [a0], (b0,))
    eo, oe = along(o, EDGE), along(e, INNER)
    a1, b1, c0 = near(t1), far(t1), far(a0)
    t2, a1, four0 = gate(z, [eo, o, oe, eo], [a1, [narrow, a0, b0, c0]], (b1,))
    eoe, d0 = along(oe, EDGE), sibling(four0)
    a2, b2, c1 = near(t2), far(t2), far(a1)
    t3, a2, four1 = gate(z, [eoe, oe, e, eoe], [a2, [t1, a1, b1, c1]], (b2, d0))
    a3, b3, c2, d1 = near(t3), far(t3), far(a2), sibling(four1)
    a3, four2, trio = gate(z, [], [a3, [t2, a2, b2, c2], [t3, a3, b3]], (d1,))
    c3, d2, d3 = far(a3), sibling(four2), sibling(trio)
    last = sibling(c3)
    steps = chosen(z, [jnp.array(row, jnp.int32) for row in ((0, 1, 2, 3), (1, 0, 2, 3), (2, 1, 0, 3), (3, 2, 1, 0))])
    return [four0, d0, four1, d1, four2, d2, trio, c3, d3, last], steps


def summed(sources, deps=(), windows=(), scalars=None, split=False):
    shape, count = sources[0].shape, len(sources)

    def kernel(sc, *refs):
        outs = refs[count + len(deps) :]
        value = refs[0][...].astype(F32)
        for n in range(1, count):
            value = value + refs[n][...].astype(F32)
        value = value.astype(BF)
        if windows:
            outs[-1][...] = value
            for out, (start, size) in zip(outs, windows):
                out[...] = outs[-1][pl.ds(sc[start], size)]
        elif split:
            for n, out in enumerate(outs):
                out[...] = value[n]
        else:
            outs[0][...] = value

    shapes = [shape[1:]] * shape[0] if split else [(size,) + shape[1:] for _, size in windows] or [shape]
    results = call(
        kernel,
        [jnp.zeros((1,), jnp.int32) if scalars is None else scalars, *sources],
        [sds(one, BF) for one in shapes],
        [SM] + [VM] * count,
        scratch=[pltpu.VMEM(shape, BF)] if windows else [],
        limit=12, deps=deps,
    )
    return results if len(shapes) > 1 else results[0]


def pair_sum(keep, send, deps=()):
    def kernel(x, y, z, *rest):
        for n, ref in enumerate((y, z)):
            rest[-1][n] = (x[n].astype(F32) + ref[...].astype(F32)).astype(BF)

    got = [sibling(one) for one in send]
    return call(kernel, [*in_hbm([keep]), *got], [sds(keep.shape, BF)], [VM] * 3, limit=12, deps=deps)[0]


def plane_sum(x):
    for bit in (1, 2, 4):
        x = x + toward(x, lambda i, bit=bit: i ^ bit)
    return x


def local(
    tokens,
    cotangent,
    lengths,
    weights,
    vectors,
    moments,
    left_stats,
    right_stats,
    left_root,
    right_root,
    decays,
):
    dp, fsdp = lax.axis_size("dp"), lax.axis_size("fsdp")
    assert tokens.shape[0] == 1
    staged = (dp, fsdp) == (4, GROUPS)
    seq_total = tokens.shape[0] * dp * fsdp
    tok, cot = tokens[0], cotangent[0]
    narrow = weights.astype(BF)
    if staged:
        me = lax.axis_index("fsdp")
        core = lax.rem(me, 2)
        slots = slot_of(jnp.arange(GROUPS, dtype=jnp.int32) ^ me, core)
        pieces, steps = gather_weights(narrow)
    else:
        me = jnp.int32(0)
        core = jnp.int32(0)
        slots = slot_of(jnp.arange(GROUPS, dtype=jnp.int32), core)
        full = lax.all_gather(lax.all_gather(narrow, "dp", axis=0, tiled=True), "fsdp", axis=1, tiled=True)
        full = full.reshape(NBLK // PART, PART, GROUPS, TB // GROUPS, TB)
        place = [SLOT_TABLE.index(s) for s in range(GROUPS)]
        pieces = []
        for t in range(NBLK // PART):
            every = [full[t, :, place[s]] for s in range(GROUPS)]
            if t < 3:
                pieces += [jnp.stack(every[:HELD]), jnp.stack(every[HELD:])]
            else:
                pieces += [jnp.stack(every[:3]), every[3], jnp.stack(every[4:7]), every[7]]
        steps = jnp.arange(4, dtype=jnp.int32)
    scalars = jnp.concatenate([slots, steps, lengths, core[None], me[None]]).astype(jnp.int32)

    row16 = TB // GROUPS
    act = sds((NMAX, D), BF)
    wide = sds((NMAX, D), F32)
    summary = sds((K, D), BF)
    shape = (NMAX, D)
    square = (D, D)
    r_terms = sds((4, HID, row16, TB), BF)
    a_terms = sds((4, ATT, row16, TB), BF)
    held = [square, square, square, (NMAX, K), shape, shape, shape, (D, NMAX), shape, shape, (NMAX, FF)]
    (wq, wk, wv, cm, q, k, v, mixt, fl, out, gh, gr, gb, gm, *r_ship, ks, vs, lse, norms, sums_b) = call(
        layer,
        [scalars, tok, *in_hbm([cot]), vectors] + in_hbm(pieces),
        [pltpu.HBM(one, BF) for one in held]
        + [pltpu.HBM(shape, F32), pltpu.HBM(shape, BF), pltpu.HBM(shape, BF)]
        + shipped_shapes(HID)
        + [summary, summary, sds((H, NMAX), F32), sds((2, LANES), F32), sds((10, D), F32)],
        [SM, VM, ANY, VM] + [ANY] * ARRAYS,
        [ANY] * KEPT + [VM] * 5,
        scratch=[
            pltpu.VMEM((4, GROUPS, PART, row16, TB), BF),
            *[pltpu.VMEM(one, BF) for one in (shape, shape, shape, (D, NMAX), square, square, square, square, (NMAX, K), shape, shape, (NMAX, FF))],
            pltpu.VMEM((NMAX, FF), F32),
            pltpu.VMEM((NMAX, FF), BF),
            pltpu.VMEM(shape, BF),
            pltpu.VMEM(shape, F32),
            pltpu.VMEM(shape, F32),
            pltpu.VMEM((NMAX, LANES), F32),
            pltpu.VMEM(shape, BF),
            pltpu.VMEM(shape, BF),
            pltpu.VMEM(shape, F32),
            pltpu.VMEM(shape, BF),
            pltpu.VMEM(shape, BF),
            pltpu.VMEM(r_terms.shape, BF),
            pltpu.VMEM(r_terms.shape, BF),
            pltpu.SemaphoreType.DMA((4, GROUPS)),
            pltpu.SemaphoreType.DMA((KEPT - SHIPPED,)),
            pltpu.SemaphoreType.DMA(()),
            pltpu.SemaphoreType.DMA((FF // STEP, SHIPPED)),
        ],
        limit=60,
    )
    deps = ()
    if staged:
        z = lax.axis_index("dp")
        odd = z % 2
        cut_r = 3 * PART - (ATT + HID)
        cut_h = 2 * PART - ATT
        rest_a, rest_h = ATT - PART, HID - cut_h
        ranges = jnp.stack([odd * cut_r, (1 - odd) * cut_r, odd * rest_a, (1 - odd) * rest_a, (1 - odd) * cut_h, odd * cut_h])
        right, left = right_root.astype(BF), left_root.astype(BF)
        roots = jnp.stack([left, right])
        roots = [roots, near(roots), far(roots), toward(roots, lambda i: i ^ 6)]
        r_rest, r_keep, send_rest, *send = r_ship
        r_pair = pair_sum(r_keep, [tie(send[0], roots[1:]), send[1]])
        r_back = far(r_pair)
        r_came = sibling(send_rest)
        other_roots = [sibling(piece) for piece in roots]
        deps = (r_pair,)
    gq, gk, gv, sums_a, *a_ship = call(
        attention_backward,
        [scalars, *in_hbm([tok, q]), ks, vs, lse, *in_hbm([gm, k, v, gb, mixt, cm])],
        [act, act, act, sds((3, D), F32)] + shipped_shapes(ATT),
        [SM, ANY, ANY] + [VM] * 3 + [ANY] * 6,
        [VM] * 4 + [ANY] * SHIPPED,
        scratch=[
            *[pltpu.VMEM(one, BF) for one in ((K, D), (K, D), a_terms.shape, a_terms.shape, shape, shape, shape, (D, NMAX), (NMAX, K), shape, shape, shape)],
            pltpu.SemaphoreType.DMA((8,)),
            pltpu.SemaphoreType.DMA((5, SHIPPED)),
        ],
        limit=28, deps=deps,
    )
    local_vectors = jnp.concatenate([sums_a, sums_b], axis=0)
    local_norms = norms[:, 0]
    if staged:
        weight_sums = jnp.sum(weights * weights, axis=(1, 2))
        packed = jnp.concatenate([local_norms, weight_sums, jnp.zeros((D - 2 - PART,), F32)])
        packed = jnp.concatenate([local_vectors, packed[None]], axis=0)
        packed = packed + sibling(packed)
        r_own, r_first = summed([*in_hbm([r_rest]), r_came, r_back], other_roots, split=True)
        r_last = near(r_first)
        a_rest, a_keep, send_rest, *send = a_ship
        a_pair = pair_sum(a_keep, [tie(send[0], (r_first,)), send[1]], (packed,))
        a_back = far(a_pair)
        a_came = sibling(send_rest)
        r_stay, r_leave = summed([r_own, r_last], (), [(0, PART), (1, PART)], ranges)
        r_edge = along(r_leave, EDGE)
        deps = (a_pair,)
    in_grads, *h_ship = call(
        closing,
        [scalars, *in_hbm([fl, gh, gr]), gq, gk, gv, *in_hbm([wq, wk, wv])],
        [act] + shipped_shapes(HID),
        [SM, ANY, ANY, ANY] + [VM] * 3 + [ANY] * 3,
        [VM] + [ANY] * SHIPPED,
        scratch=[
            *[pltpu.VMEM(one, BF) for one in (r_terms.shape, r_terms.shape, shape, (NMAX, FF), square, square, square)],
            pltpu.VMEM(shape, F32),
            pltpu.SemaphoreType.DMA((6,)),
            pltpu.SemaphoreType.DMA((SHIPPED,)),
        ],
        limit=28, deps=deps,
    )
    if staged:
        packed = packed + toward(packed, lambda i: i ^ 2)
        a_own, a_first = summed([*in_hbm([a_rest]), a_came, a_back], (r_leave, packed), split=True)
        a_last = near(a_first)
        h_rest, h_keep, send_rest, *send = h_ship
        h_pair = pair_sum(h_keep, send)
        h_back = far(h_pair)
        h_came = sibling(send_rest)
        a_stay, a_leave = summed([a_own, a_last], (), [(2, PART), (3, PART)], ranges)
        a_edge = along(a_leave, EDGE)
        packed = packed + toward(packed, lambda i: i ^ 4)
        weight_squares = packed[-1, 2 : 2 + PART]
        h_own, h_first = summed([*in_hbm([h_rest]), h_came, h_back], (r_edge, a_leave, packed), split=True)
        h_last = near(h_first)
        r_half = summed([r_stay, r_edge], (h_first,))
        a_half = summed([a_stay, a_edge], (h_first,))
        upper = z >= 2
        wide_cross = along(jnp.where(upper, a_half, r_half), SKIP)
        slim_cross = along(jnp.where(upper, a_half[PART - rest_a :], r_half[:rest_a]), TURN)
        packed = packed + along(packed, EDGE)
        h_stay, h_leave = summed([h_own, h_last], (packed,), [(4, rest_h), (5, rest_h)], ranges)
        h_edge, h_inner, h_turn = along(h_leave, EDGE), along(h_leave, INNER), along(h_stay, TURN)
        packed = packed + along(packed, CROSS)
        grad_rows, low_rows = call(
            assemble,
            [jnp.stack([z, jnp.int32(seq_total)])]
            + [a_half, r_half, wide_cross, slim_cross, h_stay, h_edge, h_inner, h_turn],
            [pltpu.HBM(weights.shape, F32), sds(weights.shape, BF)],
            [SM] + [VM] * 8,
            limit=10, deps=(packed,),
        )
        vector_total, norm_totals = packed[:-1], packed[-1, :2]
        low_near, low_far = near(low_rows), far(low_rows)
        low = [low_rows, low_near, low_far, far(low_near)]
        rows = sds(weights.shape, F32)
        one = pl.BlockSpec((BATCH, row16, TB), lambda n: (n, 0, 0))
        halved = [pl.BlockSpec((None, BATCH, row16, TB), lambda n, at=at: (at, n, 0, 0)) for at in range(2)]
        new_weights, new_left, new_right = pl.pallas_call(
            step_kernel,
            grid=(PART // BATCH,),
            out_shape=[rows, rows, rows],
            in_specs=[SM, SM, SM] + [one] * (5 + GROUPS) + [halved[0]] * GROUPS + [halved[1]] * GROUPS,
            out_specs=[one, one, one],
            compiler_params=pltpu.CompilerParams(vmem_limit_bytes=24 * 1024 * 1024),
            cost_estimate=pl.CostEstimate(flops=1, bytes_accessed=1, transcendentals=0),
        )(
            scalars, decays.reshape(-1), jnp.sqrt(weight_squares / (TB * TB)),
            *in_hbm([
                grad_rows, left_root, left_stats, right_stats, weights,
                *low, *(sibling(piece) for piece in low),
                *roots, *other_roots, *roots, *other_roots,
            ]),
        )
    else:
        def join(ship):
            both = jnp.concatenate(ship[:3] + [ship[3][None], ship[4][None]], axis=0)
            return jnp.stack([both[s] for s in SLOT_TABLE], axis=1).reshape(-1, TB, TB)

        every = jnp.concatenate([join(a_ship), join(h_ship), join(r_ship)], axis=0)
        inner = lax.psum_scatter(every, "fsdp", scatter_dimension=1, tiled=True)
        total = lax.psum_scatter(inner, "dp", scatter_dimension=0, tiled=True).astype(F32)
        grad_rows = total / seq_total
        vector_total, norm_totals = lax.psum((local_vectors, local_norms), ("dp", "fsdp"))
        high = lax.Precision.HIGHEST
        whole = lax.all_gather(grad_rows.astype(BF), "fsdp", axis=1, tiled=True).astype(F32)
        count = grad_rows.shape[1]
        slab = lax.dynamic_slice_in_dim(whole, lax.axis_index("fsdp") * count, count, 2)
        gram_left = jnp.einsum("brc,bsc->brs", grad_rows, whole, precision=high)
        gram_right = jnp.einsum("bic,bis->bcs", slab, whole, precision=high)
        decay_left = decays[:, 0][:, None, None]
        decay_right = decays[:, 1][:, None, None]
        new_left = decay_left * left_stats + (1.0 - decay_left) * gram_left
        new_right = decay_right * right_stats + (1.0 - decay_right) * gram_right
        columns = jnp.einsum("bis,bcs->bic", whole, right_root, precision=high)
        applied = lax.all_gather(columns.astype(BF), "fsdp", axis=2, tiled=True).astype(F32)
        precond = jnp.einsum("brs,bsc->brc", left_root, applied, precision=high)
        precond_squares, weight_squares = lax.psum(
            (jnp.sum(precond * precond, axis=(1, 2)), jnp.sum(weights * weights, axis=(1, 2))), "fsdp"
        )
        tile_area = TB * TB
        weight_scale = jnp.sqrt(weight_squares / tile_area)
        precond_scale = lax.rsqrt(precond_squares / tile_area + EPS_STEP)
        new_weights = weights - STEP_RATE * (weight_scale * precond_scale)[:, None, None] * precond
    vector_grad = vector_total / seq_total
    summary_norms = norm_totals / seq_total
    new_moments = MOMENT_DECAY * moments + (1.0 - MOMENT_DECAY) * vector_grad
    row_scale = jnp.sqrt(jnp.mean(jnp.square(vectors), axis=1, keepdims=True))
    moment_scale = lax.rsqrt(jnp.mean(jnp.square(new_moments), axis=1, keepdims=True) + EPS_STEP)
    new_vectors = vectors - STEP_RATE * row_scale * new_moments * moment_scale
    return (
        out[None],
        in_grads[None],
        new_weights,
        grad_rows,
        new_left,
        new_right,
        new_vectors,
        new_moments,
        summary_norms,
    )


def solution(mesh):
    in_specs = (
        P(("dp", "fsdp"), None, None),
        P(("dp", "fsdp"), None, None),
        P(("dp", "fsdp")),
        P("dp", "fsdp", None),
        P(),
        P(),
        P("dp", "fsdp", None),
        P("dp", "fsdp", None),
        P("dp", "fsdp", None),
        P("dp", "fsdp", None),
        P("dp", None),
    )
    out_specs = (
        P(("dp", "fsdp"), None, None),
        P(("dp", "fsdp"), None, None),
        P("dp", "fsdp", None),
        P("dp", "fsdp", None),
        P("dp", "fsdp", None),
        P("dp", "fsdp", None),
        P(),
        P(),
        P(),
    )
    return jax.shard_map(local, mesh=mesh, in_specs=in_specs, out_specs=out_specs, check_vma=False)
```

```python
import functools

import jax
import jax.numpy as jnp
from jax import lax
from jax.experimental import pallas as pl
from jax.experimental.pallas import tpu as pltpu
from jax.sharding import PartitionSpec as P

D = 768
H = 12
HD = 64
FF = 3072
K = 256
NMAX = 512
TB = 128
LANES = 128
PART = 110
GROUPS = 8

EPS_NORM = 1e-05
EPS_STEP = 1e-06
STEP_RATE = 0.25
MOMENT_DECAY = 0.9
SQRT_HALF = 0.7071067811865476
INV_SQRT_TWO_PI = 0.3989422804014327
SCALE = HD ** (-0.5)

QUARTER = (D // TB) ** 2
ATT = 4 * QUARTER + NMAX // TB * (K // TB)
HID = D // TB * (FF // TB)
NBLK = ATT + 2 * HID
BF = jnp.bfloat16
F32 = jnp.float32

ANY = pl.BlockSpec(memory_space=pl.ANY)
VM = pl.BlockSpec(memory_space=pltpu.VMEM)
SM = pl.BlockSpec(memory_space=pltpu.SMEM)


def sds(shape, dtype):
    return jax.ShapeDtypeStruct(shape, dtype)


def nn(a, b):
    return lax.dot_general(a, b, (((1,), (0,)), ((), ())), preferred_element_type=F32)


def nt(a, b):
    return lax.dot_general(a, b, (((1,), (1,)), ((), ())), preferred_element_type=F32)


def tn(a, b):
    return lax.dot_general(a, b, (((0,), (0,)), ((), ())), preferred_element_type=F32)


def layer_norm(value):
    centre = jnp.mean(value, axis=-1, keepdims=True)
    shifted = value - centre
    spread = jnp.mean(shifted * shifted, axis=-1, keepdims=True)
    inverse = lax.rsqrt(spread + EPS_NORM)
    return shifted * inverse, inverse


def norm_backward(grad_out, normed, inverse, gain):
    scaled = grad_out * gain
    centred = scaled - jnp.mean(scaled, axis=-1, keepdims=True)
    return inverse * (centred - normed * jnp.mean(scaled * normed, axis=-1, keepdims=True))


def column_sum(value):
    return jnp.sum(value.astype(F32), axis=0, keepdims=True)


def valid_rows(length, width):
    return lax.broadcasted_iota(jnp.int32, (NMAX, width), 0) < length


HELD = GROUPS // 2
ARRAYS = 10


def piece_at(pieces, step, s):
    if step < 3:
        return pieces[2 * step + s // HELD].at[s % HELD]
    trio, last = pieces[6 + 2 * (s // HELD)], pieces[7 + 2 * (s // HELD)]
    return last if s % HELD == HELD - 1 else trio.at[s % HELD]


def fetch(sc, pieces, raw, sem):
    for part in range(4):
        for step in range(4):

            @pl.when(sc[8 + part] == step)
            def _():
                for s in range(GROUPS):
                    pltpu.make_async_copy(piece_at(pieces, step, s), raw.at[part, s], sem.at[part, s]).start()


def fetched(pieces, raw, sem, part):
    for s in range(GROUPS):
        pltpu.make_async_copy(piece_at(pieces, 0, s), raw.at[part, s], sem.at[part, s]).wait()


def lay_out(slots, raw, at, first, count, dst, dst_first, per_row):
    for n in range(count):
        i, j = divmod(n + dst_first, per_row)
        for r in range(GROUPS):
            dst[i * TB + 16 * r : i * TB + 16 * r + 16, j * TB : (j + 1) * TB] = raw[at, slots[r], first + n]


def splitter(sc):
    even = sc[13] == 0
    mine = [jnp.where(even, sc[2 * m], sc[2 * m + 1]) for m in range(4)]
    other = [jnp.where(even, sc[2 * m + 1], sc[2 * m]) - 4 for m in range(4)]

    def put(keep, send, b, value):
        low = value.astype(BF)
        for m in range(4):
            first = low[32 * m : 32 * m + 16]
            second = low[32 * m + 16 : 32 * m + 32]
            keep[mine[m], b] = jnp.where(even, first, second)
            send[other[m], b] = jnp.where(even, second, first)

    return put


SHIPPED = 5


def shipped(keep, send, outs, span, sem):
    cuts = [(keep, pl.ds(0, 2)), (keep, pl.ds(2, 2)), (send, pl.ds(0, 2)), (send, 2), (send, 3)]
    return [
        pltpu.make_async_copy(source.at[at, span], out.at[span] if isinstance(at, int) else out.at[:, span], sem.at[n])
        for n, ((source, at), out) in enumerate(zip(cuts, outs))
    ]


def shipped_shapes(count):
    one = (count, TB // GROUPS, TB)
    return [pltpu.HBM((2,) + one, BF)] * 3 + [pltpu.HBM(one, BF)] * 2


STEP = 256


def tiles(raw, slots, block):
    part, b = divmod(block, PART)
    return [raw[part, slots[r], b] for r in range(GROUPS)]


def hidden_columns(raw, slots, g):
    count = STEP // TB
    rows = []
    for i in range(D // TB):
        blocks = [tiles(raw, slots, ATT + i * (FF // TB) + g * count + c) for c in range(count)]
        rows += [jnp.concatenate([block[r] for block in blocks], axis=1) for r in range(GROUPS)]
    return jnp.concatenate(rows, axis=0)


def return_rows(raw, slots, g):
    count = STEP // TB
    rows = []
    for i in range(count):
        blocks = [tiles(raw, slots, ATT + HID + (g * count + i) * (D // TB) + j) for j in range(D // TB)]
        rows += [jnp.concatenate([block[r] for block in blocks], axis=1) for r in range(GROUPS)]
    return jnp.concatenate(rows, axis=0)


KEPT = 19


def layer(sc, tok, cot, vec, *rest):
    pieces, rest = rest[:ARRAYS], rest[ARRAYS:]
    stored, rest = rest[:KEPT], rest[KEPT:]
    ks_o, vs_o, lse_o, norm_o, sums_o = rest[:5]
    (raw, q_o, k_o, v_o, mixt_o, wq_o, wk_o, wv_o, wo_o, cm_o, mix_o, fl_o, gh_o, slope, act, gsl, acc, nf, ni,
     cot_v, out_o, gr_o, gb_o, gm_o, keep_o, send_o, sem, osem, csem, tsem) = rest[5:]
    fetch(sc, pieces, raw, sem)
    cot_copy = pltpu.make_async_copy(cot, cot_v, csem)
    cot_copy.start()
    slots = [sc[r] for r in range(GROUPS)]
    put = splitter(sc)
    nb = nd = D // TB
    copies = []

    def store(*refs):
        for ref in refs:
            copy = pltpu.make_async_copy(ref, stored[len(copies)], osem.at[len(copies)])
            copy.start()
            copies.append(copy)

    fetched(pieces, raw, sem, 0)
    for m, dst in enumerate((wq_o, wk_o, wv_o)):
        lay_out(slots, raw, 0, m * QUARTER, QUARTER, dst, 0, nb)
    head = PART - 3 * QUARTER
    lay_out(slots, raw, 0, 3 * QUARTER, head, wo_o, 0, nb)
    x = tok[...]
    q_o[...] = (nn(x, wq_o[...]) + vec[0:1]).astype(BF)
    k_o[...] = (nn(x, wk_o[...]) + vec[1:2]).astype(BF)
    v_o[...] = (nn(x, wv_o[...]) + vec[2:3]).astype(BF)
    fetched(pieces, raw, sem, 1)
    lay_out(slots, raw, 1, 0, QUARTER - head, wo_o, head, nb)
    lay_out(slots, raw, 1, QUARTER - head, ATT - 4 * QUARTER, cm_o, 0, K // TB)
    store(wq_o, wk_o, wv_o, cm_o, q_o, k_o, v_o)
    masked = jnp.where(valid_rows(sc[12], K), cm_o[...], jnp.zeros((), BF))
    ks_o[...] = tn(masked, k_o[...]).astype(BF)
    vs_o[...] = tn(masked, v_o[...]).astype(BF)
    for n, ref in enumerate((ks_o, vs_o)):
        square = jnp.square(ref[...].astype(F32))
        total = jnp.sum(jnp.sum(square, axis=0, keepdims=True), axis=1, keepdims=True)
        norm_o[n : n + 1, :] = jnp.broadcast_to(jnp.sqrt(total), (1, LANES))
    lane = lax.broadcasted_iota(jnp.int32, (K, LANES), 1) < HD
    for p in range(H // 2):
        cols = slice(p * LANES, (p + 1) * LANES)
        q_p, ks_p, vs_p = q_o[:, cols], ks_o[:, cols], vs_o[:, cols]
        zero = jnp.zeros((), BF)
        parts, values = [], []
        for half in range(2):
            sel = lane if half == 0 else jnp.logical_not(lane)
            scores = nt(jnp.where(sel, ks_p, zero), q_p) * SCALE
            peak = jnp.max(scores, axis=0, keepdims=True)
            raised = jnp.exp(scores - peak)
            total = jnp.sum(raised, axis=0, keepdims=True)
            lse_o[2 * p + half : 2 * p + half + 1, :] = peak + jnp.log(total)
            parts.append((raised * (1.0 / total)).astype(BF))
            values.append(jnp.where(sel, vs_p, zero))
        mixt = tn(jnp.concatenate(values, axis=0), jnp.concatenate(parts, axis=0)).astype(BF)
        mixt_o[cols, :] = mixt
        mix_o[:, cols] = mixt.T
    store(mixt_o)
    branch = nn(mix_o[...], wo_o[...]) + vec[3:4]
    normed, inverse = layer_norm(x.astype(F32) + branch)
    nf[...] = normed
    ni[...] = jnp.broadcast_to(inverse, (NMAX, LANES))
    first = normed * vec[4:5] + vec[5:6]
    fl_o[...] = first.astype(BF)
    store(fl_o)
    acc[...] = first + vec[10:11]
    for at in (2, 3):
        fetched(pieces, raw, sem, at)
    for g in range(FF // STEP):
        cols = slice(g * STEP, (g + 1) * STEP)
        row, off = 6 + (g * STEP) // D, (g * STEP) % D
        hidden = nn(fl_o[...], hidden_columns(raw, slots, g)) + vec[row : row + 1, off : off + STEP]
        phi = 0.5 * (1.0 + lax.erf(hidden * SQRT_HALF))
        low = (hidden * phi).astype(BF)
        act[:, cols] = low
        slope[:, cols] = phi + hidden * INV_SQRT_TWO_PI * jnp.exp(-0.5 * hidden * hidden)
        acc[...] += nn(low, return_rows(raw, slots, g))
    valid = valid_rows(sc[12], D)
    normed2, inverse2 = layer_norm(acc[...])
    result = normed2 * vec[11:12] + vec[12:13]
    out_o[...] = jnp.where(valid, result, 0.0).astype(BF)
    store(out_o)
    cot_copy.wait()
    grad_result = jnp.where(valid, cot_v[...].astype(F32), 0.0)
    sums_o[8:9, :] = column_sum(grad_result * normed2)
    sums_o[9:10, :] = column_sum(grad_result)
    grad_second = norm_backward(grad_result, normed2, inverse2, vec[11:12])
    acc[...] = grad_second
    gsl[...] = grad_second.astype(BF)
    sums_o[7:8, :] = column_sum(gsl[...])
    for g in range(FF // STEP):
        cols = slice(g * STEP, (g + 1) * STEP)
        gh = (nt(gsl[...], return_rows(raw, slots, g)) * slope[:, cols]).astype(BF)
        gh_o[:, cols] = gh
        row, off = (g * STEP) // D, (g * STEP) % D
        sums_o[3 + row : 4 + row, off : off + STEP] = column_sum(gh)
        acc[...] += nt(gh, hidden_columns(raw, slots, g))
        terms = tn(act[:, cols], gsl[...])
        for i in range(STEP // TB):
            for j in range(nd):
                put(keep_o, send_o, (g * (STEP // TB) + i) * nd + j, terms[i * TB : (i + 1) * TB, j * TB : (j + 1) * TB])
        span = pl.ds(g * (STEP // TB) * nd, (STEP // TB) * nd)
        for copy in shipped(keep_o, send_o, stored[-SHIPPED:], span, tsem.at[g]):
            copy.start()
    store(gh_o)
    grad_first = acc[...]
    normed, inverse = nf[...], ni[:, 0:1]
    sums_o[1:2, :] = column_sum(grad_first * normed)
    sums_o[2:3, :] = column_sum(grad_first)
    grad_resid = norm_backward(grad_first, normed, inverse, vec[4:5])
    gr_o[...] = grad_resid
    low = grad_resid.astype(BF)
    gb_o[...] = low
    sums_o[0:1, :] = column_sum(low)
    store(gr_o, gb_o)
    gm_o[...] = nt(low, wo_o[...]).astype(BF)
    store(gm_o)
    for copy in copies:
        copy.wait()
    for g in range(FF // STEP):
        span = pl.ds(g * (STEP // TB) * nd, (STEP // TB) * nd)
        for copy in shipped(keep_o, send_o, stored[-SHIPPED:], span, tsem.at[g]):
            copy.wait()


def attention_backward(sc, tok, q, ks, vs, lse, gm, k, v, gb, mixt, cm, *rest):
    gq_o, gk_o, gv_o, sums_o, *outs = rest[-23:-14]
    gks_o, gvs_o, keep_o, send_o, *held, sem, tsem = rest[-14:]
    ships = []

    def ship(n, first, count):
        for copy in shipped(keep_o, send_o, outs, pl.ds(first, count), tsem.at[n]):
            copy.start()
            ships.append(copy)

    copies = [
        pltpu.make_async_copy(source, target, sem.at[n])
        for n, (source, target) in enumerate(zip((q, gm, tok, mixt, cm, k, v, gb), held))
    ]
    for copy in copies:
        copy.start()
    q, gm, tok, mixt, cm, k, v, gb = held
    for copy in copies[:2]:
        copy.wait()
    lane = lax.broadcasted_iota(jnp.int32, (K, LANES), 1) < HD
    zero = jnp.zeros((), BF)
    for p in range(H // 2):
        cols = slice(p * LANES, (p + 1) * LANES)
        q_p, ks_p, vs_p, gm_p = q[:, cols], ks[:, cols], vs[:, cols], gm[:, cols]
        keys, grads, gvs, gks = [], [], [], []
        for half in range(2):
            sel = lane if half == 0 else jnp.logical_not(lane)
            key = jnp.where(sel, ks_p, zero)
            attend = jnp.exp(nt(key, q_p) * SCALE - lse[2 * p + half : 2 * p + half + 1, :])
            grad_attend = nt(jnp.where(sel, vs_p, zero), gm_p)
            mean = jnp.sum(grad_attend * attend, axis=0, keepdims=True)
            grad_scores = (attend * (grad_attend - mean)).astype(BF)
            gvs.append(nn(attend.astype(BF), gm_p))
            gks.append(nn(grad_scores, q_p))
            keys.append(key)
            grads.append(grad_scores)
        gvs_o[:, cols] = jnp.where(lane, gvs[0], gvs[1]).astype(BF)
        gks_o[:, cols] = (jnp.where(lane, gks[0], gks[1]) * SCALE).astype(BF)
        gqt = tn(jnp.concatenate(keys, axis=0), jnp.concatenate(grads, axis=0)) * SCALE
        gq_o[:, cols] = gqt.astype(BF).T
    put = splitter(sc)
    nd, nk = D // TB, K // TB
    for copy in copies[2:]:
        copy.wait()
    masked = jnp.where(valid_rows(sc[12], K), cm[...], zero)
    gk_o[...] = nn(masked, gks_o[...]).astype(BF)
    gv_o[...] = nn(masked, gvs_o[...]).astype(BF)
    tokt = tok[...].T
    lhs = (tokt, tokt, tokt, mixt[...])
    for m, grad in enumerate((gq_o, gk_o, gv_o, gb)):
        if m < 3:
            sums_o[m : m + 1, :] = column_sum(grad[...])
        terms = nn(lhs[m], grad[...])
        for i in range(nd):
            for j in range(nd):
                put(keep_o, send_o, m * QUARTER + i * nd + j, terms[i * TB : (i + 1) * TB, j * TB : (j + 1) * TB])
        ship(m, m * QUARTER, QUARTER)
    comp = nt(k[...], gks_o[...]) + nt(v[...], gvs_o[...])
    comp = jnp.where(valid_rows(sc[12], K), comp, 0.0)
    for i in range(NMAX // TB):
        for j in range(nk):
            put(keep_o, send_o, 4 * QUARTER + i * nk + j, comp[i * TB : (i + 1) * TB, j * TB : (j + 1) * TB])
    ship(4, 4 * QUARTER, ATT - 4 * QUARTER)
    for copy in ships:
        copy.wait()


def closing(sc, fl, gh, gr, gq, gk, gv, wq, wk, wv, *rest):
    in_o, *outs = rest[-16:-10]
    keep_o, send_o, *held, gr_v, sem, tsem = rest[-10:]
    copies = [
        pltpu.make_async_copy(source, target, sem.at[n])
        for n, (source, target) in enumerate(zip((fl, gh, wq, wk, wv, gr), (*held, gr_v)))
    ]
    for copy in copies:
        copy.start()
    fl, gh, wq, wk, wv = held
    put = splitter(sc)
    for copy in copies[:2]:
        copy.wait()
    nh, nd = FF // TB, D // TB
    flt = fl[...].T
    for g in range(FF // STEP):
        terms = nn(flt, gh[:, g * STEP : (g + 1) * STEP])
        for i in range(nd):
            for j in range(STEP // TB):
                put(keep_o, send_o, i * nh + g * (STEP // TB) + j, terms[i * TB : (i + 1) * TB, j * TB : (j + 1) * TB])
    ships = shipped(keep_o, send_o, outs, pl.ds(0, HID), tsem)
    for copy in ships:
        copy.start()
    for copy in copies[2:]:
        copy.wait()
    total = gr_v[...] + nt(gq[...], wq[...])
    total = total + nt(gk[...], wk[...])
    total = total + nt(gv[...], wv[...])
    in_o[...] = total.astype(BF)
    for copy in ships:
        copy.wait()


def assemble(at, wide_a, wide_r, wide_x, slim_x, h_stay, h_x, h_y, h_z, *rest):
    rows_o, low_o, scale = rest[-2], rest[-1], at[1].astype(F32)
    upper = at[0] >= 2
    size, slim, late = wide_a.shape[0], slim_x.shape[0], h_stay.shape[0]

    def emit(first, count, value):
        value = value * (1.0 / scale)
        rows_o[first : first + count] = value
        low_o[first : first + count] = value.astype(BF)

    def hidden(count):
        value = h_stay[:count].astype(F32)
        for ref in (h_x, h_y, h_z):
            value = value + ref[:count].astype(F32)
        return value

    @pl.when(at[0] % 3 == 0)
    def _():
        emit(0, size, jnp.where(upper, wide_r[...], wide_a[...]).astype(F32) + wide_x[...].astype(F32))

    @pl.when(at[0] == 1)
    def _():
        emit(0, slim, wide_a[size - slim :].astype(F32) + slim_x[...].astype(F32))
        emit(slim, size - slim, hidden(size - slim))

    @pl.when(at[0] == 2)
    def _():
        emit(0, late, hidden(late))
        emit(late, size - late, wide_r[: size - late].astype(F32) + slim_x[: size - late].astype(F32))


BATCH = 22


def halves(value):
    high = value.astype(BF)
    return high, (value - high.astype(F32)).astype(BF)


def step_kernel(sc, dec, size, own, lroot, lstat, rstat, weight, *rest):
    here, there, lefts, rights = (rest[n * HELD : (n + 1) * HELD] for n in (0, 1, 2, 4))
    other_lefts, other_rights = rest[3 * HELD : 4 * HELD], rest[5 * HELD : 6 * HELD]
    nw_o, nl_o, nr_o = rest[6 * HELD :]
    slots = [sc[r] for r in range(GROUPS)]
    even = sc[13] == 0
    mine = [jnp.where(even, slots[2 * m], slots[2 * m + 1]) for m in range(4)]
    other = [jnp.where(even, slots[2 * m + 1], slots[2 * m]) - HELD for m in range(4)]
    pick_row = lax.broadcasted_iota(jnp.int32, (16, TB), 0) + sc[14] * 16
    select = (lax.broadcasted_iota(jnp.int32, (16, TB), 1) == pick_row).astype(BF)
    start = pl.program_id(0) * BATCH

    def ordered(pairs):
        rows = []
        for a, b in pairs:
            rows += [jnp.where(even, a, b), jnp.where(even, b, a)]
        return jnp.concatenate(rows, axis=0)

    def tile(refs, slot, n):
        value = refs[0][n]
        for at in range(1, HELD):
            value = jnp.where(slot == at, refs[at][n], value)
        return value

    def whole(here, there, n):
        return ordered([(tile(here, mine[m], n), tile(there, other[m], n)) for m in range(4)])

    bs = range(BATCH)
    grads = [whole(here, there, n) for n in bs]
    across = [nt(jnp.concatenate([own[n].astype(BF), select], axis=0), g) for n, g in zip(bs, grads)]
    left = [jnp.concatenate([whole(lefts, other_lefts, n), *halves(lroot[n])], axis=0) for n in bs]
    down = [nn(jnp.concatenate([f, a[16:].astype(BF)], axis=0), g) for f, a, g in zip(left, across, grads)]
    mids = [
        jnp.concatenate([d[:TB].astype(BF), *halves(d[TB : TB + 16] + d[TB + 16 : TB + 32])], axis=0) for d in down
    ]
    last = [nn(m, whole(rights, other_rights, n)) for n, m in zip(bs, mids)]
    for n, a, d, p in zip(bs, across, down, last):
        decay = dec[2 * (start + n)]
        nl_o[n] = decay * lstat[n] + (1.0 - decay) * a[:16]
        decay = dec[2 * (start + n) + 1]
        nr_o[n] = decay * rstat[n] + (1.0 - decay) * d[TB + 32 :]
        full = p[:TB]
        squares = jnp.sum(jnp.sum(full * full, axis=0, keepdims=True), axis=1, keepdims=True)
        scale = size[start + n] * lax.rsqrt(squares * (1.0 / (TB * TB)) + EPS_STEP)
        nw_o[n] = weight[n] - STEP_RATE * scale * (p[TB : TB + 16] + p[TB + 16 :])


def in_hbm(arrays):
    return [pltpu.with_memory_space_constraint(a, pltpu.HBM) for a in arrays]


def call(kernel, ins, outs, in_specs, out_specs=None, scratch=(), limit=60, deps=()):
    return pl.pallas_call(
        kernel,
        out_shape=outs,
        in_specs=in_specs + [ANY] * len(deps),
        out_specs=out_specs or [VM] * len(outs),
        scratch_shapes=list(scratch),
        compiler_params=pltpu.CompilerParams(vmem_limit_bytes=limit * 1024 * 1024),
        cost_estimate=pl.CostEstimate(flops=1, bytes_accessed=1, transcendentals=0),
    )(*ins, *deps)


SLOT_TABLE = (0, 4, 1, 6, 2, 5, 3, 7)


def slot_of(code, core):
    other, x, y = code & 1, (code >> 1) & 1, code >> 2
    return 4 * other + jnp.where((other ^ core) == 0, x + 2 * y, y + 2 * x)


def toward(x, move):
    return lax.ppermute(x, "fsdp", [(i, move(i)) for i in range(GROUPS)])


def near(x):
    return toward(x, lambda i: i ^ 2 if i % 2 == 0 else i ^ 4)


def far(x):
    return toward(x, lambda i: i ^ 4 if i % 2 == 0 else i ^ 2)


def sibling(x):
    return toward(x, lambda i: i ^ 1)


def along(x, pairs):
    return lax.ppermute(x, "dp", pairs)


def gate(index, options, copies, deps=()):
    flat, plan = [], []
    for entry in copies:
        group = entry if isinstance(entry, list) else [entry]
        plan.append((len(flat), len(group) if isinstance(entry, list) else 0))
        flat += group
    count = len(options)
    outs = [sds(options[0].shape, options[0].dtype)] if count else []
    for entry in copies:
        if isinstance(entry, list):
            outs.append(pltpu.HBM((len(entry),) + entry[0].shape, BF))
        else:
            outs.append(pltpu.HBM(entry.shape, BF) if entry.ndim == 4 else sds(entry.shape, BF))

    def kernel(at, *refs):
        sem = refs[-1]
        out = refs[-1 - len(outs) : -1]
        given = refs[count : count + len(flat)]
        started = []
        for n, (first, size) in enumerate(plan):
            target = out[n + (1 if count else 0)]
            for m in range(max(size, 1)):
                copy = pltpu.make_async_copy(
                    given[first + m], target.at[m] if size else target, sem.at[1 + first + m]
                )
                copy.start()
                started.append(copy)
        for n in range(count):

            @pl.when(at[0] == n)
            def _():
                pltpu.make_async_copy(refs[n], out[0], sem.at[0]).start()

        for copy in started:
            copy.wait()
        if count:
            pltpu.make_async_copy(refs[0], out[0], sem.at[0]).wait()

    return pl.pallas_call(
        kernel,
        out_shape=outs,
        in_specs=[SM] + [ANY] * (count + len(flat) + len(deps)),
        out_specs=[ANY] * len(outs),
        scratch_shapes=[pltpu.SemaphoreType.DMA((1 + len(flat),))],
        compiler_params=pltpu.CompilerParams(vmem_limit_bytes=2**20),
        cost_estimate=pl.CostEstimate(flops=1, bytes_accessed=1, transcendentals=0),
    )(index[None], *options, *flat, *deps)


def tie(x, deps):
    def kernel(*refs):
        pass

    return pl.pallas_call(
        kernel,
        out_shape=sds(x.shape, x.dtype),
        in_specs=[ANY] * (1 + len(deps)),
        out_specs=ANY,
        input_output_aliases={0: 0},
        compiler_params=pltpu.CompilerParams(vmem_limit_bytes=2**20),
        cost_estimate=pl.CostEstimate(flops=1, bytes_accessed=1, transcendentals=0),
    )(*in_hbm([x]), *deps)


def chosen(index, options):
    value = options[0]
    for i in range(1, len(options)):
        value = jnp.where(index == i, options[i], value)
    return value


EDGE = [(0, 1), (1, 0), (2, 3), (3, 2)]
INNER = [(0, 0), (1, 2), (2, 1), (3, 3)]


CROSS = [(0, 2), (1, 3), (2, 0), (3, 1)]
SKIP = [(0, 1), (1, 3), (2, 0), (3, 2)]
TURN = [(0, 2), (1, 0), (2, 3), (3, 1)]


def gather_weights(narrow, early):
    z = lax.axis_index("dp")
    e, o = along(narrow, EDGE), along(narrow, INNER)
    a0, b0 = near(narrow), far(narrow)
    t1, a0 = gate(z, [e, e, o, e], [a0], (b0,))
    eo, oe = along(o, EDGE), along(e, INNER)
    a1, b1, c0 = near(t1), far(t1), far(a0)
    t2, a1, four0 = gate(z, [eo, o, oe, eo], [a1, [narrow, a0, b0, c0]], (b1,))
    eoe, d0 = along(oe, EDGE), sibling(four0)
    a2, b2, c1 = near(t2), far(t2), far(a1)
    t3, a2, four1 = gate(z, [eoe, oe, e, eoe], [a2, [t1, a1, b1, c1]], (b2, d0))
    a3, b3, c2, d1 = near(t3), far(t3), far(a2), sibling(four1)
    a3, four2, trio = gate(z, [], [a3, [t2, a2, b2, c2], [t3, a3, b3]], (d1, early))
    c3, d2, d3 = far(a3), sibling(four2), sibling(trio)
    last = sibling(c3)
    steps = chosen(z, [jnp.array(row, jnp.int32) for row in ((0, 1, 2, 3), (1, 0, 2, 3), (2, 1, 0, 3), (3, 2, 1, 0))])
    return [four0, d0, four1, d1, four2, d2, trio, c3, d3, last], steps


def summed(sources, deps=(), windows=(), scalars=None, split=False):
    shape, count = sources[0].shape, len(sources)

    def kernel(sc, *refs):
        outs = refs[count + len(deps) :]
        value = refs[0][...].astype(F32)
        for n in range(1, count):
            value = value + refs[n][...].astype(F32)
        value = value.astype(BF)
        if windows:
            outs[-1][...] = value
            for out, (start, size) in zip(outs, windows):
                out[...] = outs[-1][pl.ds(sc[start], size)]
        elif split:
            for n, out in enumerate(outs):
                out[...] = value[n]
        else:
            outs[0][...] = value

    shapes = [shape[1:]] * shape[0] if split else [(size,) + shape[1:] for _, size in windows] or [shape]
    results = call(
        kernel,
        [jnp.zeros((1,), jnp.int32) if scalars is None else scalars, *sources],
        [sds(one, BF) for one in shapes],
        [SM] + [VM] * count,
        scratch=[pltpu.VMEM(shape, BF)] if windows else [],
        limit=12, deps=deps,
    )
    return results if len(shapes) > 1 else results[0]


def pair_sum(keep, send, deps=()):
    def kernel(x, y, z, *rest):
        for n, ref in enumerate((y, z)):
            rest[-1][n] = (x[n].astype(F32) + ref[...].astype(F32)).astype(BF)

    got = [sibling(one) for one in send]
    return call(kernel, [*in_hbm([keep]), *got], [sds(keep.shape, BF)], [VM] * 3, limit=12, deps=deps)[0]


def plane_sum(x):
    for bit in (1, 2, 4):
        x = x + toward(x, lambda i, bit=bit: i ^ bit)
    return x


def local(
    tokens,
    cotangent,
    lengths,
    weights,
    vectors,
    moments,
    left_stats,
    right_stats,
    left_root,
    right_root,
    decays,
):
    dp, fsdp = lax.axis_size("dp"), lax.axis_size("fsdp")
    assert tokens.shape[0] == 1
    staged = (dp, fsdp) == (4, GROUPS)
    seq_total = tokens.shape[0] * dp * fsdp
    tok, cot = tokens[0], cotangent[0]
    narrow = weights.astype(BF)
    if staged:
        me = lax.axis_index("fsdp")
        core = lax.rem(me, 2)
        slots = slot_of(jnp.arange(GROUPS, dtype=jnp.int32) ^ me, core)
        roots = jnp.stack([left_root.astype(BF), right_root.astype(BF)])
        pieces, steps = gather_weights(narrow, roots)
    else:
        me = jnp.int32(0)
        core = jnp.int32(0)
        slots = slot_of(jnp.arange(GROUPS, dtype=jnp.int32), core)
        full = lax.all_gather(lax.all_gather(narrow, "dp", axis=0, tiled=True), "fsdp", axis=1, tiled=True)
        full = full.reshape(NBLK // PART, PART, GROUPS, TB // GROUPS, TB)
        place = [SLOT_TABLE.index(s) for s in range(GROUPS)]
        pieces = []
        for t in range(NBLK // PART):
            every = [full[t, :, place[s]] for s in range(GROUPS)]
            if t < 3:
                pieces += [jnp.stack(every[:HELD]), jnp.stack(every[HELD:])]
            else:
                pieces += [jnp.stack(every[:3]), every[3], jnp.stack(every[4:7]), every[7]]
        steps = jnp.arange(4, dtype=jnp.int32)
    scalars = jnp.concatenate([slots, steps, lengths, core[None], me[None]]).astype(jnp.int32)

    row16 = TB // GROUPS
    act = sds((NMAX, D), BF)
    wide = sds((NMAX, D), F32)
    summary = sds((K, D), BF)
    shape = (NMAX, D)
    square = (D, D)
    r_terms = sds((4, HID, row16, TB), BF)
    a_terms = sds((4, ATT, row16, TB), BF)
    held = [square, square, square, (NMAX, K), shape, shape, shape, (D, NMAX), shape, shape, (NMAX, FF)]
    (wq, wk, wv, cm, q, k, v, mixt, fl, out, gh, gr, gb, gm, *r_ship, ks, vs, lse, norms, sums_b) = call(
        layer,
        [scalars, tok, *in_hbm([cot]), vectors] + in_hbm(pieces),
        [pltpu.HBM(one, BF) for one in held]
        + [pltpu.HBM(shape, F32), pltpu.HBM(shape, BF), pltpu.HBM(shape, BF)]
        + shipped_shapes(HID)
        + [summary, summary, sds((H, NMAX), F32), sds((2, LANES), F32), sds((10, D), F32)],
        [SM, VM, ANY, VM] + [ANY] * ARRAYS,
        [ANY] * KEPT + [VM] * 5,
        scratch=[
            pltpu.VMEM((4, GROUPS, PART, row16, TB), BF),
            *[pltpu.VMEM(one, BF) for one in (shape, shape, shape, (D, NMAX), square, square, square, square, (NMAX, K), shape, shape, (NMAX, FF))],
            pltpu.VMEM((NMAX, FF), F32),
            pltpu.VMEM((NMAX, FF), BF),
            pltpu.VMEM(shape, BF),
            pltpu.VMEM(shape, F32),
            pltpu.VMEM(shape, F32),
            pltpu.VMEM((NMAX, LANES), F32),
            pltpu.VMEM(shape, BF),
            pltpu.VMEM(shape, BF),
            pltpu.VMEM(shape, F32),
            pltpu.VMEM(shape, BF),
            pltpu.VMEM(shape, BF),
            pltpu.VMEM(r_terms.shape, BF),
            pltpu.VMEM(r_terms.shape, BF),
            pltpu.SemaphoreType.DMA((4, GROUPS)),
            pltpu.SemaphoreType.DMA((KEPT - SHIPPED,)),
            pltpu.SemaphoreType.DMA(()),
            pltpu.SemaphoreType.DMA((FF // STEP, SHIPPED)),
        ],
        limit=60,
    )
    deps = ()
    if staged:
        z = lax.axis_index("dp")
        odd = z % 2
        cut_r = 3 * PART - (ATT + HID)
        cut_h = 2 * PART - ATT
        rest_a, rest_h = ATT - PART, HID - cut_h
        ranges = jnp.stack([odd * cut_r, (1 - odd) * cut_r, odd * rest_a, (1 - odd) * rest_a, (1 - odd) * cut_h, odd * cut_h])
        roots = [roots, near(roots), far(roots), toward(roots, lambda i: i ^ 6)]
        r_rest, r_keep, send_rest, *send = r_ship
        r_pair = pair_sum(r_keep, [tie(send[0], roots[1:]), send[1]])
        r_back = far(r_pair)
        r_came = sibling(send_rest)
        other_roots = [sibling(piece) for piece in roots]
        deps = (r_pair,)
    gq, gk, gv, sums_a, *a_ship = call(
        attention_backward,
        [scalars, *in_hbm([tok, q]), ks, vs, lse, *in_hbm([gm, k, v, gb, mixt, cm])],
        [act, act, act, sds((3, D), F32)] + shipped_shapes(ATT),
        [SM, ANY, ANY] + [VM] * 3 + [ANY] * 6,
        [VM] * 4 + [ANY] * SHIPPED,
        scratch=[
            *[pltpu.VMEM(one, BF) for one in ((K, D), (K, D), a_terms.shape, a_terms.shape, shape, shape, shape, (D, NMAX), (NMAX, K), shape, shape, shape)],
            pltpu.SemaphoreType.DMA((8,)),
            pltpu.SemaphoreType.DMA((5, SHIPPED)),
        ],
        limit=28, deps=deps,
    )
    local_vectors = jnp.concatenate([sums_a, sums_b], axis=0)
    local_norms = norms[:, 0]
    if staged:
        weight_sums = jnp.sum(jnp.square(lax.optimization_barrier(weights)), axis=(1, 2))
        packed = jnp.concatenate([local_norms, weight_sums, jnp.zeros((D - 2 - PART,), F32)])
        packed = jnp.concatenate([local_vectors, packed[None]], axis=0)
        packed = packed + sibling(packed)
        r_own, r_first = summed([*in_hbm([r_rest]), r_came, r_back], other_roots, split=True)
        r_last = near(r_first)
        a_rest, a_keep, send_rest, *send = a_ship
        a_pair = pair_sum(a_keep, [tie(send[0], (r_first,)), send[1]], (packed,))
        a_back = far(a_pair)
        a_came = sibling(send_rest)
        r_stay, r_leave = summed([r_own, r_last], (), [(0, PART), (1, PART)], ranges)
        r_edge = along(r_leave, EDGE)
        deps = (a_pair,)
    in_grads, *h_ship = call(
        closing,
        [scalars, *in_hbm([fl, gh, gr]), gq, gk, gv, *in_hbm([wq, wk, wv])],
        [act] + shipped_shapes(HID),
        [SM, ANY, ANY, ANY] + [VM] * 3 + [ANY] * 3,
        [VM] + [ANY] * SHIPPED,
        scratch=[
            *[pltpu.VMEM(one, BF) for one in (r_terms.shape, r_terms.shape, shape, (NMAX, FF), square, square, square)],
            pltpu.VMEM(shape, F32),
            pltpu.SemaphoreType.DMA((6,)),
            pltpu.SemaphoreType.DMA((SHIPPED,)),
        ],
        limit=28, deps=deps,
    )
    if staged:
        packed = packed + toward(packed, lambda i: i ^ 2)
        a_own, a_first = summed([*in_hbm([a_rest]), a_came, a_back], (r_leave,), split=True)
        a_last = near(a_first)
        h_rest, h_keep, send_rest, *send = h_ship
        h_pair = pair_sum(h_keep, send)
        h_back = far(h_pair)
        h_came = sibling(send_rest)
        a_stay, a_leave = summed([a_own, a_last], (packed,), [(2, PART), (3, PART)], ranges)
        a_edge = along(a_leave, EDGE)
        packed = packed + toward(packed, lambda i: i ^ 4)
        weight_squares = packed[-1, 2 : 2 + PART]
        h_own, h_first = summed([*in_hbm([h_rest]), h_came, h_back], (r_edge, a_leave, packed), split=True)
        h_last = near(h_first)
        r_half = summed([r_stay, r_edge], (h_first,))
        a_half = summed([a_stay, a_edge], (h_first,))
        upper = z >= 2
        wide_cross = along(jnp.where(upper, a_half, r_half), SKIP)
        slim_cross = along(jnp.where(upper, a_half[PART - rest_a :], r_half[:rest_a]), TURN)
        packed = packed + along(packed, EDGE)
        h_stay, h_leave = summed([h_own, h_last], (packed,), [(4, rest_h), (5, rest_h)], ranges)
        h_edge, h_inner, h_turn = along(h_leave, EDGE), along(h_leave, INNER), along(h_stay, TURN)
        packed = packed + along(packed, CROSS)
        grad_rows, low_rows = call(
            assemble,
            [jnp.stack([z, jnp.int32(seq_total)])]
            + [a_half, r_half, wide_cross, slim_cross, h_stay, h_edge, h_inner, h_turn],
            [pltpu.HBM(weights.shape, F32), sds(weights.shape, BF)],
            [SM] + [VM] * 8,
            limit=10, deps=(packed,),
        )
        vector_total, norm_totals = packed[:-1], packed[-1, :2]
        low_near, low_far = near(low_rows), far(low_rows)
        low = [low_rows, low_near, low_far, far(low_near)]
        rows = sds(weights.shape, F32)
        one = pl.BlockSpec((BATCH, row16, TB), lambda n: (n, 0, 0))
        halved = [pl.BlockSpec((None, BATCH, row16, TB), lambda n, at=at: (at, n, 0, 0)) for at in range(2)]
        new_weights, new_left, new_right = pl.pallas_call(
            step_kernel,
            grid=(PART // BATCH,),
            out_shape=[rows, rows, rows],
            in_specs=[SM, SM, SM] + [one] * (5 + GROUPS) + [halved[0]] * GROUPS + [halved[1]] * GROUPS,
            out_specs=[one, one, one],
            compiler_params=pltpu.CompilerParams(vmem_limit_bytes=24 * 1024 * 1024),
            cost_estimate=pl.CostEstimate(flops=1, bytes_accessed=1, transcendentals=0),
        )(
            scalars, decays.reshape(-1), jnp.sqrt(weight_squares / (TB * TB)),
            *in_hbm([
                grad_rows, left_root, left_stats, right_stats, weights,
                *low, *(sibling(piece) for piece in low),
                *roots, *other_roots, *roots, *other_roots,
            ]),
        )
    else:
        def join(ship):
            both = jnp.concatenate(ship[:3] + [ship[3][None], ship[4][None]], axis=0)
            return jnp.stack([both[s] for s in SLOT_TABLE], axis=1).reshape(-1, TB, TB)

        every = jnp.concatenate([join(a_ship), join(h_ship), join(r_ship)], axis=0)
        inner = lax.psum_scatter(every, "fsdp", scatter_dimension=1, tiled=True)
        total = lax.psum_scatter(inner, "dp", scatter_dimension=0, tiled=True).astype(F32)
        grad_rows = total / seq_total
        vector_total, norm_totals = lax.psum((local_vectors, local_norms), ("dp", "fsdp"))
        high = lax.Precision.HIGHEST
        whole = lax.all_gather(grad_rows.astype(BF), "fsdp", axis=1, tiled=True).astype(F32)
        count = grad_rows.shape[1]
        slab = lax.dynamic_slice_in_dim(whole, lax.axis_index("fsdp") * count, count, 2)
        gram_left = jnp.einsum("brc,bsc->brs", grad_rows, whole, precision=high)
        gram_right = jnp.einsum("bic,bis->bcs", slab, whole, precision=high)
        decay_left = decays[:, 0][:, None, None]
        decay_right = decays[:, 1][:, None, None]
        new_left = decay_left * left_stats + (1.0 - decay_left) * gram_left
        new_right = decay_right * right_stats + (1.0 - decay_right) * gram_right
        columns = jnp.einsum("bis,bcs->bic", whole, right_root, precision=high)
        applied = lax.all_gather(columns.astype(BF), "fsdp", axis=2, tiled=True).astype(F32)
        precond = jnp.einsum("brs,bsc->brc", left_root, applied, precision=high)
        precond_squares, weight_squares = lax.psum(
            (jnp.sum(precond * precond, axis=(1, 2)), jnp.sum(weights * weights, axis=(1, 2))), "fsdp"
        )
        tile_area = TB * TB
        weight_scale = jnp.sqrt(weight_squares / tile_area)
        precond_scale = lax.rsqrt(precond_squares / tile_area + EPS_STEP)
        new_weights = weights - STEP_RATE * (weight_scale * precond_scale)[:, None, None] * precond
    vector_grad = vector_total / seq_total
    summary_norms = norm_totals / seq_total
    new_moments = MOMENT_DECAY * moments + (1.0 - MOMENT_DECAY) * vector_grad
    row_scale = jnp.sqrt(jnp.mean(jnp.square(vectors), axis=1, keepdims=True))
    moment_scale = lax.rsqrt(jnp.mean(jnp.square(new_moments), axis=1, keepdims=True) + EPS_STEP)
    new_vectors = vectors - STEP_RATE * row_scale * new_moments * moment_scale
    return (
        out[None],
        in_grads[None],
        new_weights,
        grad_rows,
        new_left,
        new_right,
        new_vectors,
        new_moments,
        summary_norms,
    )


def solution(mesh):
    in_specs = (
        P(("dp", "fsdp"), None, None),
        P(("dp", "fsdp"), None, None),
        P(("dp", "fsdp")),
        P("dp", "fsdp", None),
        P(),
        P(),
        P("dp", "fsdp", None),
        P("dp", "fsdp", None),
        P("dp", "fsdp", None),
        P("dp", "fsdp", None),
        P("dp", None),
    )
    out_specs = (
        P(("dp", "fsdp"), None, None),
        P(("dp", "fsdp"), None, None),
        P("dp", "fsdp", None),
        P("dp", "fsdp", None),
        P("dp", "fsdp", None),
        P("dp", "fsdp", None),
        P(),
        P(),
        P(),
    )
    return jax.shard_map(local, mesh=mesh, in_specs=in_specs, out_specs=out_specs, check_vma=False)
```

```python
import functools

import jax
import jax.numpy as jnp
from jax import lax
from jax.experimental import pallas as pl
from jax.experimental.pallas import tpu as pltpu
from jax.sharding import PartitionSpec as P

D = 768
H = 12
HD = 64
FF = 3072
K = 256
NMAX = 512
TB = 128
LANES = 128
PART = 110
GROUPS = 8

EPS_NORM = 1e-05
EPS_STEP = 1e-06
STEP_RATE = 0.25
MOMENT_DECAY = 0.9
SQRT_HALF = 0.7071067811865476
INV_SQRT_TWO_PI = 0.3989422804014327
SCALE = HD ** (-0.5)

QUARTER = (D // TB) ** 2
ATT = 4 * QUARTER + NMAX // TB * (K // TB)
HID = D // TB * (FF // TB)
NBLK = ATT + 2 * HID
BF = jnp.bfloat16
F32 = jnp.float32

ANY = pl.BlockSpec(memory_space=pl.ANY)
VM = pl.BlockSpec(memory_space=pltpu.VMEM)
SM = pl.BlockSpec(memory_space=pltpu.SMEM)


def sds(shape, dtype):
    return jax.ShapeDtypeStruct(shape, dtype)


def nn(a, b):
    return lax.dot_general(a, b, (((1,), (0,)), ((), ())), preferred_element_type=F32)


def nt(a, b):
    return lax.dot_general(a, b, (((1,), (1,)), ((), ())), preferred_element_type=F32)


def tn(a, b):
    return lax.dot_general(a, b, (((0,), (0,)), ((), ())), preferred_element_type=F32)


def layer_norm(value):
    centre = jnp.mean(value, axis=-1, keepdims=True)
    shifted = value - centre
    spread = jnp.mean(shifted * shifted, axis=-1, keepdims=True)
    inverse = lax.rsqrt(spread + EPS_NORM)
    return shifted * inverse, inverse


def norm_backward(grad_out, normed, inverse, gain):
    scaled = grad_out * gain
    centred = scaled - jnp.mean(scaled, axis=-1, keepdims=True)
    return inverse * (centred - normed * jnp.mean(scaled * normed, axis=-1, keepdims=True))


def column_sum(value):
    return jnp.sum(value.astype(F32), axis=0, keepdims=True)


def valid_rows(length, width):
    return lax.broadcasted_iota(jnp.int32, (NMAX, width), 0) < length


HELD = GROUPS // 2
ARRAYS = 10


def piece_at(pieces, step, s):
    if step < 3:
        return pieces[2 * step + s // HELD].at[s % HELD]
    trio, last = pieces[6 + 2 * (s // HELD)], pieces[7 + 2 * (s // HELD)]
    return last if s % HELD == HELD - 1 else trio.at[s % HELD]


def fetch(sc, pieces, raw, sem):
    for part in range(4):
        for step in range(4):

            @pl.when(sc[8 + part] == step)
            def _():
                for s in range(GROUPS):
                    pltpu.make_async_copy(piece_at(pieces, step, s), raw.at[part, s], sem.at[part, s]).start()


def fetched(pieces, raw, sem, part):
    for s in range(GROUPS):
        pltpu.make_async_copy(piece_at(pieces, 0, s), raw.at[part, s], sem.at[part, s]).wait()


def lay_out(slots, raw, at, first, count, dst, dst_first, per_row):
    for n in range(count):
        i, j = divmod(n + dst_first, per_row)
        for r in range(GROUPS):
            dst[i * TB + 16 * r : i * TB + 16 * r + 16, j * TB : (j + 1) * TB] = raw[at, slots[r], first + n]


def splitter(sc):
    even = sc[13] == 0
    mine = [jnp.where(even, sc[2 * m], sc[2 * m + 1]) for m in range(4)]
    other = [jnp.where(even, sc[2 * m + 1], sc[2 * m]) - 4 for m in range(4)]

    def put(keep, send, b, value):
        low = value.astype(BF)
        for m in range(4):
            first = low[32 * m : 32 * m + 16]
            second = low[32 * m + 16 : 32 * m + 32]
            keep[mine[m], b] = jnp.where(even, first, second)
            send[other[m], b] = jnp.where(even, second, first)

    return put


SHIPPED = 5


def shipped(keep, send, outs, span, sem):
    cuts = [(keep, pl.ds(0, 2)), (keep, pl.ds(2, 2)), (send, pl.ds(0, 2)), (send, 2), (send, 3)]
    return [
        pltpu.make_async_copy(source.at[at, span], out.at[span] if isinstance(at, int) else out.at[:, span], sem.at[n])
        for n, ((source, at), out) in enumerate(zip(cuts, outs))
    ]


def shipped_shapes(count):
    one = (count, TB // GROUPS, TB)
    return [pltpu.HBM((2,) + one, BF)] * 3 + [pltpu.HBM(one, BF)] * 2


STEP = 256


def tiles(raw, slots, block):
    part, b = divmod(block, PART)
    return [raw[part, slots[r], b] for r in range(GROUPS)]


def hidden_columns(raw, slots, g):
    count = STEP // TB
    rows = []
    for i in range(D // TB):
        blocks = [tiles(raw, slots, ATT + i * (FF // TB) + g * count + c) for c in range(count)]
        rows += [jnp.concatenate([block[r] for block in blocks], axis=1) for r in range(GROUPS)]
    return jnp.concatenate(rows, axis=0)


def return_rows(raw, slots, g):
    count = STEP // TB
    rows = []
    for i in range(count):
        blocks = [tiles(raw, slots, ATT + HID + (g * count + i) * (D // TB) + j) for j in range(D // TB)]
        rows += [jnp.concatenate([block[r] for block in blocks], axis=1) for r in range(GROUPS)]
    return jnp.concatenate(rows, axis=0)


KEPT = 19


def layer(sc, tok, cot, vec, *rest):
    pieces, rest = rest[:ARRAYS], rest[ARRAYS:]
    stored, rest = rest[:KEPT], rest[KEPT:]
    ks_o, vs_o, lse_o, norm_o, sums_o = rest[:5]
    (raw, q_o, k_o, v_o, mixt_o, wq_o, wk_o, wv_o, wo_o, cm_o, mix_o, fl_o, gh_o, slope, act, gsl, acc, nf, ni,
     cot_v, out_o, gr_o, gb_o, gm_o, keep_o, send_o, sem, osem, csem, tsem) = rest[5:]
    fetch(sc, pieces, raw, sem)
    cot_copy = pltpu.make_async_copy(cot, cot_v, csem)
    cot_copy.start()
    slots = [sc[r] for r in range(GROUPS)]
    put = splitter(sc)
    nb = nd = D // TB
    copies = []

    def store(*refs):
        for ref in refs:
            copy = pltpu.make_async_copy(ref, stored[len(copies)], osem.at[len(copies)])
            copy.start()
            copies.append(copy)

    fetched(pieces, raw, sem, 0)
    for m, dst in enumerate((wq_o, wk_o, wv_o)):
        lay_out(slots, raw, 0, m * QUARTER, QUARTER, dst, 0, nb)
    head = PART - 3 * QUARTER
    lay_out(slots, raw, 0, 3 * QUARTER, head, wo_o, 0, nb)
    x = tok[...]
    q_o[...] = (nn(x, wq_o[...]) + vec[0:1]).astype(BF)
    k_o[...] = (nn(x, wk_o[...]) + vec[1:2]).astype(BF)
    v_o[...] = (nn(x, wv_o[...]) + vec[2:3]).astype(BF)
    fetched(pieces, raw, sem, 1)
    lay_out(slots, raw, 1, 0, QUARTER - head, wo_o, head, nb)
    lay_out(slots, raw, 1, QUARTER - head, ATT - 4 * QUARTER, cm_o, 0, K // TB)
    store(wq_o, wk_o, wv_o, cm_o, q_o, k_o, v_o)
    masked = jnp.where(valid_rows(sc[12], K), cm_o[...], jnp.zeros((), BF))
    ks_o[...] = tn(masked, k_o[...]).astype(BF)
    vs_o[...] = tn(masked, v_o[...]).astype(BF)
    for n, ref in enumerate((ks_o, vs_o)):
        square = jnp.square(ref[...].astype(F32))
        total = jnp.sum(jnp.sum(square, axis=0, keepdims=True), axis=1, keepdims=True)
        norm_o[n : n + 1, :] = jnp.broadcast_to(jnp.sqrt(total), (1, LANES))
    lane = lax.broadcasted_iota(jnp.int32, (K, LANES), 1) < HD
    for p in range(H // 2):
        cols = slice(p * LANES, (p + 1) * LANES)
        q_p, ks_p, vs_p = q_o[:, cols], ks_o[:, cols], vs_o[:, cols]
        zero = jnp.zeros((), BF)
        parts, values = [], []
        for half in range(2):
            sel = lane if half == 0 else jnp.logical_not(lane)
            scores = nt(jnp.where(sel, ks_p, zero), q_p) * SCALE
            peak = jnp.max(scores, axis=0, keepdims=True)
            raised = jnp.exp(scores - peak)
            total = jnp.sum(raised, axis=0, keepdims=True)
            lse_o[2 * p + half : 2 * p + half + 1, :] = peak + jnp.log(total)
            parts.append((raised * (1.0 / total)).astype(BF))
            values.append(jnp.where(sel, vs_p, zero))
        mixt = tn(jnp.concatenate(values, axis=0), jnp.concatenate(parts, axis=0)).astype(BF)
        mixt_o[cols, :] = mixt
        mix_o[:, cols] = mixt.T
    store(mixt_o)
    branch = nn(mix_o[...], wo_o[...]) + vec[3:4]
    normed, inverse = layer_norm(x.astype(F32) + branch)
    nf[...] = normed
    ni[...] = jnp.broadcast_to(inverse, (NMAX, LANES))
    first = normed * vec[4:5] + vec[5:6]
    fl_o[...] = first.astype(BF)
    store(fl_o)
    acc[...] = first + vec[10:11]
    for at in (2, 3):
        fetched(pieces, raw, sem, at)
    for g in range(FF // STEP):
        cols = slice(g * STEP, (g + 1) * STEP)
        row, off = 6 + (g * STEP) // D, (g * STEP) % D
        hidden = nn(fl_o[...], hidden_columns(raw, slots, g)) + vec[row : row + 1, off : off + STEP]
        phi = 0.5 * (1.0 + lax.erf(hidden * SQRT_HALF))
        low = (hidden * phi).astype(BF)
        act[:, cols] = low
        slope[:, cols] = phi + hidden * INV_SQRT_TWO_PI * jnp.exp(-0.5 * hidden * hidden)
        acc[...] += nn(low, return_rows(raw, slots, g))
    valid = valid_rows(sc[12], D)
    normed2, inverse2 = layer_norm(acc[...])
    result = normed2 * vec[11:12] + vec[12:13]
    out_o[...] = jnp.where(valid, result, 0.0).astype(BF)
    store(out_o)
    cot_copy.wait()
    grad_result = jnp.where(valid, cot_v[...].astype(F32), 0.0)
    sums_o[8:9, :] = column_sum(grad_result * normed2)
    sums_o[9:10, :] = column_sum(grad_result)
    grad_second = norm_backward(grad_result, normed2, inverse2, vec[11:12])
    acc[...] = grad_second
    gsl[...] = grad_second.astype(BF)
    sums_o[7:8, :] = column_sum(gsl[...])
    for g in range(FF // STEP):
        cols = slice(g * STEP, (g + 1) * STEP)
        gh = (nt(gsl[...], return_rows(raw, slots, g)) * slope[:, cols]).astype(BF)
        gh_o[:, cols] = gh
        row, off = (g * STEP) // D, (g * STEP) % D
        sums_o[3 + row : 4 + row, off : off + STEP] = column_sum(gh)
        acc[...] += nt(gh, hidden_columns(raw, slots, g))
        terms = tn(act[:, cols], gsl[...])
        for i in range(STEP // TB):
            for j in range(nd):
                put(keep_o, send_o, (g * (STEP // TB) + i) * nd + j, terms[i * TB : (i + 1) * TB, j * TB : (j + 1) * TB])
        span = pl.ds(g * (STEP // TB) * nd, (STEP // TB) * nd)
        for copy in shipped(keep_o, send_o, stored[-SHIPPED:], span, tsem.at[g]):
            copy.start()
    store(gh_o)
    grad_first = acc[...]
    normed, inverse = nf[...], ni[:, 0:1]
    sums_o[1:2, :] = column_sum(grad_first * normed)
    sums_o[2:3, :] = column_sum(grad_first)
    grad_resid = norm_backward(grad_first, normed, inverse, vec[4:5])
    gr_o[...] = grad_resid
    low = grad_resid.astype(BF)
    gb_o[...] = low
    sums_o[0:1, :] = column_sum(low)
    store(gr_o, gb_o)
    gm_o[...] = nt(low, wo_o[...]).astype(BF)
    store(gm_o)
    for copy in copies:
        copy.wait()
    for g in range(FF // STEP):
        span = pl.ds(g * (STEP // TB) * nd, (STEP // TB) * nd)
        for copy in shipped(keep_o, send_o, stored[-SHIPPED:], span, tsem.at[g]):
            copy.wait()


def attention_backward(sc, tok, q, ks, vs, lse, gm, k, v, gb, mixt, cm, *rest):
    gq_o, gk_o, gv_o, sums_o, *outs = rest[-23:-14]
    gks_o, gvs_o, keep_o, send_o, *held, sem, tsem = rest[-14:]
    ships = []

    def ship(n, first, count):
        for copy in shipped(keep_o, send_o, outs, pl.ds(first, count), tsem.at[n]):
            copy.start()
            ships.append(copy)

    copies = [
        pltpu.make_async_copy(source, target, sem.at[n])
        for n, (source, target) in enumerate(zip((q, gm, tok, mixt, cm, k, v, gb), held))
    ]
    for copy in copies:
        copy.start()
    q, gm, tok, mixt, cm, k, v, gb = held
    for copy in copies[:2]:
        copy.wait()
    lane = lax.broadcasted_iota(jnp.int32, (K, LANES), 1) < HD
    zero = jnp.zeros((), BF)
    for p in range(H // 2):
        cols = slice(p * LANES, (p + 1) * LANES)
        q_p, ks_p, vs_p, gm_p = q[:, cols], ks[:, cols], vs[:, cols], gm[:, cols]
        keys, grads, gvs, gks = [], [], [], []
        for half in range(2):
            sel = lane if half == 0 else jnp.logical_not(lane)
            key = jnp.where(sel, ks_p, zero)
            attend = jnp.exp(nt(key, q_p) * SCALE - lse[2 * p + half : 2 * p + half + 1, :])
            grad_attend = nt(jnp.where(sel, vs_p, zero), gm_p)
            mean = jnp.sum(grad_attend * attend, axis=0, keepdims=True)
            grad_scores = (attend * (grad_attend - mean)).astype(BF)
            gvs.append(nn(attend.astype(BF), gm_p))
            gks.append(nn(grad_scores, q_p))
            keys.append(key)
            grads.append(grad_scores)
        gvs_o[:, cols] = jnp.where(lane, gvs[0], gvs[1]).astype(BF)
        gks_o[:, cols] = (jnp.where(lane, gks[0], gks[1]) * SCALE).astype(BF)
        gqt = tn(jnp.concatenate(keys, axis=0), jnp.concatenate(grads, axis=0)) * SCALE
        gq_o[:, cols] = gqt.astype(BF).T
    put = splitter(sc)
    nd, nk = D // TB, K // TB
    for copy in copies[2:]:
        copy.wait()
    masked = jnp.where(valid_rows(sc[12], K), cm[...], zero)
    gk_o[...] = nn(masked, gks_o[...]).astype(BF)
    gv_o[...] = nn(masked, gvs_o[...]).astype(BF)
    tokt = tok[...].T
    lhs = (tokt, tokt, tokt, mixt[...])
    for m, grad in enumerate((gq_o, gk_o, gv_o, gb)):
        if m < 3:
            sums_o[m : m + 1, :] = column_sum(grad[...])
        terms = nn(lhs[m], grad[...])
        for i in range(nd):
            for j in range(nd):
                put(keep_o, send_o, m * QUARTER + i * nd + j, terms[i * TB : (i + 1) * TB, j * TB : (j + 1) * TB])
        ship(m, m * QUARTER, QUARTER)
    comp = nt(k[...], gks_o[...]) + nt(v[...], gvs_o[...])
    comp = jnp.where(valid_rows(sc[12], K), comp, 0.0)
    for i in range(NMAX // TB):
        for j in range(nk):
            put(keep_o, send_o, 4 * QUARTER + i * nk + j, comp[i * TB : (i + 1) * TB, j * TB : (j + 1) * TB])
    ship(4, 4 * QUARTER, ATT - 4 * QUARTER)
    for copy in ships:
        copy.wait()


def closing(sc, fl, gh, gr, gq, gk, gv, wq, wk, wv, *rest):
    in_o, *outs = rest[-16:-10]
    keep_o, send_o, *held, gr_v, sem, tsem = rest[-10:]
    copies = [
        pltpu.make_async_copy(source, target, sem.at[n])
        for n, (source, target) in enumerate(zip((fl, gh, wq, wk, wv, gr), (*held, gr_v)))
    ]
    for copy in copies:
        copy.start()
    fl, gh, wq, wk, wv = held
    put = splitter(sc)
    for copy in copies[:2]:
        copy.wait()
    nh, nd = FF // TB, D // TB
    flt = fl[...].T
    for g in range(FF // STEP):
        terms = nn(flt, gh[:, g * STEP : (g + 1) * STEP])
        for i in range(nd):
            for j in range(STEP // TB):
                put(keep_o, send_o, i * nh + g * (STEP // TB) + j, terms[i * TB : (i + 1) * TB, j * TB : (j + 1) * TB])
    ships = shipped(keep_o, send_o, outs, pl.ds(0, HID), tsem)
    for copy in ships:
        copy.start()
    for copy in copies[2:]:
        copy.wait()
    total = gr_v[...] + nt(gq[...], wq[...])
    total = total + nt(gk[...], wk[...])
    total = total + nt(gv[...], wv[...])
    in_o[...] = total.astype(BF)
    for copy in ships:
        copy.wait()


def assemble(at, wide_a, wide_r, wide_x, slim_x, h_stay, h_x, h_y, h_z, *rest):
    rows_o, low_o, scale = rest[-2], rest[-1], at[1].astype(F32)
    upper = at[0] >= 2
    size, slim, late = wide_a.shape[0], slim_x.shape[0], h_stay.shape[0]

    def emit(first, count, value):
        value = value * (1.0 / scale)
        rows_o[first : first + count] = value
        low_o[first : first + count] = value.astype(BF)

    def hidden(count):
        value = h_stay[:count].astype(F32)
        for ref in (h_x, h_y, h_z):
            value = value + ref[:count].astype(F32)
        return value

    @pl.when(at[0] % 3 == 0)
    def _():
        emit(0, size, jnp.where(upper, wide_r[...], wide_a[...]).astype(F32) + wide_x[...].astype(F32))

    @pl.when(at[0] == 1)
    def _():
        emit(0, slim, wide_a[size - slim :].astype(F32) + slim_x[...].astype(F32))
        emit(slim, size - slim, hidden(size - slim))

    @pl.when(at[0] == 2)
    def _():
        emit(0, late, hidden(late))
        emit(late, size - late, wide_r[: size - late].astype(F32) + slim_x[: size - late].astype(F32))


BATCH = 22


def halves(value):
    high = value.astype(BF)
    return high, (value - high.astype(F32)).astype(BF)


def step_kernel(sc, dec, size, own, lroot, lstat, rstat, weight, *rest):
    here, there, lefts, rights = (rest[n * HELD : (n + 1) * HELD] for n in (0, 1, 2, 4))
    other_lefts, other_rights = rest[3 * HELD : 4 * HELD], rest[5 * HELD : 6 * HELD]
    nw_o, nl_o, nr_o = rest[6 * HELD :]
    slots = [sc[r] for r in range(GROUPS)]
    even = sc[13] == 0
    mine = [jnp.where(even, slots[2 * m], slots[2 * m + 1]) for m in range(4)]
    other = [jnp.where(even, slots[2 * m + 1], slots[2 * m]) - HELD for m in range(4)]
    pick_row = lax.broadcasted_iota(jnp.int32, (16, TB), 0) + sc[14] * 16
    select = (lax.broadcasted_iota(jnp.int32, (16, TB), 1) == pick_row).astype(BF)
    start = pl.program_id(0) * BATCH

    def ordered(pairs):
        rows = []
        for a, b in pairs:
            rows += [jnp.where(even, a, b), jnp.where(even, b, a)]
        return jnp.concatenate(rows, axis=0)

    def tile(refs, slot, n):
        value = refs[0][n]
        for at in range(1, HELD):
            value = jnp.where(slot == at, refs[at][n], value)
        return value

    def whole(here, there, n):
        return ordered([(tile(here, mine[m], n), tile(there, other[m], n)) for m in range(4)])

    bs = range(BATCH)
    grads = [whole(here, there, n) for n in bs]
    across = [nt(jnp.concatenate([own[n].astype(BF), select], axis=0), g) for n, g in zip(bs, grads)]
    left = [jnp.concatenate([whole(lefts, other_lefts, n), *halves(lroot[n])], axis=0) for n in bs]
    down = [nn(jnp.concatenate([f, a[16:].astype(BF)], axis=0), g) for f, a, g in zip(left, across, grads)]
    mids = [
        jnp.concatenate([d[:TB].astype(BF), *halves(d[TB : TB + 16] + d[TB + 16 : TB + 32])], axis=0) for d in down
    ]
    last = [nn(m, whole(rights, other_rights, n)) for n, m in zip(bs, mids)]
    for n, a, d, p in zip(bs, across, down, last):
        decay = dec[2 * (start + n)]
        nl_o[n] = decay * lstat[n] + (1.0 - decay) * a[:16]
        decay = dec[2 * (start + n) + 1]
        nr_o[n] = decay * rstat[n] + (1.0 - decay) * d[TB + 32 :]
        full = p[:TB]
        squares = jnp.sum(jnp.sum(full * full, axis=0, keepdims=True), axis=1, keepdims=True)
        scale = size[start + n] * lax.rsqrt(squares * (1.0 / (TB * TB)) + EPS_STEP)
        nw_o[n] = weight[n] - STEP_RATE * scale * (p[TB : TB + 16] + p[TB + 16 :])


def in_hbm(arrays):
    return [pltpu.with_memory_space_constraint(a, pltpu.HBM) for a in arrays]


def call(kernel, ins, outs, in_specs, out_specs=None, scratch=(), limit=60, deps=()):
    return pl.pallas_call(
        kernel,
        out_shape=outs,
        in_specs=in_specs + [ANY] * len(deps),
        out_specs=out_specs or [VM] * len(outs),
        scratch_shapes=list(scratch),
        compiler_params=pltpu.CompilerParams(vmem_limit_bytes=limit * 1024 * 1024),
        cost_estimate=pl.CostEstimate(flops=1, bytes_accessed=1, transcendentals=0),
    )(*ins, *deps)


SLOT_TABLE = (0, 4, 1, 6, 2, 5, 3, 7)


def slot_of(code, core):
    other, x, y = code & 1, (code >> 1) & 1, code >> 2
    return 4 * other + jnp.where((other ^ core) == 0, x + 2 * y, y + 2 * x)


def toward(x, move):
    return lax.ppermute(x, "fsdp", [(i, move(i)) for i in range(GROUPS)])


def near(x):
    return toward(x, lambda i: i ^ 2 if i % 2 == 0 else i ^ 4)


def far(x):
    return toward(x, lambda i: i ^ 4 if i % 2 == 0 else i ^ 2)


def sibling(x):
    return toward(x, lambda i: i ^ 1)


def along(x, pairs):
    return lax.ppermute(x, "dp", pairs)


def gate(index, options, copies, deps=()):
    flat, plan = [], []
    for entry in copies:
        group = entry if isinstance(entry, list) else [entry]
        plan.append((len(flat), len(group) if isinstance(entry, list) else 0))
        flat += group
    count = len(options)
    outs = [sds(options[0].shape, options[0].dtype)] if count else []
    for entry in copies:
        if isinstance(entry, list):
            outs.append(pltpu.HBM((len(entry),) + entry[0].shape, BF))
        else:
            outs.append(pltpu.HBM(entry.shape, BF) if entry.ndim == 4 else sds(entry.shape, BF))

    def kernel(at, *refs):
        sem = refs[-1]
        out = refs[-1 - len(outs) : -1]
        given = refs[count : count + len(flat)]
        started = []
        for n, (first, size) in enumerate(plan):
            target = out[n + (1 if count else 0)]
            for m in range(max(size, 1)):
                copy = pltpu.make_async_copy(
                    given[first + m], target.at[m] if size else target, sem.at[1 + first + m]
                )
                copy.start()
                started.append(copy)
        for n in range(count):

            @pl.when(at[0] == n)
            def _():
                pltpu.make_async_copy(refs[n], out[0], sem.at[0]).start()

        for copy in started:
            copy.wait()
        if count:
            pltpu.make_async_copy(refs[0], out[0], sem.at[0]).wait()

    return pl.pallas_call(
        kernel,
        out_shape=outs,
        in_specs=[SM] + [ANY] * (count + len(flat) + len(deps)),
        out_specs=[ANY] * len(outs),
        scratch_shapes=[pltpu.SemaphoreType.DMA((1 + len(flat),))],
        compiler_params=pltpu.CompilerParams(vmem_limit_bytes=2**20),
        cost_estimate=pl.CostEstimate(flops=1, bytes_accessed=1, transcendentals=0),
    )(index[None], *options, *flat, *deps)


def tie(x, deps):
    def kernel(*refs):
        pass

    return pl.pallas_call(
        kernel,
        out_shape=sds(x.shape, x.dtype),
        in_specs=[ANY] * (1 + len(deps)),
        out_specs=ANY,
        input_output_aliases={0: 0},
        compiler_params=pltpu.CompilerParams(vmem_limit_bytes=2**20),
        cost_estimate=pl.CostEstimate(flops=1, bytes_accessed=1, transcendentals=0),
    )(*in_hbm([x]), *deps)


def chosen(index, options):
    value = options[0]
    for i in range(1, len(options)):
        value = jnp.where(index == i, options[i], value)
    return value


EDGE = [(0, 1), (1, 0), (2, 3), (3, 2)]
INNER = [(0, 0), (1, 2), (2, 1), (3, 3)]


CROSS = [(0, 2), (1, 3), (2, 0), (3, 1)]
SKIP = [(0, 1), (1, 3), (2, 0), (3, 2)]
TURN = [(0, 2), (1, 0), (2, 3), (3, 1)]


def gather_weights(narrow, early):
    z = lax.axis_index("dp")
    e, o = along(narrow, EDGE), along(narrow, INNER)
    a0, b0 = near(narrow), far(narrow)
    t1, a0 = gate(z, [e, e, o, e], [a0], (b0,))
    eo, oe = along(o, EDGE), along(e, INNER)
    a1, b1, c0 = near(t1), far(t1), far(a0)
    t2, a1, four0 = gate(z, [eo, o, oe, eo], [a1, [narrow, a0, b0, c0]], (b1,))
    eoe, d0 = along(oe, EDGE), sibling(four0)
    a2, b2, c1 = near(t2), far(t2), far(a1)
    t3, a2, four1 = gate(z, [eoe, oe, e, eoe], [a2, [t1, a1, b1, c1]], (b2, d0))
    a3, b3, c2, d1 = near(t3), far(t3), far(a2), sibling(four1)
    a3, four2, trio = gate(z, [], [a3, [t2, a2, b2, c2], [t3, a3, b3]], (d1, early))
    c3, d2, d3 = far(a3), sibling(four2), sibling(trio)
    last = sibling(c3)
    steps = chosen(z, [jnp.array(row, jnp.int32) for row in ((0, 1, 2, 3), (1, 0, 2, 3), (2, 1, 0, 3), (3, 2, 1, 0))])
    return [four0, d0, four1, d1, four2, d2, trio, c3, d3, last], steps


def summed(sources, deps=(), windows=(), scalars=None, split=False):
    shape, count = sources[0].shape, len(sources)

    def kernel(sc, *refs):
        outs = refs[count + len(deps) :]
        value = refs[0][...].astype(F32)
        for n in range(1, count):
            value = value + refs[n][...].astype(F32)
        value = value.astype(BF)
        if windows:
            outs[-1][...] = value
            for out, (start, size) in zip(outs, windows):
                out[...] = outs[-1][pl.ds(sc[start], size)]
        elif split:
            for n, out in enumerate(outs):
                out[...] = value[n]
        else:
            outs[0][...] = value

    shapes = [shape[1:]] * shape[0] if split else [(size,) + shape[1:] for _, size in windows] or [shape]
    results = call(
        kernel,
        [jnp.zeros((1,), jnp.int32) if scalars is None else scalars, *sources],
        [sds(one, BF) for one in shapes],
        [SM] + [VM] * count,
        scratch=[pltpu.VMEM(shape, BF)] if windows else [],
        limit=12, deps=deps,
    )
    return results if len(shapes) > 1 else results[0]


def pair_sum(keep, send, deps=()):
    def kernel(x, y, z, *rest):
        for n, ref in enumerate((y, z)):
            rest[-1][n] = (x[n].astype(F32) + ref[...].astype(F32)).astype(BF)

    got = [sibling(one) for one in send]
    return call(kernel, [*in_hbm([keep]), *got], [sds(keep.shape, BF)], [VM] * 3, limit=12, deps=deps)[0]


def plane_sum(x):
    for bit in (1, 2, 4):
        x = x + toward(x, lambda i, bit=bit: i ^ bit)
    return x


def local(
    tokens,
    cotangent,
    lengths,
    weights,
    vectors,
    moments,
    left_stats,
    right_stats,
    left_root,
    right_root,
    decays,
):
    dp, fsdp = lax.axis_size("dp"), lax.axis_size("fsdp")
    assert tokens.shape[0] == 1
    staged = (dp, fsdp) == (4, GROUPS)
    seq_total = tokens.shape[0] * dp * fsdp
    tok, cot = tokens[0], cotangent[0]
    narrow = weights.astype(BF)
    if staged:
        me = lax.axis_index("fsdp")
        core = lax.rem(me, 2)
        slots = slot_of(jnp.arange(GROUPS, dtype=jnp.int32) ^ me, core)
        roots = jnp.stack([left_root.astype(BF), right_root.astype(BF)])
        pieces, steps = gather_weights(narrow, roots)
    else:
        me = jnp.int32(0)
        core = jnp.int32(0)
        slots = slot_of(jnp.arange(GROUPS, dtype=jnp.int32), core)
        full = lax.all_gather(lax.all_gather(narrow, "dp", axis=0, tiled=True), "fsdp", axis=1, tiled=True)
        full = full.reshape(NBLK // PART, PART, GROUPS, TB // GROUPS, TB)
        place = [SLOT_TABLE.index(s) for s in range(GROUPS)]
        pieces = []
        for t in range(NBLK // PART):
            every = [full[t, :, place[s]] for s in range(GROUPS)]
            if t < 3:
                pieces += [jnp.stack(every[:HELD]), jnp.stack(every[HELD:])]
            else:
                pieces += [jnp.stack(every[:3]), every[3], jnp.stack(every[4:7]), every[7]]
        steps = jnp.arange(4, dtype=jnp.int32)
    scalars = jnp.concatenate([slots, steps, lengths, core[None], me[None]]).astype(jnp.int32)

    row16 = TB // GROUPS
    act = sds((NMAX, D), BF)
    wide = sds((NMAX, D), F32)
    summary = sds((K, D), BF)
    shape = (NMAX, D)
    square = (D, D)
    r_terms = sds((4, HID, row16, TB), BF)
    a_terms = sds((4, ATT, row16, TB), BF)
    held = [square, square, square, (NMAX, K), shape, shape, shape, (D, NMAX), shape, shape, (NMAX, FF)]
    (wq, wk, wv, cm, q, k, v, mixt, fl, out, gh, gr, gb, gm, *r_ship, ks, vs, lse, norms, sums_b) = call(
        layer,
        [scalars, tok, *in_hbm([cot]), vectors] + in_hbm(pieces),
        [pltpu.HBM(one, BF) for one in held]
        + [pltpu.HBM(shape, F32), pltpu.HBM(shape, BF), pltpu.HBM(shape, BF)]
        + shipped_shapes(HID)
        + [summary, summary, sds((H, NMAX), F32), sds((2, LANES), F32), sds((10, D), F32)],
        [SM, VM, ANY, VM] + [ANY] * ARRAYS,
        [ANY] * KEPT + [VM] * 5,
        scratch=[
            pltpu.VMEM((4, GROUPS, PART, row16, TB), BF),
            *[pltpu.VMEM(one, BF) for one in (shape, shape, shape, (D, NMAX), square, square, square, square, (NMAX, K), shape, shape, (NMAX, FF))],
            pltpu.VMEM((NMAX, FF), F32),
            pltpu.VMEM((NMAX, FF), BF),
            pltpu.VMEM(shape, BF),
            pltpu.VMEM(shape, F32),
            pltpu.VMEM(shape, F32),
            pltpu.VMEM((NMAX, LANES), F32),
            pltpu.VMEM(shape, BF),
            pltpu.VMEM(shape, BF),
            pltpu.VMEM(shape, F32),
            pltpu.VMEM(shape, BF),
            pltpu.VMEM(shape, BF),
            pltpu.VMEM(r_terms.shape, BF),
            pltpu.VMEM(r_terms.shape, BF),
            pltpu.SemaphoreType.DMA((4, GROUPS)),
            pltpu.SemaphoreType.DMA((KEPT - SHIPPED,)),
            pltpu.SemaphoreType.DMA(()),
            pltpu.SemaphoreType.DMA((FF // STEP, SHIPPED)),
        ],
        limit=60,
    )
    deps = ()
    if staged:
        z = lax.axis_index("dp")
        odd = z % 2
        cut_r = 3 * PART - (ATT + HID)
        cut_h = 2 * PART - ATT
        rest_a, rest_h = ATT - PART, HID - cut_h
        ranges = jnp.stack([odd * cut_r, (1 - odd) * cut_r, odd * rest_a, (1 - odd) * rest_a, (1 - odd) * cut_h, odd * cut_h])
        roots = [roots, near(roots), far(roots), toward(roots, lambda i: i ^ 6)]
        r_rest, r_keep, send_rest, *send = r_ship
        r_pair = pair_sum(r_keep, [tie(send[0], roots[1:]), send[1]])
        r_back = far(r_pair)
        r_came = sibling(send_rest)
        other_roots = [sibling(piece) for piece in roots]
        deps = (r_pair,)
    gq, gk, gv, sums_a, *a_ship = call(
        attention_backward,
        [scalars, *in_hbm([tok, q]), ks, vs, lse, *in_hbm([gm, k, v, gb, mixt, cm])],
        [act, act, act, sds((3, D), F32)] + shipped_shapes(ATT),
        [SM, ANY, ANY] + [VM] * 3 + [ANY] * 6,
        [VM] * 4 + [ANY] * SHIPPED,
        scratch=[
            *[pltpu.VMEM(one, BF) for one in ((K, D), (K, D), a_terms.shape, a_terms.shape, shape, shape, shape, (D, NMAX), (NMAX, K), shape, shape, shape)],
            pltpu.SemaphoreType.DMA((8,)),
            pltpu.SemaphoreType.DMA((5, SHIPPED)),
        ],
        limit=28, deps=deps,
    )
    local_vectors = jnp.concatenate([sums_a, sums_b], axis=0)
    local_norms = norms[:, 0]
    if staged:
        weight_sums = jnp.sum(jnp.square(lax.optimization_barrier(weights)), axis=(1, 2))
        packed = jnp.concatenate([local_norms, weight_sums, jnp.zeros((D - 2 - PART,), F32)])
        packed = jnp.concatenate([local_vectors, packed[None]], axis=0)
        packed = packed + sibling(packed)
        r_own, r_first = summed([*in_hbm([r_rest]), r_came, r_back], other_roots, split=True)
        r_last = near(r_first)
        a_rest, a_keep, send_rest, *send = a_ship
        a_pair = pair_sum(a_keep, [tie(send[0], (r_first,)), send[1]], (packed,))
        a_back = far(a_pair)
        a_came = sibling(send_rest)
        r_stay, r_leave = summed([r_own, r_last], (), [(0, PART), (1, PART)], ranges)
        r_edge = along(r_leave, EDGE)
        deps = (a_pair,)
    in_grads, *h_ship = call(
        closing,
        [scalars, *in_hbm([fl, gh, gr]), gq, gk, gv, *in_hbm([wq, wk, wv])],
        [act] + shipped_shapes(HID),
        [SM, ANY, ANY, ANY] + [VM] * 3 + [ANY] * 3,
        [VM] + [ANY] * SHIPPED,
        scratch=[
            *[pltpu.VMEM(one, BF) for one in (r_terms.shape, r_terms.shape, shape, (NMAX, FF), square, square, square)],
            pltpu.VMEM(shape, F32),
            pltpu.SemaphoreType.DMA((6,)),
            pltpu.SemaphoreType.DMA((SHIPPED,)),
        ],
        limit=28, deps=deps,
    )
    if staged:
        packed = packed + toward(packed, lambda i: i ^ 2)
        a_own, a_first = summed([*in_hbm([a_rest]), a_came, a_back], (r_leave,), split=True)
        a_last = near(a_first)
        h_rest, h_keep, send_rest, *send = h_ship
        h_pair = pair_sum(h_keep, send)
        h_back = far(h_pair)
        h_came = sibling(send_rest)
        a_stay, a_leave = summed([a_own, a_last], (packed,), [(2, PART), (3, PART)], ranges)
        a_edge = along(a_leave, EDGE)
        packed = packed + toward(packed, lambda i: i ^ 4)
        weight_squares = packed[-1, 2 : 2 + PART]
        h_own, h_first = summed([*in_hbm([h_rest]), h_came, h_back], (r_edge, a_leave, packed), split=True)
        h_last = near(h_first)
        r_half = summed([r_stay, r_edge], (h_first,))
        a_half = summed([a_stay, a_edge], (h_first,))
        upper = z >= 2
        wide_cross = along(jnp.where(upper, a_half, r_half), SKIP)
        slim_cross = along(jnp.where(upper, a_half[PART - rest_a :], r_half[:rest_a]), TURN)
        packed = packed + along(packed, EDGE)
        h_stay, h_leave = summed([h_own, h_last], (packed,), [(4, rest_h), (5, rest_h)], ranges)
        h_edge, h_inner, h_turn = along(h_leave, EDGE), along(h_leave, INNER), along(h_stay, TURN)
        grad_rows, low_rows = call(
            assemble,
            [jnp.stack([z, jnp.int32(seq_total)])]
            + [a_half, r_half, wide_cross, slim_cross, h_stay, h_edge, h_inner, h_turn],
            [pltpu.HBM(weights.shape, F32), sds(weights.shape, BF)],
            [SM] + [VM] * 8,
            limit=10,
        )
        low_near, low_far = near(low_rows), far(low_rows)
        packed = tie(packed, (low_near, low_far))
        packed = packed + along(packed, CROSS)
        vector_total, norm_totals = packed[:-1], packed[-1, :2]
        low = [low_rows, low_near, low_far, far(low_near)]
        rows = sds(weights.shape, F32)
        one = pl.BlockSpec((BATCH, row16, TB), lambda n: (n, 0, 0))
        halved = [pl.BlockSpec((None, BATCH, row16, TB), lambda n, at=at: (at, n, 0, 0)) for at in range(2)]
        new_weights, new_left, new_right = pl.pallas_call(
            step_kernel,
            grid=(PART // BATCH,),
            out_shape=[rows, rows, rows],
            in_specs=[SM, SM, SM] + [one] * (5 + GROUPS) + [halved[0]] * GROUPS + [halved[1]] * GROUPS,
            out_specs=[one, one, one],
            compiler_params=pltpu.CompilerParams(vmem_limit_bytes=24 * 1024 * 1024),
            cost_estimate=pl.CostEstimate(flops=1, bytes_accessed=1, transcendentals=0),
        )(
            scalars, decays.reshape(-1), jnp.sqrt(weight_squares / (TB * TB)),
            *in_hbm([
                grad_rows, left_root, left_stats, right_stats, weights,
                *low, *(sibling(piece) for piece in low),
                *roots, *other_roots, *roots, *other_roots,
            ]),
        )
    else:
        def join(ship):
            both = jnp.concatenate(ship[:3] + [ship[3][None], ship[4][None]], axis=0)
            return jnp.stack([both[s] for s in SLOT_TABLE], axis=1).reshape(-1, TB, TB)

        every = jnp.concatenate([join(a_ship), join(h_ship), join(r_ship)], axis=0)
        inner = lax.psum_scatter(every, "fsdp", scatter_dimension=1, tiled=True)
        total = lax.psum_scatter(inner, "dp", scatter_dimension=0, tiled=True).astype(F32)
        grad_rows = total / seq_total
        vector_total, norm_totals = lax.psum((local_vectors, local_norms), ("dp", "fsdp"))
        high = lax.Precision.HIGHEST
        whole = lax.all_gather(grad_rows.astype(BF), "fsdp", axis=1, tiled=True).astype(F32)
        count = grad_rows.shape[1]
        slab = lax.dynamic_slice_in_dim(whole, lax.axis_index("fsdp") * count, count, 2)
        gram_left = jnp.einsum("brc,bsc->brs", grad_rows, whole, precision=high)
        gram_right = jnp.einsum("bic,bis->bcs", slab, whole, precision=high)
        decay_left = decays[:, 0][:, None, None]
        decay_right = decays[:, 1][:, None, None]
        new_left = decay_left * left_stats + (1.0 - decay_left) * gram_left
        new_right = decay_right * right_stats + (1.0 - decay_right) * gram_right
        columns = jnp.einsum("bis,bcs->bic", whole, right_root, precision=high)
        applied = lax.all_gather(columns.astype(BF), "fsdp", axis=2, tiled=True).astype(F32)
        precond = jnp.einsum("brs,bsc->brc", left_root, applied, precision=high)
        precond_squares, weight_squares = lax.psum(
            (jnp.sum(precond * precond, axis=(1, 2)), jnp.sum(weights * weights, axis=(1, 2))), "fsdp"
        )
        tile_area = TB * TB
        weight_scale = jnp.sqrt(weight_squares / tile_area)
        precond_scale = lax.rsqrt(precond_squares / tile_area + EPS_STEP)
        new_weights = weights - STEP_RATE * (weight_scale * precond_scale)[:, None, None] * precond
    vector_grad = vector_total / seq_total
    summary_norms = norm_totals / seq_total
    new_moments = MOMENT_DECAY * moments + (1.0 - MOMENT_DECAY) * vector_grad
    row_scale = jnp.sqrt(jnp.mean(jnp.square(vectors), axis=1, keepdims=True))
    moment_scale = lax.rsqrt(jnp.mean(jnp.square(new_moments), axis=1, keepdims=True) + EPS_STEP)
    new_vectors = vectors - STEP_RATE * row_scale * new_moments * moment_scale
    return (
        out[None],
        in_grads[None],
        new_weights,
        grad_rows,
        new_left,
        new_right,
        new_vectors,
        new_moments,
        summary_norms,
    )


def solution(mesh):
    in_specs = (
        P(("dp", "fsdp"), None, None),
        P(("dp", "fsdp"), None, None),
        P(("dp", "fsdp")),
        P("dp", "fsdp", None),
        P(),
        P(),
        P("dp", "fsdp", None),
        P("dp", "fsdp", None),
        P("dp", "fsdp", None),
        P("dp", "fsdp", None),
        P("dp", None),
    )
    out_specs = (
        P(("dp", "fsdp"), None, None),
        P(("dp", "fsdp"), None, None),
        P("dp", "fsdp", None),
        P("dp", "fsdp", None),
        P("dp", "fsdp", None),
        P("dp", "fsdp", None),
        P(),
        P(),
        P(),
    )
    return jax.shard_map(local, mesh=mesh, in_specs=in_specs, out_specs=out_specs, check_vma=False)
```
